256 devices in a mesh: shard: 128 (over z, x, y), mp: 2 (over core).
Axes of the slice: x: 4, y: 4, z: 8, core: 2. Of those that a mesh axis runs over, the one named last changes fastest.
Arguments:
- item_rows: float32 [32768, 256], P('shard', 'mp'), may hold values from -6 to 6
- first_moment: float32 [32768, 256], P('shard', 'mp'), may hold values from -2 to 2
- second_moment: float32 [32768, 256], P('shard', 'mp'), may hold values from 0.01 to 4
- item_cot: bfloat16 [32768, 256], P('shard', 'mp'), may hold values from -6 to 6
- tile_bits: int32 [2048, 8, 128], P('shard'), may hold values from 0 to 65535, as said below
- tile_item: int32 [2048], P('shard'), may hold values from 0 to 1
- tile_dest: int32 [2048], P('shard'), may hold values from 0 to 127
- basket_gain: float32 [256], replicated, may hold values from 0.1 to 1.9
- item_gain: float32 [256], replicated, may hold values from 0.1 to 1.9
- gate_basket: bfloat16 [256, 2048], P(None, 'mp'), may hold values from -0.375 to 0.375
- up_basket: bfloat16 [256, 2048], P(None, 'mp'), may hold values from -0.375 to 0.375
- down_basket: bfloat16 [2048, 256], P('mp'), may hold values from -0.125 to 0.125
- gate_item: bfloat16 [256, 2048], P(None, 'mp'), may hold values from -0.375 to 0.375
- up_item: bfloat16 [256, 2048], P(None, 'mp'), may hold values from -0.375 to 0.375
- down_item: bfloat16 [2048, 256], P('mp'), may hold values from -0.125 to 0.125
Outputs:
- new_rows: float32 [32768, 256], P('shard', 'mp')
- new_first: float32 [32768, 256], P('shard', 'mp')
- new_second: float32 [32768, 256], P('shard', 'mp')
The draws below stay inside these ranges and needn't reach their ends.
Inputs may be any that keep to these rules, and one draw needn't show every extreme that they name: `tile_bits`: each word holds 16 independent incidence bits in its low bits.
All inputs are finite; a program needn't handle non-finite values.
Results may differ from the reference program's by a relative error of at most 0.007.
Values may be sent and summed in bfloat16 or wider, within the bound.
A program may use at most 128 MiB of HBM per device.

```python
import math
import jax
import jax.numpy as jnp
import numpy as np
from jax import lax

D = 256
FF = 2048
BLOCK = 128
ITEM_BLOCKS = 2
TILE_DEV = 16
WORDS = 8
TILES = 2048
BASKET_BLOCKS = 128
ITEMS = 32768
N_SHARD = 128


def draw_tile_bits(key, part):
    return jax.random.randint(key, (TILES, WORDS, BLOCK), 0, 65536, dtype=jnp.int32)


def touch_ends(values, rng, least, largest):
    dims = values.shape
    spot = [jax.random.randint(jax.random.fold_in(rng, axis), (), 0, dims[axis]) for axis in range(len(dims))]
    values = values.at[tuple(spot)].set(least)
    longest = dims.index(max(dims))
    spot[longest] = (spot[longest] + 1) % dims[longest]
    return values.at[tuple(spot)].set(largest)


def steps_of(own_key, shape, shards, least, high):
    def one(position, parts):
        steps = jax.random.uniform(jax.random.fold_in(jax.random.fold_in(own_key, 6), position), (parts,), jnp.float32, least / len(shards), high / len(shards))
        return jnp.repeat(jnp.exp(steps), shape[position] // parts).reshape((-1,) + (1,) * (len(shape) - position - 1))

    level = one(*shards[0])
    for cut in shards[1:]:
        level = level * one(*cut)
    return level


def rank_table(amount, skew):
    portions = [(1 << 20) // math.isqrt(standing ** skew) + 1 for standing in range(1, amount + 1)]
    scale = 1 + sum(portions) // (1 << 30)
    return np.cumsum(np.array([max(1, weight // scale) for weight in portions]))


def ranked_ids(key, dims, count, skew):
    grid = rank_table(count, skew)
    pick = jax.random.randint(jax.random.fold_in(key, 1), dims, 0, int(grid[count - 1]))
    rank = jnp.searchsorted(jnp.asarray(grid, jnp.int32), pick, side="right")
    return jax.random.permutation(jax.random.fold_in(key, 2), count)[rank].astype(jnp.int32)


def gaussian(own_key, extent, deviation, reach, pieces=(), kind=jnp.bfloat16):
    values = jax.random.normal(own_key, extent, jnp.float32) * deviation
    if len(pieces) > 0:
        values = steps_of(own_key, extent, pieces, -0.22, 0.18) * values
    return jnp.clip(values, min=-reach, max=reach).astype(kind)


def setup_inputs(seed: int = 0) -> dict:
    splits = jax.random.split(jax.random.key(seed), 16)
    item_rows = gaussian(splits[0], (ITEMS, D), 1.0, 6.0, ((0, 128), (1, 2)), jnp.float32)
    first_moment = gaussian(splits[1], (ITEMS, D), 0.3, 2.0, ((0, 128), (1, 2)), jnp.float32)
    second_moment = jnp.clip(jnp.exp(math.log(4.0) - 5.9914646 * jax.random.uniform(splits[2], (ITEMS, D), jnp.float32) ** steps_of(splits[2], (ITEMS, D), ((0, 128), (1, 2)), -0.2, 0.2)), 0.01, 4.0)
    item_cot = gaussian(splits[3], (ITEMS, D), 1.0, 6.0, ((0, 128), (1, 2)))
    tile_bits = draw_tile_bits(jax.random.fold_in(splits[15], 71), 0)
    tile_item = touch_ends(ranked_ids(splits[5], (TILES,), ITEM_BLOCKS, 2), jax.random.fold_in(splits[5], 3), 0, ITEM_BLOCKS - 1).astype(jnp.int32)
    tile_dest = touch_ends(ranked_ids(splits[6], (TILES,), BASKET_BLOCKS, 2), jax.random.fold_in(splits[6], 3), 0, BASKET_BLOCKS - 1).astype(jnp.int32)
    basket_gain = jnp.clip(1.0 + 0.18 * jax.random.normal(splits[7], (D,), jnp.float32), 0.1, 1.9)
    item_gain = jnp.clip(1.0 + 0.18 * jax.random.normal(splits[8], (D,), jnp.float32), 0.1, 1.9)
    gate_basket = gaussian(splits[9], (D, FF), D ** -0.5, 0.375, ((1, 2),))
    up_basket = gaussian(splits[10], (D, FF), D ** -0.5, 0.375, ((1, 2),))
    down_basket = gaussian(splits[11], (FF, D), FF ** -0.5, 0.125, ((0, 2),))
    gate_item = gaussian(splits[12], (D, FF), D ** -0.5, 0.375, ((1, 2),))
    up_item = gaussian(splits[13], (D, FF), D ** -0.5, 0.375, ((1, 2),))
    down_item = gaussian(splits[14], (FF, D), FF ** -0.5, 0.125, ((0, 2),))
    return {"item_rows": item_rows, "first_moment": first_moment, "second_moment": second_moment, "item_cot": item_cot, "tile_bits": tile_bits, "tile_item": tile_item, "tile_dest": tile_dest, "basket_gain": basket_gain, "item_gain": item_gain, "gate_basket": gate_basket, "up_basket": up_basket, "down_basket": down_basket, "gate_item": gate_item, "up_item": up_item, "down_item": down_item}


NORM_EPSILON = 1e-05
LEARNING_RATE = 0.01
BETA_FIRST = 0.9
BETA_SECOND = 0.99
ADAM_EPSILON = 1e-08

def unpack_tiles(packed):
    shifts = jnp.arange(16, dtype=jnp.int32)
    bit_values = jnp.right_shift(packed[:, :, None, :], shifts[None, None, :, None]) & 1
    return bit_values.reshape(packed.shape[0], packed.shape[1] * 16, packed.shape[2]).astype(jnp.bfloat16)

def silu_parts(gate_values):
    sigmoid = jax.nn.sigmoid(gate_values)
    return (gate_values * sigmoid, sigmoid * (1.0 + gate_values * (1.0 - sigmoid)))

def rms_scale(values):
    return lax.rsqrt(lax.optimization_barrier(jnp.mean(values * values, axis=-1, keepdims=True)) + NORM_EPSILON)

def reference(item_rows, first_moment, second_moment, item_cot, tile_bits, tile_item, tile_dest, basket_gain, item_gain, gate_basket, up_basket, down_basket, gate_item, up_item, down_item):
    packed_all = tile_bits.reshape(N_SHARD, TILE_DEV, BLOCK // 16, BLOCK)
    item_index = tile_item.reshape(N_SHARD, TILE_DEV).astype(jnp.int32)
    dest_index = tile_dest.reshape(N_SHARD, TILE_DEV).astype(jnp.int32)

    def owner_sum(source):

        def add_device(total, inputs):
            packed_dev, item_dev, dest_dev, source_dev = inputs
            masks = unpack_tiles(packed_dev).astype(jnp.float32)
            picked = jnp.take(source_dev, item_dev, axis=0).astype(jnp.float32)
            partial_sums = jnp.einsum('tib,tif->tbf', masks, picked)
            return (total + jax.ops.segment_sum(partial_sums, dest_dev, num_segments=N_SHARD), None)
        start_total = jnp.zeros((N_SHARD, BLOCK, D), jnp.float32)
        total, unused = lax.scan(add_device, start_total, (packed_all, item_index, dest_index, source))
        return total.reshape(N_SHARD * BLOCK, D)

    def owner_spread(blocks):
        blocks = blocks.reshape(N_SHARD, BLOCK, D)

        def one_device(inputs):
            packed_dev, item_dev, dest_dev = inputs
            masks = unpack_tiles(packed_dev).astype(jnp.float32)
            selected = jnp.take(blocks, dest_dev, axis=0).astype(jnp.float32)
            contrib = jnp.einsum('tib,tbf->tif', masks, selected)
            return jax.ops.segment_sum(contrib, item_dev, num_segments=ITEM_BLOCKS)
        spread = lax.map(one_device, (packed_all, item_index, dest_index))
        return spread.reshape(N_SHARD * ITEM_BLOCKS * BLOCK, D)
    rows_bf = item_rows.astype(jnp.bfloat16).reshape(N_SHARD, ITEM_BLOCKS, BLOCK, D)
    basket_sum = owner_sum(rows_bf)
    scale_basket = rms_scale(basket_sum)
    normed = basket_sum * scale_basket * basket_gain
    normed_bf = normed.astype(jnp.bfloat16)
    gate_pre = jnp.dot(normed_bf, gate_basket, preferred_element_type=jnp.float32)
    up_pre = jnp.dot(normed_bf, up_basket, preferred_element_type=jnp.float32)
    silu_value, silu_slope = silu_parts(gate_pre)
    hidden = (silu_value * up_pre).astype(jnp.bfloat16)
    basket_out = (normed + jnp.dot(hidden, down_basket, preferred_element_type=jnp.float32)).astype(jnp.bfloat16)
    message = owner_spread(basket_out)

    def item_backward(inputs):
        message_dev, cot_dev = inputs
        scale_item = rms_scale(message_dev)
        query = (message_dev * scale_item * item_gain).astype(jnp.bfloat16)
        gate_item_pre = jnp.dot(query, gate_item, preferred_element_type=jnp.float32)
        up_item_pre = jnp.dot(query, up_item, preferred_element_type=jnp.float32)
        item_value, item_slope = silu_parts(gate_item_pre)
        grad_hidden = jnp.dot(cot_dev, down_item.T, preferred_element_type=jnp.float32)
        grad_up = (grad_hidden * item_value).astype(jnp.bfloat16)
        grad_gate = (grad_hidden * up_item_pre * item_slope).astype(jnp.bfloat16)
        grad_query = jnp.dot(grad_gate, gate_item.T, preferred_element_type=jnp.float32) + jnp.dot(grad_up, up_item.T, preferred_element_type=jnp.float32)
        inner = lax.optimization_barrier(jnp.sum(item_gain * grad_query * message_dev, axis=1, keepdims=True))
        cubed = scale_item * scale_item * scale_item
        grad_message = scale_item * item_gain * grad_query - message_dev * cubed * inner / D
        return grad_message.astype(jnp.bfloat16)
    grad_message = lax.map(item_backward, (message.reshape(N_SHARD, ITEM_BLOCKS * BLOCK, D), item_cot.reshape(N_SHARD, ITEM_BLOCKS * BLOCK, D)))
    grad_out = owner_sum(grad_message.reshape(N_SHARD, ITEM_BLOCKS, BLOCK, D))
    grad_out_bf = grad_out.astype(jnp.bfloat16)
    grad_basket_hidden = jnp.dot(grad_out_bf, down_basket.T, preferred_element_type=jnp.float32)
    grad_basket_up = (grad_basket_hidden * silu_value).astype(jnp.bfloat16)
    grad_basket_gate = (grad_basket_hidden * up_pre * silu_slope).astype(jnp.bfloat16)
    grad_normed = grad_out + (jnp.dot(grad_basket_gate, gate_basket.T, preferred_element_type=jnp.float32) + jnp.dot(grad_basket_up, up_basket.T, preferred_element_type=jnp.float32))
    inner_basket = lax.optimization_barrier(jnp.sum(basket_gain * grad_normed * basket_sum, axis=1, keepdims=True))
    cubed_basket = scale_basket * scale_basket * scale_basket
    grad_sum = (scale_basket * basket_gain * grad_normed - basket_sum * cubed_basket * inner_basket / D).astype(jnp.bfloat16)
    back_items = owner_spread(grad_sum)
    gradient = item_cot.astype(jnp.float32) + back_items
    new_first = BETA_FIRST * first_moment + (1.0 - BETA_FIRST) * gradient
    new_second = BETA_SECOND * second_moment + (1.0 - BETA_SECOND) * gradient * gradient
    new_rows = item_rows - LEARNING_RATE * new_first / (jnp.sqrt(new_second) + ADAM_EPSILON)
    return (new_rows, new_first, new_second)
```

```python
import jax
import jax.numpy as jnp
from jax import lax
from jax.experimental import pallas as pl
from jax.experimental.pallas import tpu as pltpu
from jax.sharding import PartitionSpec as P

D = 256
HALF = 128
BLOCK = 128
TILE_DEV = 16
RING = 8
PLANE = 16
COLUMNS = 16
OWN = 64
HIDDEN = 1024

NORM_EPSILON = 1e-05
LEARNING_RATE = 0.01
BETA_FIRST = 0.9
BETA_SECOND = 0.99
ADAM_EPSILON = 1e-08

MESH = pl.DeviceIdType.MESH
BF = jnp.bfloat16
F32 = jnp.float32


def dot(a, b):
    return jnp.dot(a, b, preferred_element_type=F32)


def dot_nt(a, b):
    return lax.dot_general(a, b, (((1,), (1,)), ((), ())), preferred_element_type=F32)


def silu_parts(gate_values):
    sigmoid = jax.nn.sigmoid(gate_values)
    return (gate_values * sigmoid, sigmoid * (1.0 + gate_values * (1.0 - sigmoid)))


def rms_scale(values):
    return lax.rsqrt(jnp.mean(values * values, axis=-1, keepdims=True) + NORM_EPSILON)


def rows16(start, size):
    return pl.ds(pl.multiple_of(start, 16), size)


def kernel(
    rows_ref,
    cot_ref,
    bits_ref,
    item_ref,
    dest_ref,
    gain_b_ref,
    gain_i_ref,
    gate_b_ref,
    up_b_ref,
    down_b_ref,
    gate_i_ref,
    up_i_ref,
    down_i_ref,
    back_ref,
    wide,
    tall,
    words_out,
    words_in,
    ring_rows,
    spread_mat,
    collect_mat,
    select_cols,
    select_rows,
    tile_sums,
    owner_out,
    owner_in,
    block_out,
    block_in,
    picked,
    item_out,
    item_in,
    back_in,
    grad_out_buf,
    cot_whole,
    gate_keep,
    up_keep,
    sum_keep,
    weight_own,
    weight_send,
    weight_recv,
    cot_send,
    cot_recv,
    words_send,
    words_recv,
    rows_send,
    rows_recv,
    grad_send,
    grad_recv,
    item_send,
    item_recv,
    back_send,
    back_recv,
    owner_send,
    owner_recv,
    block_send,
    block_recv,
):
    shard = lax.axis_index("shard")
    m = lax.axis_index("mp")
    other = 1 - m
    z = lax.div(shard, PLANE)
    q = lax.rem(shard, PLANE)
    me = 2 * q + m

    def remote(src, dst, send, recv, z_to, q_to, m_to):
        return pltpu.make_async_remote_copy(
            src_ref=src,
            dst_ref=dst,
            send_sem=send,
            recv_sem=recv,
            device_id=(z_to * PLANE + q_to, m_to),
            device_id_type=MESH,
        )

    weights = (
        (gate_b_ref, wide.at[0]),
        (up_b_ref, wide.at[1]),
        (down_b_ref, tall.at[0]),
        (gate_i_ref, wide.at[2]),
        (up_i_ref, wide.at[3]),
        (down_i_ref, tall.at[1]),
    )

    def own_weight(n):
        src, dst = weights[n]
        return pltpu.make_async_copy(src, dst.at[m], weight_own.at[n])

    def sibling_weight(n):
        src, dst = weights[n]
        return remote(src, dst.at[m], weight_send.at[n], weight_recv.at[n], z, q, other)

    barrier = pltpu.get_barrier_semaphore()

    def greet_plane(step, carry):
        k = lax.rem(me + step, 2 * PLANE)
        pl.semaphore_signal(
            barrier,
            inc=1,
            device_id=(z * PLANE + lax.div(k, 2), lax.rem(k, 2)),
            device_id_type=MESH,
        )
        return carry

    def greet_ring(step, carry):
        z_to = lax.rem(z + step, RING)
        for m_to in range(2):
            pl.semaphore_signal(
                barrier, inc=1, device_id=(z_to * PLANE + q, m_to), device_id_type=MESH
            )
        return carry

    lax.fori_loop(1, 2 * PLANE, greet_plane, 0)
    lax.fori_loop(1, RING, greet_ring, 0)
    for n in range(6):
        own_weight(n).start()

    ring_rows[0, z] = rows_ref[...].astype(BF)
    sub = lax.broadcasted_iota(jnp.int32, (8, 128), 0)
    lane = lax.broadcasted_iota(jnp.int32, (8, 128), 1)
    group = lane // COLUMNS
    items = []
    for half in range(2):
        values = jnp.zeros((8, 128), jnp.int32)
        for t in range(8):
            values = jnp.where(group == t, item_ref[half * 8 + t], values)
        items.append(values)
    dests = jnp.zeros((8, 128), jnp.int32)
    for t in range(TILE_DEV):
        dests = jnp.where(lane == z * TILE_DEV + t, dest_ref[t], dests)
    about = jnp.where(sub == 0, items[0], jnp.where(sub == 1, items[1], dests))
    for z_to in range(RING):
        for half in range(2):
            values = jnp.zeros((8, 128), jnp.int32)
            for t in range(8):
                shift = (COLUMNS * (t - z_to)) % 128
                turned = bits_ref[half * 8 + t]
                if shift:
                    turned = pltpu.roll(turned, shift, 1)
                values = jnp.where(group == t, turned, values)
            words_out[z_to, half] = values
        words_out[z_to, 2] = about
    words_in[z] = words_out[z]

    pl.semaphore_wait(barrier, 2 * PLANE - 1 + 2 * (RING - 1))

    def words_copy(z_to):
        return remote(
            words_out.at[z_to], words_in.at[z], words_send.at[z_to], words_recv.at[z], z_to, q, m
        )

    def rows_copy(z_to):
        return remote(
            ring_rows.at[0, z],
            ring_rows.at[0, z],
            rows_send.at[z_to],
            rows_recv.at[z],
            z_to,
            q,
            m,
        )

    def start_ring(step, carry):
        z_to = lax.rem(z + step, RING)
        words_copy(z_to).start()
        rows_copy(z_to).start()
        return carry

    lax.fori_loop(1, RING, start_ring, 0)

    def cot_copy():
        return remote(
            cot_ref.at[rows16(other * BLOCK, BLOCK)],
            cot_whole.at[m],
            cot_send,
            cot_recv,
            z,
            q,
            other,
        )

    for n in range(3):
        sibling_weight(n).start()
    cot_copy().start()
    for n in range(3, 6):
        sibling_weight(n).start()
    cot_whole[m] = cot_ref[rows16(m * BLOCK, BLOCK), :]

    def wait_words(z_from):
        remote(
            words_in.at[z_from],
            words_in.at[z_from],
            words_send.at[z],
            words_recv.at[z_from],
            z,
            q,
            other,
        ).wait_recv()

    def wait_rows(z_from):
        remote(
            ring_rows.at[0, z_from],
            ring_rows.at[0, z_from],
            rows_send.at[z],
            rows_recv.at[z_from],
            z,
            q,
            other,
        ).wait_recv()

    left = lax.broadcasted_iota(jnp.int32, (256, 256), 0)
    right = lax.broadcasted_iota(jnp.int32, (256, 256), 1)
    swap = jnp.where(
        (left // COLUMNS == right % COLUMNS) & (left % COLUMNS == right // COLUMNS), 1.0, 0.0
    ).astype(BF)

    def unpack(z_from):
        about_in = words_in[z_from, 2]
        shifts = lax.broadcasted_iota(jnp.int32, (8, 16, 128), 1)
        halves = []
        for half in range(2):
            packed = jnp.broadcast_to(words_in[z_from, half][:, None, :], (8, 16, 128))
            bits = (jnp.right_shift(packed, shifts) & 1).reshape(128, 128).astype(F32)
            halves.append((bits, jnp.broadcast_to(about_in[half : half + 1, :], (128, 128))))
        blocks = []
        for block in range(2):
            blocks.append(
                jnp.concatenate(
                    [jnp.where(item == block, bits, 0.0) for bits, item in halves], axis=1
                )
            )
        mat = jnp.concatenate(blocks, axis=0).astype(BF)
        spread_mat[z_from] = dot(mat, swap).astype(BF)
        collect_mat[z_from] = dot_nt(swap, mat).astype(BF)

    def add_tiles(phase, z_from):
        sums = dot(collect_mat[z_from], ring_rows[phase, z_from])
        high = sums.astype(BF)
        low = (sums - high.astype(F32)).astype(BF)
        tile_sums[:, rows16(z_from * TILE_DEV, TILE_DEV), :] = high.reshape(16, 16, 128)
        tile_sums[:, rows16(BLOCK + z_from * TILE_DEV, TILE_DEV), :] = low.reshape(16, 16, 128)

    unpack(z)
    add_tiles(0, z)

    def take_ring(step, carry):
        z_from = lax.rem(z + step, RING)
        wait_words(z_from)
        unpack(z_from)
        wait_rows(z_from)
        add_tiles(0, z_from)
        return carry

    lax.fori_loop(1, RING, take_ring, 0)

    all_dest = words_in[0, 2][2:3, :]
    for z_from in range(1, RING):
        all_dest = all_dest + words_in[z_from, 2][2:3, :]
    block_of = lax.broadcasted_iota(jnp.int32, (128, 128), 0)
    column_of = lax.broadcasted_iota(jnp.int32, (128, 128), 1)
    one_hot = jnp.where(block_of == all_dest, 1.0, 0.0).astype(BF)
    select_cols[...] = jnp.concatenate([one_hot, one_hot], axis=1)
    eye = jnp.where(block_of == column_of, 1.0, 0.0).astype(BF)
    select_rows[...] = dot_nt(eye, one_hot).astype(BF)

    def owner_copy(phase, q_to, m_to):
        return remote(
            owner_out.at[phase, q_to, rows16(m_to * OWN, OWN)],
            owner_in.at[phase, q, m],
            owner_send.at[phase, q_to, m_to],
            owner_recv.at[phase, q, m],
            z,
            q_to,
            m_to,
        )

    def block_copy(phase, q_to, m_to):
        return remote(
            block_out.at[phase, m_to],
            block_in.at[phase, q, rows16(m * OWN, OWN)],
            block_send.at[phase, q_to, m_to],
            block_recv.at[phase, q, m],
            z,
            q_to,
            m_to,
        )

    def sum_at_owners(phase):
        def send_column(step, carry):
            j = lax.rem(q + step, PLANE)
            owner_out[phase, j] = dot(select_cols[...], tile_sums[j]).astype(BF)
            for m_to in range(2):
                owner_copy(phase, j, m_to).start()
            return carry

        lax.fori_loop(1, PLANE, send_column, 0)
        owner_out[phase, q] = dot(select_cols[...], tile_sums[q]).astype(BF)
        owner_copy(phase, q, other).start()
        owner_in[phase, q, m] = owner_out[phase, q, rows16(m * OWN, OWN), :]

        def take(step, carry):
            k = lax.rem(me + step, 2 * PLANE)
            q_from, m_from = lax.div(k, 2), lax.rem(k, 2)
            remote(
                owner_in.at[phase, q_from, m_from],
                owner_in.at[phase, q_from, m_from],
                owner_send.at[phase, q, m],
                owner_recv.at[phase, q_from, m_from],
                z,
                q,
                other,
            ).wait_recv()
            return carry

        lax.fori_loop(1, 2 * PLANE, take, 0)
        halves = []
        for m_from in range(2):
            total = owner_in[phase, 0, m_from].astype(F32)
            for q_from in range(1, PLANE):
                total = total + owner_in[phase, q_from, m_from].astype(F32)
            halves.append(total)
        return jnp.concatenate(halves, axis=1)

    def send_blocks(phase, values):
        for m_to in range(2):
            block_out[phase, m_to] = values[:, m_to * HALF : (m_to + 1) * HALF]

        def send(step, carry):
            k = lax.rem(me + step, 2 * PLANE)
            block_copy(phase, lax.div(k, 2), lax.rem(k, 2)).start()
            return carry

        lax.fori_loop(1, 2 * PLANE, send, 0)
        block_in[phase, q, rows16(m * OWN, OWN), :] = block_out[phase, m]

    def wait_block(phase, q_from, m_from):
        remote(
            block_out.at[phase, m_from],
            block_in.at[phase, q_from, rows16(m_from * OWN, OWN)],
            block_send.at[phase, q, m],
            block_recv.at[phase, q_from, m_from],
            z,
            q,
            other,
        ).wait_recv()

    def pick(phase, j):
        chosen = dot(select_rows[...], block_in[phase, j]).astype(BF)
        picked[:, rows16(j * COLUMNS, COLUMNS), :] = chosen.reshape(8, 16, 128)

    def pick_all(phase):
        wait_block(phase, q, other)
        pick(phase, q)

        def step_pick(step, carry):
            j = lax.rem(q + PLANE - step, PLANE)
            for m_from in range(2):
                wait_block(phase, j, m_from)
            pick(phase, j)
            return carry

        lax.fori_loop(1, PLANE, step_pick, 0)

    basket_gain = gain_b_ref[...]
    item_gain = gain_i_ref[...]

    basket_sum = sum_at_owners(0)
    sum_keep[...] = basket_sum
    for n in range(3):
        own_weight(n).wait()
        sibling_weight(n).wait_recv()
    normed = basket_sum * rms_scale(basket_sum) * basket_gain
    normed_bf = normed.astype(BF)
    total = normed
    for h in range(2):
        gate_pre = dot(normed_bf, wide[0, h])
        up_pre = dot(normed_bf, wide[1, h])
        gate_keep[h] = gate_pre
        up_keep[h] = up_pre
        hidden = (gate_pre * jax.nn.sigmoid(gate_pre) * up_pre).astype(BF)
        total = total + dot(hidden, tall[0, h])
    send_blocks(0, total.astype(BF))
    pick_all(0)

    def item_copy(z_to, m_to):
        return remote(
            item_out.at[0, z_to, rows16(m_to * BLOCK, BLOCK)],
            item_in.at[z, m],
            item_send.at[z_to, m_to],
            item_recv.at[z, m],
            z_to,
            q,
            m_to,
        )

    def send_items(step, carry):
        z_to = lax.rem(z + step, RING)
        item_out[0, z_to] = dot(spread_mat[z_to], picked[z_to]).astype(BF)
        for m_to in range(2):
            item_copy(z_to, m_to).start()
        return carry

    lax.fori_loop(1, RING, send_items, 0)
    item_out[0, z] = dot(spread_mat[z], picked[z]).astype(BF)
    item_copy(z, other).start()
    item_in[z, m] = item_out[0, z, rows16(m * BLOCK, BLOCK), :]

    def wait_item(z_from, m_from):
        remote(
            item_in.at[z_from, m_from],
            item_in.at[z_from, m_from],
            item_send.at[z, m],
            item_recv.at[z_from, m_from],
            z,
            q,
            other,
        ).wait_recv()

    for n in range(3, 6):
        own_weight(n).wait()
        sibling_weight(n).wait_recv()
    cot_copy_in = remote(
        cot_whole.at[other], cot_whole.at[other], cot_send, cot_recv, z, q, other
    )
    cot_copy_in.wait_recv()
    wait_item(z, other)

    def take_items(step, carry):
        z_from = lax.rem(z + step, RING)
        for m_from in range(2):
            wait_item(z_from, m_from)
        return carry

    lax.fori_loop(1, RING, take_items, 0)
    halves = []
    for m_from in range(2):
        summed = item_in[0, m_from].astype(F32)
        for z_from in range(1, RING):
            summed = summed + item_in[z_from, m_from].astype(F32)
        halves.append(summed)
    message = jnp.concatenate(halves, axis=1)
    cot_full = jnp.concatenate([cot_whole[0], cot_whole[1]], axis=1)
    scale_item = rms_scale(message)
    query = (message * scale_item * item_gain).astype(BF)
    grad_query = jnp.zeros((BLOCK, D), F32)
    for h in range(2):
        gate_pre = dot(query, wide[2, h])
        up_pre = dot(query, wide[3, h])
        grad_hidden = dot_nt(cot_full, tall[1, h])
        value, slope = silu_parts(gate_pre)
        grad_up = (grad_hidden * value).astype(BF)
        grad_gate = (grad_hidden * up_pre * slope).astype(BF)
        grad_query = grad_query + dot_nt(grad_gate, wide[2, h]) + dot_nt(grad_up, wide[3, h])
    inner = jnp.sum(item_gain * grad_query * message, axis=1, keepdims=True)
    cubed = scale_item * scale_item * scale_item
    grad_message = (scale_item * item_gain * grad_query - message * cubed * inner / D).astype(BF)
    for m_to in range(2):
        grad_out_buf[m_to] = grad_message[:, m_to * HALF : (m_to + 1) * HALF]

    def grad_copy(z_to, m_to):
        return remote(
            grad_out_buf.at[m_to],
            ring_rows.at[1, z, rows16(m * BLOCK, BLOCK)],
            grad_send.at[z_to, m_to],
            grad_recv.at[z, m],
            z_to,
            q,
            m_to,
        )

    def send_grads(step, carry):
        z_to = lax.rem(z + step, RING)
        for m_to in range(2):
            grad_copy(z_to, m_to).start()
        return carry

    grad_copy(z, other).start()
    lax.fori_loop(1, RING, send_grads, 0)
    ring_rows[1, z, rows16(m * BLOCK, BLOCK), :] = grad_out_buf[m]

    def wait_grad(z_from, m_from):
        remote(
            grad_out_buf.at[m_from],
            ring_rows.at[1, z_from, rows16(m_from * BLOCK, BLOCK)],
            grad_send.at[z, m],
            grad_recv.at[z_from, m_from],
            z,
            q,
            other,
        ).wait_recv()

    wait_grad(z, other)
    add_tiles(1, z)

    def take_grads(step, carry):
        z_from = lax.rem(z + step, RING)
        for m_from in range(2):
            wait_grad(z_from, m_from)
        add_tiles(1, z_from)
        return carry

    lax.fori_loop(1, RING, take_grads, 0)
    grad_out = sum_at_owners(1)
    grad_out_bf = grad_out.astype(BF)
    grad_normed = grad_out
    for h in range(2):
        grad_hidden = dot_nt(grad_out_bf, tall[0, h])
        value, slope = silu_parts(gate_keep[h])
        grad_up = (grad_hidden * value).astype(BF)
        grad_gate = (grad_hidden * up_keep[h] * slope).astype(BF)
        grad_normed = grad_normed + (dot_nt(grad_gate, wide[0, h]) + dot_nt(grad_up, wide[1, h]))
    sums = sum_keep[...]
    scale_basket = rms_scale(sums)
    inner_basket = jnp.sum(basket_gain * grad_normed * sums, axis=1, keepdims=True)
    cubed_basket = scale_basket * scale_basket * scale_basket
    grad_sum = scale_basket * basket_gain * grad_normed - sums * cubed_basket * inner_basket / D
    send_blocks(1, grad_sum.astype(BF))
    pick_all(1)

    def back_copy(z_to):
        return remote(
            item_out.at[1, z_to], back_in.at[z], back_send.at[z_to], back_recv.at[z], z_to, q, m
        )

    def send_back(step, carry):
        z_to = lax.rem(z + step, RING)
        item_out[1, z_to] = dot(spread_mat[z_to], picked[z_to]).astype(BF)
        back_copy(z_to).start()
        return carry

    lax.fori_loop(1, RING, send_back, 0)
    back_in[z] = dot(spread_mat[z], picked[z]).astype(BF)

    def take_back(step, carry):
        z_from = lax.rem(z + step, RING)
        remote(
            back_in.at[z_from],
            back_in.at[z_from],
            back_send.at[z],
            back_recv.at[z_from],
            z,
            q,
            other,
        ).wait_recv()
        return carry

    lax.fori_loop(1, RING, take_back, 0)
    back = back_in[0].astype(F32)
    for z_from in range(1, RING):
        back = back + back_in[z_from].astype(F32)
    back_ref[...] = back

    for n in range(6):
        sibling_weight(n).wait_send()
    cot_copy().wait_send()
    item_copy(z, other).wait_send()
    grad_copy(z, other).wait_send()

    def drain_ring(step, carry):
        z_to = lax.rem(z + step, RING)
        words_copy(z_to).wait_send()
        rows_copy(z_to).wait_send()
        for m_to in range(2):
            item_copy(z_to, m_to).wait_send()
            grad_copy(z_to, m_to).wait_send()
        back_copy(z_to).wait_send()
        return carry

    lax.fori_loop(1, RING, drain_ring, 0)

    def drain_plane(step, carry):
        k = lax.rem(me + step, 2 * PLANE)
        q_to, m_to = lax.div(k, 2), lax.rem(k, 2)
        for phase in range(2):
            owner_copy(phase, q_to, m_to).wait_send()
            block_copy(phase, q_to, m_to).wait_send()
        return carry

    lax.fori_loop(1, 2 * PLANE, drain_plane, 0)


def local(
    item_rows,
    first_moment,
    second_moment,
    item_cot,
    tile_bits,
    tile_item,
    tile_dest,
    basket_gain,
    item_gain,
    gate_basket,
    up_basket,
    down_basket,
    gate_item,
    up_item,
    down_item,
):
    vmem = pl.BlockSpec(memory_space=pltpu.VMEM)
    smem = pl.BlockSpec(memory_space=pltpu.SMEM)
    anywhere = pl.BlockSpec(memory_space=pl.ANY)
    dma = pltpu.SemaphoreType.DMA
    back_items = pl.pallas_call(
        kernel,
        out_shape=jax.ShapeDtypeStruct((2 * BLOCK, HALF), F32),
        in_specs=[vmem, vmem, vmem, smem, smem, vmem, vmem] + [anywhere] * 6,
        out_specs=vmem,
        scratch_shapes=[
            pltpu.VMEM((4, 2, D, HIDDEN), BF),
            pltpu.VMEM((2, 2, HIDDEN, D), BF),
            pltpu.VMEM((RING, 3, 8, 128), jnp.int32),
            pltpu.VMEM((RING, 3, 8, 128), jnp.int32),
            pltpu.VMEM((2, RING, 2 * BLOCK, HALF), BF),
            pltpu.VMEM((RING, 256, 256), BF),
            pltpu.VMEM((RING, 256, 256), BF),
            pltpu.VMEM((128, 256), BF),
            pltpu.VMEM((128, 128), BF),
            pltpu.VMEM((COLUMNS, 256, HALF), BF),
            pltpu.VMEM((2, PLANE, 128, HALF), BF),
            pltpu.VMEM((2, PLANE, 2, OWN, HALF), BF),
            pltpu.VMEM((2, 2, OWN, HALF), BF),
            pltpu.VMEM((2, PLANE, 128, HALF), BF),
            pltpu.VMEM((RING, 256, HALF), BF),
            pltpu.VMEM((2, RING, 256, HALF), BF),
            pltpu.VMEM((RING, 2, BLOCK, HALF), BF),
            pltpu.VMEM((RING, 256, HALF), BF),
            pltpu.VMEM((2, BLOCK, HALF), BF),
            pltpu.VMEM((2, BLOCK, HALF), BF),
            pltpu.VMEM((2, OWN, HIDDEN), F32),
            pltpu.VMEM((2, OWN, HIDDEN), F32),
            pltpu.VMEM((OWN, D), F32),
            dma((6,)),
            dma((6,)),
            dma((6,)),
            dma,
            dma,
            dma((RING,)),
            dma((RING,)),
            dma((RING,)),
            dma((RING,)),
            dma((RING, 2)),
            dma((RING, 2)),
            dma((RING, 2)),
            dma((RING, 2)),
            dma((RING,)),
            dma((RING,)),
            dma((2, PLANE, 2)),
            dma((2, PLANE, 2)),
            dma((2, PLANE, 2)),
            dma((2, PLANE, 2)),
        ],
        compiler_params=pltpu.CompilerParams(
            collective_id=0, has_side_effects=True, vmem_limit_bytes=48 * 1024 * 1024
        ),
        name="layer",
    )(
        item_rows,
        item_cot,
        tile_bits,
        tile_item,
        tile_dest,
        basket_gain.reshape(1, D),
        item_gain.reshape(1, D),
        gate_basket,
        up_basket,
        down_basket,
        gate_item,
        up_item,
        down_item,
    )
    gradient = item_cot.astype(F32) + back_items
    new_first = BETA_FIRST * first_moment + (1.0 - BETA_FIRST) * gradient
    new_second = BETA_SECOND * second_moment + (1.0 - BETA_SECOND) * gradient * gradient
    new_rows = item_rows - LEARNING_RATE * new_first / (jnp.sqrt(new_second) + ADAM_EPSILON)
    return (new_rows, new_first, new_second)


def solution(mesh):
    split = P("shard", "mp")
    return jax.shard_map(
        local,
        mesh=mesh,
        in_specs=(
            split,
            split,
            split,
            split,
            P("shard", None, None),
            P("shard"),
            P("shard"),
            P(),
            P(),
            P(None, "mp"),
            P(None, "mp"),
            P("mp", None),
            P(None, "mp"),
            P(None, "mp"),
            P("mp", None),
        ),
        out_specs=(split, split, split),
        check_vma=False,
    )
```

```python
import jax
import jax.numpy as jnp
from jax import lax
from jax.experimental import pallas as pl
from jax.experimental.pallas import tpu as pltpu
from jax.sharding import PartitionSpec as P

D = 256
HALF = 128
BLOCK = 128
TILE_DEV = 16
RING = 8
PLANE = 16
OWN = 64
HIDDEN = 1024

NORM_EPSILON = 1e-05
LEARNING_RATE = 0.01
BETA_FIRST = 0.9
BETA_SECOND = 0.99
ADAM_EPSILON = 1e-08

MESH = pl.DeviceIdType.MESH
BF = jnp.bfloat16
F32 = jnp.float32


def dot(a, b):
    return jnp.dot(a, b, preferred_element_type=F32)


def dot_nt(a, b):
    return lax.dot_general(a, b, (((1,), (1,)), ((), ())), preferred_element_type=F32)


def silu_parts(gate_values):
    sigmoid = jax.nn.sigmoid(gate_values)
    return (gate_values * sigmoid, sigmoid * (1.0 + gate_values * (1.0 - sigmoid)))


def rms_scale(values):
    return lax.rsqrt(jnp.mean(values * values, axis=-1, keepdims=True) + NORM_EPSILON)


def rows16(start, size):
    return pl.ds(pl.multiple_of(start, 16), size)


def mode_scratch(members, columns):
    dma = pltpu.SemaphoreType.DMA
    wide = TILE_DEV * columns
    tiles = TILE_DEV * members
    slots = wide // 128 + 1
    return {
        "words_out": pltpu.VMEM((members, slots, 8, 128), jnp.int32),
        "words_in": pltpu.VMEM((members, slots, 8, 128), jnp.int32),
        "rows": pltpu.VMEM((2, members, 2 * BLOCK, HALF), BF),
        "spread": pltpu.VMEM((members, 2 * BLOCK, wide), BF),
        "collect": pltpu.VMEM((members, wide, 2 * BLOCK), BF),
        "select_cols": pltpu.VMEM((BLOCK, 2 * tiles), BF),
        "select_rows": pltpu.VMEM((tiles, BLOCK), BF),
        "tile_sums": pltpu.VMEM((columns, 2 * tiles, HALF), BF),
        "owner_out": pltpu.VMEM((2, columns, BLOCK, HALF), BF),
        "owner_in": pltpu.VMEM((2, columns, OWN, HALF), BF),
        "block_out": pltpu.VMEM((2, OWN, HALF), BF),
        "block_in": pltpu.VMEM((2, columns, BLOCK, HALF), BF),
        "picked": pltpu.VMEM((members, wide, HALF), BF),
        "item_out": pltpu.VMEM((2, members, 2 * BLOCK, HALF), BF),
        "item_in": pltpu.VMEM((members, BLOCK, HALF), BF),
        "back_in": pltpu.VMEM((members, 2 * BLOCK, HALF), BF),
        "grad_out": pltpu.VMEM((BLOCK, HALF), BF),
        "words_send": dma((members,)),
        "words_recv": dma((members,)),
        "rows_send": dma((members,)),
        "rows_recv": dma((members,)),
        "owner_send": dma((2, columns, 2)),
        "owner_recv": dma((2, columns)),
        "block_send": dma((2, columns)),
        "block_recv": dma((2, columns, 2)),
        "item_send": dma((members, 2)),
        "item_recv": dma((members,)),
        "grad_send": dma((members,)),
        "grad_recv": dma((members, 2)),
        "back_send": dma((members,)),
        "back_recv": dma((members,)),
    }


def common_scratch():
    dma = pltpu.SemaphoreType.DMA
    return {
        "wide": pltpu.VMEM((4, 2, D, HIDDEN), BF),
        "tall": pltpu.VMEM((2, 2, HIDDEN, D), BF),
        "cot_whole": pltpu.VMEM((2, BLOCK, HALF), BF),
        "gate_keep": pltpu.VMEM((2, OWN, HIDDEN), F32),
        "up_keep": pltpu.VMEM((2, OWN, HIDDEN), F32),
        "sum_keep": pltpu.VMEM((OWN, D), F32),
        "item_rows": pltpu.VMEM((2 * BLOCK, HALF), F32),
        "tile_bits": pltpu.VMEM((TILE_DEV, 8, 128), jnp.int32),
        "load_sem": dma((3,)),
        "weight_own": dma((6,)),
        "weight_send": dma((6,)),
        "weight_recv": dma((6,)),
        "cot_send": dma,
        "cot_recv": dma,
    }


class Mode:
    def __init__(self, core, refs, z, q):
        self.core = core
        self.members, self.columns = (RING, PLANE) if core == 0 else (PLANE, RING)
        self.own_member, self.own_column = (z, q) if core == 0 else (q, z)
        self.z, self.q = z, q
        self.__dict__.update(refs)

    def item_shard(self, member):
        return member * PLANE + self.q if self.core == 0 else self.z * PLANE + member

    def basket_shard(self, column):
        return self.z * PLANE + column if self.core == 0 else column * PLANE + self.q


def kernel(
    rows_hbm,
    cot_hbm,
    bits_hbm,
    item_ref,
    dest_ref,
    gain_b_ref,
    gain_i_ref,
    gate_b_ref,
    up_b_ref,
    down_b_ref,
    gate_i_ref,
    up_i_ref,
    down_i_ref,
    back_ref,
    common,
    ring_refs,
    plane_refs,
):
    shard = lax.axis_index("shard")
    m = lax.axis_index("mp")
    other = 1 - m
    z = lax.div(shard, PLANE)
    q = lax.rem(shard, PLANE)
    me = 2 * q + m
    modes = (Mode(0, ring_refs, z, q), Mode(1, plane_refs, z, q))
    wide, tall, cot_whole = common["wide"], common["tall"], common["cot_whole"]
    gate_keep, up_keep, sum_keep = common["gate_keep"], common["up_keep"], common["sum_keep"]
    rows_ref, bits_ref, load_sem = common["item_rows"], common["tile_bits"], common["load_sem"]
    weight_own, weight_send = common["weight_own"], common["weight_send"]
    weight_recv = common["weight_recv"]
    cot_send, cot_recv = common["cot_send"], common["cot_recv"]

    def remote(src, dst, send, recv, to_shard, to_core):
        return pltpu.make_async_remote_copy(
            src_ref=src,
            dst_ref=dst,
            send_sem=send,
            recv_sem=recv,
            device_id=(to_shard, to_core),
            device_id_type=MESH,
        )

    def arrival(dst, send, recv):
        return remote(dst, dst, send, recv, shard, other)

    def around(count, own, body):
        def step(n, carry):
            body(lax.rem(own + n, count))
            return carry

        lax.fori_loop(1, count, step, 0)

    def back_around(count, own, body):
        def step(n, carry):
            body(lax.rem(own + count - n, count))
            return carry

        lax.fori_loop(1, count, step, 0)

    def per_mode(body):
        for mode in modes:

            @pl.when(m == mode.core)
            def _(mode=mode):
                body(mode)

    weights = (
        (gate_b_ref, wide.at[0]),
        (up_b_ref, wide.at[1]),
        (down_b_ref, tall.at[0]),
        (gate_i_ref, wide.at[2]),
        (up_i_ref, wide.at[3]),
        (down_i_ref, tall.at[1]),
    )

    def own_weight(n):
        src, dst = weights[n]
        return pltpu.make_async_copy(src, dst.at[m], weight_own.at[n])

    def sibling_weight(n):
        src, dst = weights[n]
        return remote(src, dst.at[m], weight_send.at[n], weight_recv.at[n], shard, other)

    load_rows = pltpu.make_async_copy(rows_hbm, rows_ref, load_sem.at[0])
    load_bits = pltpu.make_async_copy(bits_hbm, bits_ref, load_sem.at[1])
    load_cot = pltpu.make_async_copy(
        cot_hbm.at[rows16(m * BLOCK, BLOCK)], cot_whole.at[m], load_sem.at[2]
    )
    load_rows.start()
    load_bits.start()

    barrier = pltpu.get_barrier_semaphore()

    def greet(to_shard, to_core):
        pl.semaphore_signal(
            barrier, inc=1, device_id=(to_shard, to_core), device_id_type=MESH
        )

    def greet_ring(z_to):
        for core in range(2):
            greet(z_to * PLANE + q, core)

    around(RING, z, greet_ring)
    around(2 * PLANE, me, lambda k: greet(z * PLANE + lax.div(k, 2), lax.rem(k, 2)))
    load_cot.start()
    for n in range(6):
        own_weight(n).start()

    sub = lax.broadcasted_iota(jnp.int32, (8, 128), 0)
    lane = lax.broadcasted_iota(jnp.int32, (8, 128), 1)

    def prepare(mode):
        mode.rows[0, mode.own_member] = rows_ref[...].astype(BF)
        columns = mode.columns
        per_slot = 128 // columns
        slots = TILE_DEV // per_slot
        if mode.core == 0:
            tiles = [bits_ref[t] for t in range(TILE_DEV)]
        else:
            left = lax.broadcasted_iota(jnp.int32, (128, 128), 0)
            right = lax.broadcasted_iota(jnp.int32, (128, 128), 1)
            order = jnp.where(
                (left % PLANE == right // columns) & (left // PLANE == right % columns), 1.0, 0.0
            ).astype(BF)
            words = bits_ref[...].reshape(128, 128)
            low = dot((words & 255).astype(F32).astype(BF), order)
            high = dot(jnp.right_shift(words, 8).astype(F32).astype(BF), order)
            words = (low + 256.0 * high).astype(jnp.int32).reshape(TILE_DEV, 8, 128)
            tiles = [words[t] for t in range(TILE_DEV)]
        group = lane // columns
        about = jnp.zeros((8, 128), jnp.int32)
        start = mode.own_member * TILE_DEV
        dest_sub = 2 + lax.div(start, 128)
        dest_lane = lax.rem(start, 128)
        for t in range(TILE_DEV):
            slot, place = t // per_slot, t % per_slot
            about = jnp.where((sub == slot) & (group == place), item_ref[t], about)
            about = jnp.where((sub == dest_sub) & (lane == dest_lane + t), dest_ref[t], about)
        for member in range(mode.members):
            for slot in range(slots):
                values = jnp.zeros((8, 128), jnp.int32)
                for place in range(per_slot):
                    turned = tiles[slot * per_slot + place]
                    shift = (columns * (place - member)) % 128
                    if shift:
                        turned = pltpu.roll(turned, shift, 1)
                    values = jnp.where(group == place, turned, values)
                mode.words_out[member, slot] = values
            mode.words_out[member, slots] = about
        mode.words_in[mode.own_member] = mode.words_out[mode.own_member]

    load_rows.wait()
    load_bits.wait()
    per_mode(prepare)

    pl.semaphore_wait(barrier, 2 * PLANE - 1 + 2 * (RING - 1))

    def words_copy(mode, member):
        return remote(
            mode.words_out.at[member],
            mode.words_in.at[mode.own_member],
            mode.words_send.at[member],
            mode.words_recv.at[mode.own_member],
            mode.item_shard(member),
            mode.core,
        )

    def rows_copy(mode, member):
        return remote(
            mode.rows.at[0, mode.own_member],
            mode.rows.at[0, mode.own_member],
            mode.rows_send.at[member],
            mode.rows_recv.at[mode.own_member],
            mode.item_shard(member),
            mode.core,
        )

    def start_rows(mode):
        around(mode.members, mode.own_member, lambda member: words_copy(mode, member).start())
        around(mode.members, mode.own_member, lambda member: rows_copy(mode, member).start())

    per_mode(start_rows)

    def cot_copy():
        return remote(
            cot_hbm.at[rows16(other * BLOCK, BLOCK)],
            cot_whole.at[m],
            cot_send,
            cot_recv,
            shard,
            other,
        )

    for n in range(3):
        sibling_weight(n).start()
    cot_copy().start()
    for n in range(3, 6):
        sibling_weight(n).start()

    def add_tiles(mode, phase, member):
        sums = dot(mode.collect[member], mode.rows[phase, member])
        high = sums.astype(BF)
        low = (sums - high.astype(F32)).astype(BF)
        shape = (mode.columns, TILE_DEV, HALF)
        tiles = TILE_DEV * mode.members
        mode.tile_sums[:, rows16(member * TILE_DEV, TILE_DEV), :] = high.reshape(shape)
        mode.tile_sums[:, rows16(tiles + member * TILE_DEV, TILE_DEV), :] = low.reshape(shape)

    def take_rows(mode):
        size = TILE_DEV * mode.columns
        slots = size // 128
        left = lax.broadcasted_iota(jnp.int32, (size, size), 0)
        right = lax.broadcasted_iota(jnp.int32, (size, size), 1)

        def turn(tile_major, column_major):
            same = (tile_major // mode.columns == column_major % TILE_DEV) & (
                tile_major % mode.columns == column_major // TILE_DEV
            )
            return jnp.where(same, 1.0, 0.0).astype(BF)

        to_columns = turn(left, right)
        from_tiles = turn(right, left)
        shifts = lax.broadcasted_iota(jnp.int32, (8, 16, 128), 1)

        def unpack(member):
            about = mode.words_in[member, slots]
            halves = []
            for slot in range(slots):
                packed = jnp.broadcast_to(mode.words_in[member, slot][:, None, :], (8, 16, 128))
                bits = (jnp.right_shift(packed, shifts) & 1).reshape(128, 128).astype(F32)
                halves.append((bits, jnp.broadcast_to(about[slot : slot + 1, :], (128, 128))))
            blocks = []
            for block in range(2):
                parts = [jnp.where(item == block, bits, 0.0) for bits, item in halves]
                blocks.append(parts[0] if slots == 1 else jnp.concatenate(parts, axis=1))
            mat = jnp.concatenate(blocks, axis=0).astype(BF)
            mode.spread[member] = dot(mat, to_columns).astype(BF)
            mode.collect[member] = dot_nt(from_tiles, mat).astype(BF)

        def take_words(member):
            arrival(
                mode.words_in.at[member],
                mode.words_send.at[member],
                mode.words_recv.at[member],
            ).wait_recv()
            unpack(member)

        unpack(mode.own_member)
        back_around(mode.members, mode.own_member, take_words)

        tiles = TILE_DEV * mode.members
        about = mode.words_in[0, slots]
        for member in range(1, mode.members):
            about = about + mode.words_in[member, slots]
        all_dest = about[2:3, :]
        if tiles > 128:
            all_dest = jnp.concatenate([all_dest, about[3:4, :]], axis=1)
        block_of = lax.broadcasted_iota(jnp.int32, (BLOCK, tiles), 0)
        one_hot = jnp.where(block_of == all_dest, 1.0, 0.0).astype(BF)
        mode.select_cols[...] = jnp.concatenate([one_hot, one_hot], axis=1)
        eye_left = lax.broadcasted_iota(jnp.int32, (tiles, tiles), 0)
        eye_right = lax.broadcasted_iota(jnp.int32, (tiles, tiles), 1)
        eye = jnp.where(eye_left == eye_right, 1.0, 0.0).astype(BF)
        mode.select_rows[...] = lax.dot_general(
            eye, one_hot, (((1,), (1,)), ((), ())), preferred_element_type=F32
        ).astype(BF)

        add_tiles(mode, 0, mode.own_member)

        def take(member):
            arrival(
                mode.rows.at[0, member], mode.rows_send.at[member], mode.rows_recv.at[member]
            ).wait_recv()
            add_tiles(mode, 0, member)

        back_around(mode.members, mode.own_member, take)

    per_mode(take_rows)

    def owner_copy(mode, phase, column, to_core):
        return remote(
            mode.owner_out.at[phase, column, rows16(to_core * OWN, OWN)],
            mode.owner_in.at[phase, mode.own_column],
            mode.owner_send.at[phase, column, to_core],
            mode.owner_recv.at[phase, mode.own_column],
            mode.basket_shard(column),
            to_core,
        )

    def send_sums(mode, phase):
        def column_sum(column):
            mode.owner_out[phase, column] = dot(
                mode.select_cols[...], mode.tile_sums[column]
            ).astype(BF)

        def send(column):
            column_sum(column)
            for to_core in range(2):
                owner_copy(mode, phase, column, to_core).start()

        around(mode.columns, mode.own_column, send)
        column_sum(mode.own_column)
        owner_copy(mode, phase, mode.own_column, 1 - mode.core).start()
        mode.owner_in[phase, mode.own_column] = mode.owner_out[
            phase, mode.own_column, mode.core * OWN : (mode.core + 1) * OWN, :
        ]

    def sum_at_owners(phase):
        per_mode(lambda mode: send_sums(mode, phase))
        for mode in modes:

            def take(column, mode=mode):
                arrival(
                    mode.owner_in.at[phase, column],
                    mode.owner_send.at[phase, column, 0],
                    mode.owner_recv.at[phase, column],
                ).wait_recv()

            back_around(mode.columns, mode.own_column, take)

            @pl.when(m != mode.core)
            def _(mode=mode, take=take):
                take(mode.own_column)

        halves = []
        for mode in modes:
            total = mode.owner_in[phase, 0].astype(F32)
            for column in range(1, mode.columns):
                total = total + mode.owner_in[phase, column].astype(F32)
            halves.append(total)
        return jnp.concatenate(halves, axis=1)

    def block_copy(mode, phase, column):
        return remote(
            mode.block_out.at[phase],
            mode.block_in.at[phase, mode.own_column, rows16(m * OWN, OWN)],
            mode.block_send.at[phase, column],
            mode.block_recv.at[phase, mode.own_column, m],
            mode.basket_shard(column),
            mode.core,
        )

    def send_blocks(phase, values):
        for mode in modes:
            mode.block_out[phase] = values[:, mode.core * HALF : (mode.core + 1) * HALF]
        for mode in modes:

            @pl.when(m != mode.core)
            def _(mode=mode):
                block_copy(mode, phase, mode.own_column).start()

            around(
                mode.columns,
                mode.own_column,
                lambda column, mode=mode: block_copy(mode, phase, column).start(),
            )

            @pl.when(m == mode.core)
            def _(mode=mode):
                place = slice(mode.core * OWN, (mode.core + 1) * OWN)
                mode.block_in[phase, mode.own_column, place, :] = mode.block_out[phase]

    def wait_block(mode, phase, column, from_core):
        arrival(
            mode.block_in.at[phase, column, rows16(from_core * OWN, OWN)],
            mode.block_send.at[phase, column],
            mode.block_recv.at[phase, column, from_core],
        ).wait_recv()

    def pick_all(mode, phase):
        def pick(column):
            chosen = dot(mode.select_rows[...], mode.block_in[phase, column]).astype(BF)
            mode.picked[:, rows16(column * TILE_DEV, TILE_DEV), :] = chosen.reshape(
                mode.members, TILE_DEV, HALF
            )

        def take(column):
            for from_core in range(2):
                wait_block(mode, phase, column, from_core)
            pick(column)

        wait_block(mode, phase, mode.own_column, 1 - mode.core)
        pick(mode.own_column)
        back_around(mode.columns, mode.own_column, take)

    basket_gain = gain_b_ref[...]
    item_gain = gain_i_ref[...]

    basket_sum = sum_at_owners(0)
    sum_keep[...] = basket_sum
    for n in range(3):
        own_weight(n).wait()
        sibling_weight(n).wait_recv()
    normed = basket_sum * rms_scale(basket_sum) * basket_gain
    normed_bf = normed.astype(BF)
    total = normed
    for h in range(2):
        gate_pre = dot(normed_bf, wide[0, h])
        up_pre = dot(normed_bf, wide[1, h])
        gate_keep[h] = gate_pre
        up_keep[h] = up_pre
        hidden = (gate_pre * jax.nn.sigmoid(gate_pre) * up_pre).astype(BF)
        total = total + dot(hidden, tall[0, h])
    send_blocks(0, total.astype(BF))

    def item_copy(mode, member, to_core):
        return remote(
            mode.item_out.at[0, member, rows16(to_core * BLOCK, BLOCK)],
            mode.item_in.at[mode.own_member],
            mode.item_send.at[member, to_core],
            mode.item_recv.at[mode.own_member],
            mode.item_shard(member),
            to_core,
        )

    def send_items(mode):
        pick_all(mode, 0)

        def partial(member):
            mode.item_out[0, member] = dot(mode.spread[member], mode.picked[member]).astype(BF)

        def send(member):
            partial(member)
            for to_core in range(2):
                item_copy(mode, member, to_core).start()

        around(mode.members, mode.own_member, send)
        partial(mode.own_member)
        item_copy(mode, mode.own_member, 1 - mode.core).start()
        mode.item_in[mode.own_member] = mode.item_out[
            0, mode.own_member, mode.core * BLOCK : (mode.core + 1) * BLOCK, :
        ]

    per_mode(send_items)

    for n in range(3, 6):
        own_weight(n).wait()
        sibling_weight(n).wait_recv()
    arrival(cot_whole.at[other], cot_send, cot_recv).wait_recv()
    load_cot.wait()
    for mode in modes:

        def take_item(member, mode=mode):
            arrival(
                mode.item_in.at[member], mode.item_send.at[member, 0], mode.item_recv.at[member]
            ).wait_recv()

        back_around(mode.members, mode.own_member, take_item)

        @pl.when(m != mode.core)
        def _(mode=mode, take_item=take_item):
            take_item(mode.own_member)

    halves = []
    for mode in modes:
        summed = mode.item_in[0].astype(F32)
        for member in range(1, mode.members):
            summed = summed + mode.item_in[member].astype(F32)
        halves.append(summed)
    message = jnp.concatenate(halves, axis=1)
    cot_full = jnp.concatenate([cot_whole[0], cot_whole[1]], axis=1)
    scale_item = rms_scale(message)
    query = (message * scale_item * item_gain).astype(BF)
    grad_query = jnp.zeros((BLOCK, D), F32)
    for h in range(2):
        gate_pre = dot(query, wide[2, h])
        up_pre = dot(query, wide[3, h])
        grad_hidden = dot_nt(cot_full, tall[1, h])
        value, slope = silu_parts(gate_pre)
        grad_up = (grad_hidden * value).astype(BF)
        grad_gate = (grad_hidden * up_pre * slope).astype(BF)
        grad_query = grad_query + dot_nt(grad_gate, wide[2, h]) + dot_nt(grad_up, wide[3, h])
    inner = jnp.sum(item_gain * grad_query * message, axis=1, keepdims=True)
    cubed = scale_item * scale_item * scale_item
    grad_message = (scale_item * item_gain * grad_query - message * cubed * inner / D).astype(BF)

    def grad_copy(mode, member):
        return remote(
            mode.grad_out,
            mode.rows.at[1, mode.own_member, rows16(m * BLOCK, BLOCK)],
            mode.grad_send.at[member],
            mode.grad_recv.at[mode.own_member, m],
            mode.item_shard(member),
            mode.core,
        )

    for mode in modes:
        mode.grad_out[...] = grad_message[:, mode.core * HALF : (mode.core + 1) * HALF]
    for mode in modes:

        @pl.when(m != mode.core)
        def _(mode=mode):
            grad_copy(mode, mode.own_member).start()

        around(
            mode.members,
            mode.own_member,
            lambda member, mode=mode: grad_copy(mode, member).start(),
        )

        @pl.when(m == mode.core)
        def _(mode=mode):
            place = slice(mode.core * BLOCK, (mode.core + 1) * BLOCK)
            mode.rows[1, mode.own_member, place, :] = mode.grad_out[...]

    def take_grads(mode):
        def wait_grad(member, from_core):
            arrival(
                mode.rows.at[1, member, rows16(from_core * BLOCK, BLOCK)],
                mode.grad_send.at[member],
                mode.grad_recv.at[member, from_core],
            ).wait_recv()

        def take(member):
            for from_core in range(2):
                wait_grad(member, from_core)
            add_tiles(mode, 1, member)

        wait_grad(mode.own_member, 1 - mode.core)
        add_tiles(mode, 1, mode.own_member)
        back_around(mode.members, mode.own_member, take)

    per_mode(take_grads)
    grad_out = sum_at_owners(1)
    grad_out_bf = grad_out.astype(BF)
    grad_normed = grad_out
    for h in range(2):
        grad_hidden = dot_nt(grad_out_bf, tall[0, h])
        value, slope = silu_parts(gate_keep[h])
        grad_up = (grad_hidden * value).astype(BF)
        grad_gate = (grad_hidden * up_keep[h] * slope).astype(BF)
        grad_normed = grad_normed + (dot_nt(grad_gate, wide[0, h]) + dot_nt(grad_up, wide[1, h]))
    sums = sum_keep[...]
    scale_basket = rms_scale(sums)
    inner_basket = jnp.sum(basket_gain * grad_normed * sums, axis=1, keepdims=True)
    cubed_basket = scale_basket * scale_basket * scale_basket
    grad_sum = scale_basket * basket_gain * grad_normed - sums * cubed_basket * inner_basket / D
    send_blocks(1, grad_sum.astype(BF))

    def back_copy(mode, member):
        return remote(
            mode.item_out.at[1, member],
            mode.back_in.at[mode.own_member],
            mode.back_send.at[member],
            mode.back_recv.at[mode.own_member],
            mode.item_shard(member),
            mode.core,
        )

    def finish(mode):
        pick_all(mode, 1)

        def send(member):
            mode.item_out[1, member] = dot(mode.spread[member], mode.picked[member]).astype(BF)
            back_copy(mode, member).start()

        around(mode.members, mode.own_member, send)
        mode.back_in[mode.own_member] = dot(
            mode.spread[mode.own_member], mode.picked[mode.own_member]
        ).astype(BF)

        def take(member):
            arrival(
                mode.back_in.at[member], mode.back_send.at[member], mode.back_recv.at[member]
            ).wait_recv()

        back_around(mode.members, mode.own_member, take)
        back = mode.back_in[0].astype(F32)
        for member in range(1, mode.members):
            back = back + mode.back_in[member].astype(F32)
        back_ref[...] = back

        def drain_member(member):
            words_copy(mode, member).wait_send()
            rows_copy(mode, member).wait_send()
            back_copy(mode, member).wait_send()
            for to_core in range(2):
                item_copy(mode, member, to_core).wait_send()

        around(mode.members, mode.own_member, drain_member)
        item_copy(mode, mode.own_member, 1 - mode.core).wait_send()

        def drain_column(column):
            for phase in range(2):
                for to_core in range(2):
                    owner_copy(mode, phase, column, to_core).wait_send()

        around(mode.columns, mode.own_column, drain_column)
        for phase in range(2):
            owner_copy(mode, phase, mode.own_column, 1 - mode.core).wait_send()

    per_mode(finish)

    for n in range(6):
        sibling_weight(n).wait_send()
    cot_copy().wait_send()
    for mode in modes:

        def drain_grad(member, mode=mode):
            grad_copy(mode, member).wait_send()

        def drain_block(column, mode=mode):
            for phase in range(2):
                block_copy(mode, phase, column).wait_send()

        around(mode.members, mode.own_member, drain_grad)
        around(mode.columns, mode.own_column, drain_block)

        @pl.when(m != mode.core)
        def _(mode=mode, drain_grad=drain_grad, drain_block=drain_block):
            drain_grad(mode.own_member)
            drain_block(mode.own_column)


def local(
    item_rows,
    first_moment,
    second_moment,
    item_cot,
    tile_bits,
    tile_item,
    tile_dest,
    basket_gain,
    item_gain,
    gate_basket,
    up_basket,
    down_basket,
    gate_item,
    up_item,
    down_item,
):
    vmem = pl.BlockSpec(memory_space=pltpu.VMEM)
    smem = pl.BlockSpec(memory_space=pltpu.SMEM)
    anywhere = pl.BlockSpec(memory_space=pltpu.HBM)
    back_items = pl.pallas_call(
        kernel,
        out_shape=jax.ShapeDtypeStruct((2 * BLOCK, HALF), F32),
        in_specs=[anywhere] * 3 + [smem, smem, vmem, vmem] + [anywhere] * 6,
        out_specs=vmem,
        scratch_shapes=[
            common_scratch(),
            mode_scratch(RING, PLANE),
            mode_scratch(PLANE, RING),
        ],
        compiler_params=pltpu.CompilerParams(
            collective_id=0, has_side_effects=True, vmem_limit_bytes=60 * 1024 * 1024
        ),
        name="layer",
    )(
        item_rows,
        item_cot,
        tile_bits,
        tile_item,
        tile_dest,
        basket_gain.reshape(1, D),
        item_gain.reshape(1, D),
        gate_basket,
        up_basket,
        down_basket,
        gate_item,
        up_item,
        down_item,
    )
    gradient = item_cot.astype(F32) + back_items
    new_first = BETA_FIRST * first_moment + (1.0 - BETA_FIRST) * gradient
    new_second = BETA_SECOND * second_moment + (1.0 - BETA_SECOND) * gradient * gradient
    new_rows = item_rows - LEARNING_RATE * new_first / (jnp.sqrt(new_second) + ADAM_EPSILON)
    return (new_rows, new_first, new_second)


def solution(mesh):
    split = P("shard", "mp")
    return jax.shard_map(
        local,
        mesh=mesh,
        in_specs=(
            split,
            split,
            split,
            split,
            P("shard", None, None),
            P("shard"),
            P("shard"),
            P(),
            P(),
            P(None, "mp"),
            P(None, "mp"),
            P("mp", None),
            P(None, "mp"),
            P(None, "mp"),
            P("mp", None),
        ),
        out_specs=(split, split, split),
        check_vma=False,
    )
```

```python
import jax
import jax.numpy as jnp
from jax import lax
from jax.experimental import pallas as pl
from jax.experimental.pallas import tpu as pltpu
from jax.sharding import PartitionSpec as P

D = 256
HALF = 128
BLOCK = 128
TILE_DEV = 16
RING = 8
PLANE = 16
PARTS = RING + PLANE
OWN = 64
HIDDEN = 1024

NORM_EPSILON = 1e-05
LEARNING_RATE = 0.01
BETA_FIRST = 0.9
BETA_SECOND = 0.99
ADAM_EPSILON = 1e-08

MESH = pl.DeviceIdType.MESH
BF = jnp.bfloat16
F32 = jnp.float32


def dot(a, b):
    return jnp.dot(a, b, preferred_element_type=F32)


def dot_nt(a, b):
    return lax.dot_general(a, b, (((1,), (1,)), ((), ())), preferred_element_type=F32)


def silu_parts(gate_values):
    sigmoid = jax.nn.sigmoid(gate_values)
    return (gate_values * sigmoid, sigmoid * (1.0 + gate_values * (1.0 - sigmoid)))


def rms_scale(values):
    return lax.rsqrt(jnp.mean(values * values, axis=-1, keepdims=True) + NORM_EPSILON)


def rows16(start, size):
    return pl.ds(pl.multiple_of(start, 16), size)


def mode_scratch(members, columns):
    wide = TILE_DEV * columns
    tiles = TILE_DEV * members
    slots = wide // 128 + 1
    return {
        "words_out": pltpu.VMEM((members, slots, 8, 128), jnp.int32),
        "words_in": pltpu.VMEM((members, slots, 8, 128), jnp.int32),
        "rows": pltpu.VMEM((2, members, 2 * BLOCK, HALF), BF),
        "spread": pltpu.VMEM((members, 2 * BLOCK, wide), BF),
        "collect": pltpu.VMEM((members, wide, 2 * BLOCK), BF),
        "select_cols": pltpu.VMEM((BLOCK, 2 * tiles), BF),
        "select_rows": pltpu.VMEM((tiles, BLOCK), BF),
        "tile_sums": pltpu.VMEM((columns, 2 * tiles, HALF), BF),
        "owner_out": pltpu.VMEM((2, 2 * columns, OWN, HALF), BF),
        "block_out": pltpu.VMEM((2, OWN, HALF), BF),
        "block_in": pltpu.VMEM((2, columns, BLOCK, HALF), BF),
        "picked": pltpu.VMEM((members, wide, HALF), BF),
        "item_out": pltpu.VMEM((2, 2 * members, BLOCK, HALF), BF),
        "back_in": pltpu.VMEM((members, 2, BLOCK, HALF), BF),
        "grad_out": pltpu.VMEM((BLOCK, HALF), BF),
    }


def common_scratch():
    dma = pltpu.SemaphoreType.DMA
    return {
        "wide": pltpu.VMEM((4, 2, D, HIDDEN), BF),
        "tall": pltpu.VMEM((2, 2, HIDDEN, D), BF),
        "cot_whole": pltpu.VMEM((2, BLOCK, HALF), BF),
        "gate_keep": pltpu.VMEM((2, OWN, HIDDEN), F32),
        "up_keep": pltpu.VMEM((2, OWN, HIDDEN), F32),
        "sum_keep": pltpu.VMEM((OWN, D), F32),
        "item_rows": pltpu.VMEM((2 * BLOCK, HALF), F32),
        "tile_bits": pltpu.VMEM((TILE_DEV, 8, 128), jnp.int32),
        "load_sem": dma((3,)),
        "weight_own": dma((6,)),
        "weight_send": dma((6,)),
        "weight_recv": dma((6,)),
        "cot_send": dma,
        "cot_recv": dma,
        "owner_in": pltpu.VMEM((2, PARTS, OWN, HALF), BF),
        "item_in": pltpu.VMEM((PARTS, BLOCK, HALF), BF),
        "words_send": dma,
        "words_recv": dma,
        "rows_send": dma,
        "rows_recv": dma((PLANE,)),
        "owner_send": dma((2,)),
        "owner_recv": dma((2,)),
        "block_send": dma((2,)),
        "block_recv": dma((2, PLANE)),
        "item_send": dma,
        "item_recv": dma,
        "grad_send": dma,
        "grad_recv": dma((PLANE,)),
        "back_send": dma,
        "back_recv": dma,
    }


class Mode:
    def __init__(self, core, refs, z, q):
        self.core = core
        self.members, self.columns = (RING, PLANE) if core == 0 else (PLANE, RING)
        self.own_member, self.own_column = (z, q) if core == 0 else (q, z)
        self.first = 0 if core == 0 else PLANE
        self.first_item = 0 if core == 0 else RING
        self.z, self.q = z, q
        self.__dict__.update(refs)

    def item_shard(self, member):
        return member * PLANE + self.q if self.core == 0 else self.z * PLANE + member

    def basket_shard(self, column):
        return self.z * PLANE + column if self.core == 0 else column * PLANE + self.q


def kernel(
    rows_hbm,
    cot_hbm,
    bits_hbm,
    item_ref,
    dest_ref,
    gain_b_ref,
    gain_i_ref,
    gate_b_ref,
    up_b_ref,
    down_b_ref,
    gate_i_ref,
    up_i_ref,
    down_i_ref,
    back_ref,
    common,
    ring_refs,
    plane_refs,
):
    shard = lax.axis_index("shard")
    m = lax.axis_index("mp")
    other = 1 - m
    z = lax.div(shard, PLANE)
    q = lax.rem(shard, PLANE)
    me = 2 * q + m
    modes = (Mode(0, ring_refs, z, q), Mode(1, plane_refs, z, q))
    wide, tall, cot_whole = common["wide"], common["tall"], common["cot_whole"]
    gate_keep, up_keep, sum_keep = common["gate_keep"], common["up_keep"], common["sum_keep"]
    rows_ref, bits_ref, load_sem = common["item_rows"], common["tile_bits"], common["load_sem"]
    weight_own, weight_send = common["weight_own"], common["weight_send"]
    weight_recv = common["weight_recv"]
    cot_send, cot_recv = common["cot_send"], common["cot_recv"]
    owner_in, item_in = common["owner_in"], common["item_in"]
    words_send, words_recv = common["words_send"], common["words_recv"]
    rows_send, rows_recv = common["rows_send"], common["rows_recv"]
    owner_send, owner_recv = common["owner_send"], common["owner_recv"]
    block_send, block_recv = common["block_send"], common["block_recv"]
    item_send, item_recv = common["item_send"], common["item_recv"]
    grad_send, grad_recv = common["grad_send"], common["grad_recv"]
    back_send, back_recv = common["back_send"], common["back_recv"]

    def remote(src, dst, send, recv, to_shard, to_core):
        return pltpu.make_async_remote_copy(
            src_ref=src,
            dst_ref=dst,
            send_sem=send,
            recv_sem=recv,
            device_id=(to_shard, to_core),
            device_id_type=MESH,
        )

    def arrived(ref, recv):
        remote(ref, ref, cot_send, recv, shard, other).wait_recv()

    def sent(ref, send):
        remote(ref, ref, send, cot_recv, shard, other).wait_send()

    def around(count, own, body):
        def step(n, carry):
            body(lax.rem(own + n, count))
            return carry

        lax.fori_loop(1, count, step, 0)

    def back_around(count, own, body):
        def step(n, carry):
            body(lax.rem(own + count - n, count))
            return carry

        lax.fori_loop(1, count, step, 0)

    def per_mode(body):
        for mode in modes:

            @pl.when(m == mode.core)
            def _(mode=mode):
                body(mode)

    weights = (
        (gate_b_ref, wide.at[0]),
        (up_b_ref, wide.at[1]),
        (down_b_ref, tall.at[0]),
        (gate_i_ref, wide.at[2]),
        (up_i_ref, wide.at[3]),
        (down_i_ref, tall.at[1]),
    )

    def own_weight(n):
        src, dst = weights[n]
        return pltpu.make_async_copy(src, dst.at[m], weight_own.at[n])

    def sibling_weight(n):
        src, dst = weights[n]
        return remote(src, dst.at[m], weight_send.at[n], weight_recv.at[n], shard, other)

    load_rows = pltpu.make_async_copy(rows_hbm, rows_ref, load_sem.at[0])
    load_bits = pltpu.make_async_copy(bits_hbm, bits_ref, load_sem.at[1])
    load_cot = pltpu.make_async_copy(
        cot_hbm.at[rows16(m * BLOCK, BLOCK)], cot_whole.at[m], load_sem.at[2]
    )
    load_rows.start()
    load_bits.start()

    barrier = pltpu.get_barrier_semaphore()

    def greet(to_shard, to_core):
        pl.semaphore_signal(
            barrier, inc=1, device_id=(to_shard, to_core), device_id_type=MESH
        )

    def greet_ring(z_to):
        for core in range(2):
            greet(z_to * PLANE + q, core)

    around(RING, z, greet_ring)
    around(2 * PLANE, me, lambda k: greet(z * PLANE + lax.div(k, 2), lax.rem(k, 2)))
    load_cot.start()
    for n in range(6):
        own_weight(n).start()

    sub = lax.broadcasted_iota(jnp.int32, (8, 128), 0)
    lane = lax.broadcasted_iota(jnp.int32, (8, 128), 1)

    def prepare(mode):
        mode.rows[0, mode.own_member] = rows_ref[...].astype(BF)
        columns = mode.columns
        per_slot = 128 // columns
        slots = TILE_DEV // per_slot
        if mode.core == 0:
            tiles = [bits_ref[t] for t in range(TILE_DEV)]
        else:
            left = lax.broadcasted_iota(jnp.int32, (128, 128), 0)
            right = lax.broadcasted_iota(jnp.int32, (128, 128), 1)
            order = jnp.where(
                (left % PLANE == right // columns) & (left // PLANE == right % columns), 1.0, 0.0
            ).astype(BF)
            words = bits_ref[...].reshape(128, 128)
            low = dot((words & 255).astype(F32).astype(BF), order)
            high = dot(jnp.right_shift(words, 8).astype(F32).astype(BF), order)
            words = (low + 256.0 * high).astype(jnp.int32).reshape(TILE_DEV, 8, 128)
            tiles = [words[t] for t in range(TILE_DEV)]
        group = lane // columns
        about = jnp.zeros((8, 128), jnp.int32)
        start = mode.own_member * TILE_DEV
        dest_sub = 2 + lax.div(start, 128)
        dest_lane = lax.rem(start, 128)
        for t in range(TILE_DEV):
            slot, place = t // per_slot, t % per_slot
            about = jnp.where((sub == slot) & (group == place), item_ref[t], about)
            about = jnp.where((sub == dest_sub) & (lane == dest_lane + t), dest_ref[t], about)
        for member in range(mode.members):
            for slot in range(slots):
                values = jnp.zeros((8, 128), jnp.int32)
                for place in range(per_slot):
                    turned = tiles[slot * per_slot + place]
                    shift = (columns * (place - member)) % 128
                    if shift:
                        turned = pltpu.roll(turned, shift, 1)
                    values = jnp.where(group == place, turned, values)
                mode.words_out[member, slot] = values
            mode.words_out[member, slots] = about
        mode.words_in[mode.own_member] = mode.words_out[mode.own_member]

    load_rows.wait()
    load_bits.wait()
    per_mode(prepare)

    pl.semaphore_wait(barrier, 2 * PLANE - 1 + 2 * (RING - 1))

    def words_copy(mode, member):
        return remote(
            mode.words_out.at[member],
            mode.words_in.at[mode.own_member],
            words_send,
            words_recv,
            mode.item_shard(member),
            mode.core,
        )

    def rows_copy(mode, member):
        return remote(
            mode.rows.at[0, mode.own_member],
            mode.rows.at[0, mode.own_member],
            rows_send,
            rows_recv.at[mode.own_member],
            mode.item_shard(member),
            mode.core,
        )

    def start_rows(mode):
        around(mode.members, mode.own_member, lambda member: words_copy(mode, member).start())
        around(mode.members, mode.own_member, lambda member: rows_copy(mode, member).start())

    per_mode(start_rows)

    def cot_copy():
        return remote(
            cot_hbm.at[rows16(other * BLOCK, BLOCK)],
            cot_whole.at[m],
            cot_send,
            cot_recv,
            shard,
            other,
        )

    for n in range(3):
        sibling_weight(n).start()
    cot_copy().start()
    for n in range(3, 6):
        sibling_weight(n).start()

    def add_tiles(mode, phase, member):
        sums = dot(mode.collect[member], mode.rows[phase, member])
        high = sums.astype(BF)
        low = (sums - high.astype(F32)).astype(BF)
        shape = (mode.columns, TILE_DEV, HALF)
        tiles = TILE_DEV * mode.members
        mode.tile_sums[:, rows16(member * TILE_DEV, TILE_DEV), :] = high.reshape(shape)
        mode.tile_sums[:, rows16(tiles + member * TILE_DEV, TILE_DEV), :] = low.reshape(shape)

    def take_rows(mode):
        size = TILE_DEV * mode.columns
        slots = size // 128
        left = lax.broadcasted_iota(jnp.int32, (size, size), 0)
        right = lax.broadcasted_iota(jnp.int32, (size, size), 1)

        def turn(tile_major, column_major):
            same = (tile_major // mode.columns == column_major % TILE_DEV) & (
                tile_major % mode.columns == column_major // TILE_DEV
            )
            return jnp.where(same, 1.0, 0.0).astype(BF)

        to_columns = turn(left, right)
        from_tiles = turn(right, left)
        shifts = lax.broadcasted_iota(jnp.int32, (8, 16, 128), 1)

        def unpack(member):
            about = mode.words_in[member, slots]
            halves = []
            for slot in range(slots):
                packed = jnp.broadcast_to(mode.words_in[member, slot][:, None, :], (8, 16, 128))
                bits = (jnp.right_shift(packed, shifts) & 1).reshape(128, 128).astype(F32)
                halves.append((bits, jnp.broadcast_to(about[slot : slot + 1, :], (128, 128))))
            blocks = []
            for block in range(2):
                parts = [jnp.where(item == block, bits, 0.0) for bits, item in halves]
                blocks.append(parts[0] if slots == 1 else jnp.concatenate(parts, axis=1))
            mat = jnp.concatenate(blocks, axis=0).astype(BF)
            mode.spread[member] = dot(mat, to_columns).astype(BF)
            mode.collect[member] = dot_nt(from_tiles, mat).astype(BF)

        unpack(mode.own_member)
        arrived(mode.words_in.at[: mode.members - 1], words_recv)
        back_around(mode.members, mode.own_member, unpack)

        tiles = TILE_DEV * mode.members
        about = mode.words_in[0, slots]
        for member in range(1, mode.members):
            about = about + mode.words_in[member, slots]
        all_dest = about[2:3, :]
        if tiles > 128:
            all_dest = jnp.concatenate([all_dest, about[3:4, :]], axis=1)
        block_of = lax.broadcasted_iota(jnp.int32, (BLOCK, tiles), 0)
        one_hot = jnp.where(block_of == all_dest, 1.0, 0.0).astype(BF)
        mode.select_cols[...] = jnp.concatenate([one_hot, one_hot], axis=1)
        eye_left = lax.broadcasted_iota(jnp.int32, (tiles, tiles), 0)
        eye_right = lax.broadcasted_iota(jnp.int32, (tiles, tiles), 1)
        eye = jnp.where(eye_left == eye_right, 1.0, 0.0).astype(BF)
        mode.select_rows[...] = lax.dot_general(
            eye, one_hot, (((1,), (1,)), ((), ())), preferred_element_type=F32
        ).astype(BF)

        add_tiles(mode, 0, mode.own_member)

        def take(member):
            arrived(mode.rows.at[0, member], rows_recv.at[member])
            add_tiles(mode, 0, member)

        back_around(mode.members, mode.own_member, take)

    per_mode(take_rows)

    def owner_copy(mode, phase, column, to_core):
        return remote(
            mode.owner_out.at[phase, 2 * column + to_core],
            owner_in.at[phase, mode.first + mode.own_column],
            owner_send.at[phase],
            owner_recv.at[phase],
            mode.basket_shard(column),
            to_core,
        )

    def send_sums(mode, phase):
        def column_sum(column):
            total = dot(mode.select_cols[...], mode.tile_sums[column]).astype(BF)
            mode.owner_out[phase, pl.ds(2 * column, 2)] = total.reshape(2, OWN, HALF)

        def send(column):
            column_sum(column)
            for to_core in range(2):
                owner_copy(mode, phase, column, to_core).start()

        around(mode.columns, mode.own_column, send)
        column_sum(mode.own_column)
        owner_copy(mode, phase, mode.own_column, 1 - mode.core).start()
        owner_in[phase, mode.first + mode.own_column] = mode.owner_out[
            phase, 2 * mode.own_column + mode.core
        ]

    def sum_at_owners(phase):
        per_mode(lambda mode: send_sums(mode, phase))
        arrived(owner_in.at[phase, : PARTS - 1], owner_recv.at[phase])
        halves = []
        for mode in modes:
            total = owner_in[phase, mode.first].astype(F32)
            for column in range(1, mode.columns):
                total = total + owner_in[phase, mode.first + column].astype(F32)
            halves.append(total)
        return jnp.concatenate(halves, axis=1)

    def block_copy(mode, phase, column):
        return remote(
            mode.block_out.at[phase],
            mode.block_in.at[phase, mode.own_column, rows16(m * OWN, OWN)],
            block_send.at[phase],
            block_recv.at[phase, mode.own_column],
            mode.basket_shard(column),
            mode.core,
        )

    def send_blocks(phase, values):
        for mode in modes:
            mode.block_out[phase] = values[:, mode.core * HALF : (mode.core + 1) * HALF]
        for mode in modes:

            @pl.when(m != mode.core)
            def _(mode=mode):
                block_copy(mode, phase, mode.own_column).start()

            around(
                mode.columns,
                mode.own_column,
                lambda column, mode=mode: block_copy(mode, phase, column).start(),
            )

            @pl.when(m == mode.core)
            def _(mode=mode):
                place = slice(mode.core * OWN, (mode.core + 1) * OWN)
                mode.block_in[phase, mode.own_column, place, :] = mode.block_out[phase]

    def pick_all(mode, phase):
        def pick(column):
            chosen = dot(mode.select_rows[...], mode.block_in[phase, column]).astype(BF)
            mode.picked[:, rows16(column * TILE_DEV, TILE_DEV), :] = chosen.reshape(
                mode.members, TILE_DEV, HALF
            )

        def take(column):
            arrived(mode.block_in.at[phase, column], block_recv.at[phase, column])
            pick(column)

        arrived(
            mode.block_in.at[phase, mode.own_column, :OWN], block_recv.at[phase, mode.own_column]
        )
        pick(mode.own_column)
        back_around(mode.columns, mode.own_column, take)

    basket_gain = gain_b_ref[...]
    item_gain = gain_i_ref[...]

    basket_sum = sum_at_owners(0)
    sum_keep[...] = basket_sum
    for n in range(3):
        own_weight(n).wait()
        sibling_weight(n).wait_recv()
    normed = basket_sum * rms_scale(basket_sum) * basket_gain
    normed_bf = normed.astype(BF)
    total = normed
    for h in range(2):
        gate_pre = dot(normed_bf, wide[0, h])
        up_pre = dot(normed_bf, wide[1, h])
        gate_keep[h] = gate_pre
        up_keep[h] = up_pre
        hidden = (gate_pre * jax.nn.sigmoid(gate_pre) * up_pre).astype(BF)
        total = total + dot(hidden, tall[0, h])
    send_blocks(0, total.astype(BF))

    def item_copy(mode, member, to_core):
        return remote(
            mode.item_out.at[0, 2 * member + to_core],
            item_in.at[mode.first_item + mode.own_member],
            item_send,
            item_recv,
            mode.item_shard(member),
            to_core,
        )

    def send_items(mode):
        pick_all(mode, 0)

        def partial(member):
            total = dot(mode.spread[member], mode.picked[member]).astype(BF)
            mode.item_out[0, pl.ds(2 * member, 2)] = total.reshape(2, BLOCK, HALF)

        def send(member):
            partial(member)
            for to_core in range(2):
                item_copy(mode, member, to_core).start()

        around(mode.members, mode.own_member, send)
        partial(mode.own_member)
        item_copy(mode, mode.own_member, 1 - mode.core).start()
        item_in[mode.first_item + mode.own_member] = mode.item_out[
            0, 2 * mode.own_member + mode.core
        ]

    per_mode(send_items)

    for n in range(3, 6):
        own_weight(n).wait()
        sibling_weight(n).wait_recv()
    arrived(cot_whole.at[other], cot_recv)
    load_cot.wait()
    arrived(item_in.at[: PARTS - 1], item_recv)
    halves = []
    for mode in modes:
        summed = item_in[mode.first_item].astype(F32)
        for member in range(1, mode.members):
            summed = summed + item_in[mode.first_item + member].astype(F32)
        halves.append(summed)
    message = jnp.concatenate(halves, axis=1)
    cot_full = jnp.concatenate([cot_whole[0], cot_whole[1]], axis=1)
    scale_item = rms_scale(message)
    query = (message * scale_item * item_gain).astype(BF)
    grad_query = jnp.zeros((BLOCK, D), F32)
    for h in range(2):
        gate_pre = dot(query, wide[2, h])
        up_pre = dot(query, wide[3, h])
        grad_hidden = dot_nt(cot_full, tall[1, h])
        value, slope = silu_parts(gate_pre)
        grad_up = (grad_hidden * value).astype(BF)
        grad_gate = (grad_hidden * up_pre * slope).astype(BF)
        grad_query = grad_query + dot_nt(grad_gate, wide[2, h]) + dot_nt(grad_up, wide[3, h])
    inner = jnp.sum(item_gain * grad_query * message, axis=1, keepdims=True)
    cubed = scale_item * scale_item * scale_item
    grad_message = (scale_item * item_gain * grad_query - message * cubed * inner / D).astype(BF)

    def grad_copy(mode, member):
        return remote(
            mode.grad_out,
            mode.rows.at[1, mode.own_member, rows16(m * BLOCK, BLOCK)],
            grad_send,
            grad_recv.at[mode.own_member],
            mode.item_shard(member),
            mode.core,
        )

    for mode in modes:
        mode.grad_out[...] = grad_message[:, mode.core * HALF : (mode.core + 1) * HALF]
    for mode in modes:

        @pl.when(m != mode.core)
        def _(mode=mode):
            grad_copy(mode, mode.own_member).start()

        around(
            mode.members,
            mode.own_member,
            lambda member, mode=mode: grad_copy(mode, member).start(),
        )

        @pl.when(m == mode.core)
        def _(mode=mode):
            place = slice(mode.core * BLOCK, (mode.core + 1) * BLOCK)
            mode.rows[1, mode.own_member, place, :] = mode.grad_out[...]

    def take_grads(mode):
        def take(member):
            arrived(mode.rows.at[1, member], grad_recv.at[member])
            add_tiles(mode, 1, member)

        arrived(mode.rows.at[1, mode.own_member, :BLOCK], grad_recv.at[mode.own_member])
        add_tiles(mode, 1, mode.own_member)
        back_around(mode.members, mode.own_member, take)

    per_mode(take_grads)
    grad_out = sum_at_owners(1)
    grad_out_bf = grad_out.astype(BF)
    grad_normed = grad_out
    for h in range(2):
        grad_hidden = dot_nt(grad_out_bf, tall[0, h])
        value, slope = silu_parts(gate_keep[h])
        grad_up = (grad_hidden * value).astype(BF)
        grad_gate = (grad_hidden * up_keep[h] * slope).astype(BF)
        grad_normed = grad_normed + (dot_nt(grad_gate, wide[0, h]) + dot_nt(grad_up, wide[1, h]))
    sums = sum_keep[...]
    scale_basket = rms_scale(sums)
    inner_basket = jnp.sum(basket_gain * grad_normed * sums, axis=1, keepdims=True)
    cubed_basket = scale_basket * scale_basket * scale_basket
    grad_sum = scale_basket * basket_gain * grad_normed - sums * cubed_basket * inner_basket / D
    send_blocks(1, grad_sum.astype(BF))

    def back_copy(mode, member):
        return remote(
            mode.item_out.at[1, pl.ds(2 * member, 2)],
            mode.back_in.at[mode.own_member],
            back_send,
            back_recv,
            mode.item_shard(member),
            mode.core,
        )

    def finish(mode):
        pick_all(mode, 1)

        def partial(member):
            total = dot(mode.spread[member], mode.picked[member]).astype(BF)
            return total.reshape(2, BLOCK, HALF)

        def send(member):
            mode.item_out[1, pl.ds(2 * member, 2)] = partial(member)
            back_copy(mode, member).start()

        around(mode.members, mode.own_member, send)
        mode.back_in[mode.own_member] = partial(mode.own_member)
        sent(mode.words_out.at[: mode.members - 1], words_send)
        sent(mode.rows.at[0, : mode.members - 1], rows_send)
        sent(mode.item_out.at[0, : 2 * mode.members - 1], item_send)
        for phase in range(2):
            sent(mode.owner_out.at[phase, : 2 * mode.columns - 1], owner_send.at[phase])
            sent(owner_in.at[phase, : PARTS - 1], block_send.at[phase])
        sent(item_in.at[: PARTS - 1], grad_send)
        arrived(mode.back_in.at[: mode.members - 1], back_recv)
        for block in range(2):
            back = mode.back_in[0, block].astype(F32)
            for member in range(1, mode.members):
                back = back + mode.back_in[member, block].astype(F32)
            back_ref[block * BLOCK : (block + 1) * BLOCK, :] = back
        sent(mode.back_in.at[: mode.members - 1], back_send)

    per_mode(finish)

    for n in range(6):
        sibling_weight(n).wait_send()
    cot_copy().wait_send()


def local(
    item_rows,
    first_moment,
    second_moment,
    item_cot,
    tile_bits,
    tile_item,
    tile_dest,
    basket_gain,
    item_gain,
    gate_basket,
    up_basket,
    down_basket,
    gate_item,
    up_item,
    down_item,
):
    vmem = pl.BlockSpec(memory_space=pltpu.VMEM)
    smem = pl.BlockSpec(memory_space=pltpu.SMEM)
    anywhere = pl.BlockSpec(memory_space=pltpu.HBM)
    back_items = pl.pallas_call(
        kernel,
        out_shape=jax.ShapeDtypeStruct((2 * BLOCK, HALF), F32),
        in_specs=[anywhere] * 3 + [smem, smem, vmem, vmem] + [anywhere] * 6,
        out_specs=vmem,
        scratch_shapes=[
            common_scratch(),
            mode_scratch(RING, PLANE),
            mode_scratch(PLANE, RING),
        ],
        compiler_params=pltpu.CompilerParams(
            collective_id=0, has_side_effects=True, vmem_limit_bytes=60 * 1024 * 1024
        ),
        name="layer",
    )(
        item_rows,
        item_cot,
        tile_bits,
        tile_item,
        tile_dest,
        basket_gain.reshape(1, D),
        item_gain.reshape(1, D),
        gate_basket,
        up_basket,
        down_basket,
        gate_item,
        up_item,
        down_item,
    )
    gradient = item_cot.astype(F32) + back_items
    new_first = BETA_FIRST * first_moment + (1.0 - BETA_FIRST) * gradient
    new_second = BETA_SECOND * second_moment + (1.0 - BETA_SECOND) * gradient * gradient
    new_rows = item_rows - LEARNING_RATE * new_first / (jnp.sqrt(new_second) + ADAM_EPSILON)
    return (new_rows, new_first, new_second)


def solution(mesh):
    split = P("shard", "mp")
    return jax.shard_map(
        local,
        mesh=mesh,
        in_specs=(
            split,
            split,
            split,
            split,
            P("shard", None, None),
            P("shard"),
            P("shard"),
            P(),
            P(),
            P(None, "mp"),
            P(None, "mp"),
            P("mp", None),
            P(None, "mp"),
            P(None, "mp"),
            P("mp", None),
        ),
        out_specs=(split, split, split),
        check_vma=False,
    )
```

```python
import jax
import jax.numpy as jnp
from jax import lax
from jax.experimental import pallas as pl
from jax.experimental.pallas import tpu as pltpu
from jax.sharding import PartitionSpec as P

D = 256
HALF = 128
BLOCK = 128
TILE_DEV = 16
RING = 8
PLANE = 16
PARTS = RING + PLANE
OWN = 64
HIDDEN = 1024

NORM_EPSILON = 1e-05
LEARNING_RATE = 0.01
BETA_FIRST = 0.9
BETA_SECOND = 0.99
ADAM_EPSILON = 1e-08

MESH = pl.DeviceIdType.MESH
BF = jnp.bfloat16
F32 = jnp.float32


def dot(a, b):
    return jnp.dot(a, b, preferred_element_type=F32)


def dot_nt(a, b):
    return lax.dot_general(a, b, (((1,), (1,)), ((), ())), preferred_element_type=F32)


def silu_parts(gate_values):
    sigmoid = jax.nn.sigmoid(gate_values)
    return (gate_values * sigmoid, sigmoid * (1.0 + gate_values * (1.0 - sigmoid)))


def rms_scale(values):
    return lax.rsqrt(jnp.mean(values * values, axis=-1, keepdims=True) + NORM_EPSILON)


def rows16(start, size):
    return pl.ds(pl.multiple_of(start, 16), size)


def mode_scratch(members, columns):
    wide = TILE_DEV * columns
    tiles = TILE_DEV * members
    slots = wide // 128 + 1
    return {
        "words_out": pltpu.VMEM((members, slots, 8, 128), jnp.int32),
        "words_in": pltpu.VMEM((members, slots, 8, 128), jnp.int32),
        "rows": pltpu.VMEM((2, members, 2 * BLOCK, HALF), BF),
        "spread": pltpu.VMEM((members, 2 * BLOCK, wide), BF),
        "collect": pltpu.VMEM((members, wide, 2 * BLOCK), BF),
        "select_cols": pltpu.VMEM((BLOCK, 2 * tiles), BF),
        "select_rows": pltpu.VMEM((tiles, BLOCK), BF),
        "tile_sums": pltpu.VMEM((columns, 2 * tiles, HALF), BF),
        "owner_out": pltpu.VMEM((2, 2 * columns, OWN, HALF), BF),
        "block_out": pltpu.VMEM((2, OWN, HALF), BF),
        "block_in": pltpu.VMEM((2, columns, BLOCK, HALF), BF),
        "picked": pltpu.VMEM((members, wide, HALF), BF),
        "item_out": pltpu.VMEM((2, 2 * members, BLOCK, HALF), BF),
        "back_in": pltpu.VMEM((members, 2, BLOCK, HALF), BF),
        "grad_out": pltpu.VMEM((BLOCK, HALF), BF),
    }


def common_scratch():
    dma = pltpu.SemaphoreType.DMA
    return {
        "wide": pltpu.VMEM((4, 2, D, HIDDEN), BF),
        "tall": pltpu.VMEM((2, 2, HIDDEN, D), BF),
        "cot_whole": pltpu.VMEM((2, BLOCK, HALF), BF),
        "gate_keep": pltpu.VMEM((2, OWN, HIDDEN), F32),
        "up_keep": pltpu.VMEM((2, OWN, HIDDEN), F32),
        "sum_keep": pltpu.VMEM((OWN, D), F32),
        "item_rows": pltpu.VMEM((2 * BLOCK, HALF), F32),
        "tile_bits": pltpu.VMEM((TILE_DEV, 8, 128), jnp.int32),
        "load_sem": dma((3,)),
        "weight_own": dma((6,)),
        "weight_send": dma((6,)),
        "weight_recv": dma((6,)),
        "cot_send": dma,
        "cot_recv": dma,
        "owner_in": pltpu.VMEM((2, PARTS, OWN, HALF), BF),
        "item_in": pltpu.VMEM((PARTS, BLOCK, HALF), BF),
        "words_send": dma,
        "words_recv": dma,
        "rows_send": dma,
        "rows_recv": dma((PLANE,)),
        "owner_send": dma((2,)),
        "owner_recv": dma((2,)),
        "block_send": dma((2,)),
        "block_recv": dma((2, PLANE)),
        "item_send": dma,
        "item_recv": dma,
        "grad_send": dma,
        "grad_recv": dma((PLANE,)),
        "back_send": dma,
        "back_recv": dma,
    }


class Mode:
    def __init__(self, core, refs, z, q):
        self.core = core
        self.members, self.columns = (RING, PLANE) if core == 0 else (PLANE, RING)
        self.own_member, self.own_column = (z, q) if core == 0 else (q, z)
        self.first = 0 if core == 0 else PLANE
        self.first_item = 0 if core == 0 else RING
        self.z, self.q = z, q
        self.__dict__.update(refs)

    def item_shard(self, member):
        return member * PLANE + self.q if self.core == 0 else self.z * PLANE + member

    def basket_shard(self, column):
        return self.z * PLANE + column if self.core == 0 else column * PLANE + self.q


def kernel(
    rows_hbm,
    cot_hbm,
    bits_hbm,
    item_ref,
    dest_ref,
    gain_b_ref,
    gain_i_ref,
    gate_b_ref,
    up_b_ref,
    down_b_ref,
    gate_i_ref,
    up_i_ref,
    down_i_ref,
    back_ref,
    common,
    ring_refs,
    plane_refs,
):
    shard = lax.axis_index("shard")
    m = lax.axis_index("mp")
    other = 1 - m
    z = lax.div(shard, PLANE)
    q = lax.rem(shard, PLANE)
    me = 2 * q + m
    modes = (Mode(0, ring_refs, z, q), Mode(1, plane_refs, z, q))
    wide, tall, cot_whole = common["wide"], common["tall"], common["cot_whole"]
    gate_keep, up_keep, sum_keep = common["gate_keep"], common["up_keep"], common["sum_keep"]
    rows_ref, bits_ref, load_sem = common["item_rows"], common["tile_bits"], common["load_sem"]
    weight_own, weight_send = common["weight_own"], common["weight_send"]
    weight_recv = common["weight_recv"]
    cot_send, cot_recv = common["cot_send"], common["cot_recv"]
    owner_in, item_in = common["owner_in"], common["item_in"]
    words_send, words_recv = common["words_send"], common["words_recv"]
    rows_send, rows_recv = common["rows_send"], common["rows_recv"]
    owner_send, owner_recv = common["owner_send"], common["owner_recv"]
    block_send, block_recv = common["block_send"], common["block_recv"]
    item_send, item_recv = common["item_send"], common["item_recv"]
    grad_send, grad_recv = common["grad_send"], common["grad_recv"]
    back_send, back_recv = common["back_send"], common["back_recv"]

    def remote(src, dst, send, recv, to_shard, to_core):
        return pltpu.make_async_remote_copy(
            src_ref=src,
            dst_ref=dst,
            send_sem=send,
            recv_sem=recv,
            device_id=(to_shard, to_core),
            device_id_type=MESH,
        )

    def arrived(ref, recv):
        remote(ref, ref, cot_send, recv, shard, other).wait_recv()

    def sent(ref, send):
        remote(ref, ref, send, cot_recv, shard, other).wait_send()

    def around(count, own, body):
        def step(n, carry):
            body(lax.rem(own + n, count))
            return carry

        lax.fori_loop(1, count, step, 0)

    def ahead(count, own, size, work, send, send_own):
        def group(n, last):
            places = [lax.rem(own + n * size + i + 1, count) for i in range(size)]
            work(places)
            for place in places[: size - 1] if last else places:
                send(place)
            if last:
                send_own()

        def step(n, carry):
            group(n, False)
            return carry

        lax.fori_loop(0, count // size - 1, step, 0)
        group(count // size - 1, True)

    def behind(count, own, size, wait_own, wait, work):
        def group(n, first):
            places = [lax.rem(own + count - n * size - i, count) for i in range(size)]
            if first:
                wait_own()
            for place in places[1:] if first else places:
                wait(place)
            work(places)

        def step(n, carry):
            group(n, False)
            return carry

        group(0, True)
        lax.fori_loop(1, count // size, step, 0)

    def per_mode(body):
        for mode in modes:

            @pl.when(m == mode.core)
            def _(mode=mode):
                body(mode)

    weights = (
        (gate_b_ref, wide.at[0]),
        (up_b_ref, wide.at[1]),
        (down_b_ref, tall.at[0]),
        (gate_i_ref, wide.at[2]),
        (up_i_ref, wide.at[3]),
        (down_i_ref, tall.at[1]),
    )

    def own_weight(n):
        src, dst = weights[n]
        return pltpu.make_async_copy(src, dst.at[m], weight_own.at[n])

    def sibling_weight(n):
        src, dst = weights[n]
        return remote(src, dst.at[m], weight_send.at[n], weight_recv.at[n], shard, other)

    load_rows = pltpu.make_async_copy(rows_hbm, rows_ref, load_sem.at[0])
    load_bits = pltpu.make_async_copy(bits_hbm, bits_ref, load_sem.at[1])
    load_cot = pltpu.make_async_copy(
        cot_hbm.at[rows16(m * BLOCK, BLOCK)], cot_whole.at[m], load_sem.at[2]
    )
    load_rows.start()
    load_bits.start()

    barrier = pltpu.get_barrier_semaphore()

    def greet(to_shard, to_core):
        pl.semaphore_signal(
            barrier, inc=1, device_id=(to_shard, to_core), device_id_type=MESH
        )

    def greet_ring(z_to):
        for core in range(2):
            greet(z_to * PLANE + q, core)

    around(RING, z, greet_ring)
    around(2 * PLANE, me, lambda k: greet(z * PLANE + lax.div(k, 2), lax.rem(k, 2)))
    load_cot.start()
    for n in range(6):
        own_weight(n).start()

    sub = lax.broadcasted_iota(jnp.int32, (8, 128), 0)
    lane = lax.broadcasted_iota(jnp.int32, (8, 128), 1)

    def prepare(mode):
        mode.rows[0, mode.own_member] = rows_ref[...].astype(BF)
        columns = mode.columns
        per_slot = 128 // columns
        slots = TILE_DEV // per_slot
        if mode.core == 0:
            tiles = [bits_ref[t] for t in range(TILE_DEV)]
        else:
            left = lax.broadcasted_iota(jnp.int32, (128, 128), 0)
            right = lax.broadcasted_iota(jnp.int32, (128, 128), 1)
            order = jnp.where(
                (left % PLANE == right // columns) & (left // PLANE == right % columns), 1.0, 0.0
            ).astype(BF)
            words = bits_ref[...].reshape(128, 128)
            low = dot((words & 255).astype(F32).astype(BF), order)
            high = dot(jnp.right_shift(words, 8).astype(F32).astype(BF), order)
            words = (low + 256.0 * high).astype(jnp.int32).reshape(TILE_DEV, 8, 128)
            tiles = [words[t] for t in range(TILE_DEV)]
        group = lane // columns
        about = jnp.zeros((8, 128), jnp.int32)
        start = mode.own_member * TILE_DEV
        dest_sub = 2 + lax.div(start, 128)
        dest_lane = lax.rem(start, 128)
        for t in range(TILE_DEV):
            slot, place = t // per_slot, t % per_slot
            about = jnp.where((sub == slot) & (group == place), item_ref[t], about)
            about = jnp.where((sub == dest_sub) & (lane == dest_lane + t), dest_ref[t], about)
        for member in range(mode.members):
            for slot in range(slots):
                values = jnp.zeros((8, 128), jnp.int32)
                for place in range(per_slot):
                    turned = tiles[slot * per_slot + place]
                    shift = (columns * (place - member)) % 128
                    if shift:
                        turned = pltpu.roll(turned, shift, 1)
                    values = jnp.where(group == place, turned, values)
                mode.words_out[member, slot] = values
            mode.words_out[member, slots] = about
        mode.words_in[mode.own_member] = mode.words_out[mode.own_member]

    load_rows.wait()
    load_bits.wait()
    per_mode(prepare)

    pl.semaphore_wait(barrier, 2 * PLANE - 1 + 2 * (RING - 1))

    def words_copy(mode, member):
        return remote(
            mode.words_out.at[member],
            mode.words_in.at[mode.own_member],
            words_send,
            words_recv,
            mode.item_shard(member),
            mode.core,
        )

    def rows_copy(mode, member):
        return remote(
            mode.rows.at[0, mode.own_member],
            mode.rows.at[0, mode.own_member],
            rows_send,
            rows_recv.at[mode.own_member],
            mode.item_shard(member),
            mode.core,
        )

    def start_rows(mode):
        around(mode.members, mode.own_member, lambda member: words_copy(mode, member).start())
        around(mode.members, mode.own_member, lambda member: rows_copy(mode, member).start())

    per_mode(start_rows)

    def cot_copy():
        return remote(
            cot_hbm.at[rows16(other * BLOCK, BLOCK)],
            cot_whole.at[m],
            cot_send,
            cot_recv,
            shard,
            other,
        )

    for n in range(3):
        sibling_weight(n).start()
    cot_copy().start()
    for n in range(3, 6):
        sibling_weight(n).start()

    def add_tiles(mode, phase, members):
        all_sums = [dot(mode.collect[member], mode.rows[phase, member]) for member in members]
        shape = (mode.columns, TILE_DEV, HALF)
        tiles = TILE_DEV * mode.members
        for member, sums in zip(members, all_sums):
            high = sums.astype(BF)
            low = (sums - high.astype(F32)).astype(BF)
            mode.tile_sums[:, rows16(member * TILE_DEV, TILE_DEV), :] = high.reshape(shape)
            mode.tile_sums[:, rows16(tiles + member * TILE_DEV, TILE_DEV), :] = low.reshape(shape)

    def take_rows(mode):
        size = TILE_DEV * mode.columns
        slots = size // 128
        left = lax.broadcasted_iota(jnp.int32, (size, size), 0)
        right = lax.broadcasted_iota(jnp.int32, (size, size), 1)

        def turn(tile_major, column_major):
            same = (tile_major // mode.columns == column_major % TILE_DEV) & (
                tile_major % mode.columns == column_major // TILE_DEV
            )
            return jnp.where(same, 1.0, 0.0).astype(BF)

        to_columns = turn(left, right)
        from_tiles = turn(right, left)
        shifts = lax.broadcasted_iota(jnp.int32, (8, 16, 128), 1)

        def unpack(member):
            about = mode.words_in[member, slots]
            halves = []
            for slot in range(slots):
                packed = jnp.broadcast_to(mode.words_in[member, slot][:, None, :], (8, 16, 128))
                bits = (jnp.right_shift(packed, shifts) & 1).reshape(128, 128).astype(F32)
                halves.append((bits, jnp.broadcast_to(about[slot : slot + 1, :], (128, 128))))
            blocks = []
            for block in range(2):
                parts = [jnp.where(item == block, bits, 0.0) for bits, item in halves]
                blocks.append(parts[0] if slots == 1 else jnp.concatenate(parts, axis=1))
            mat = jnp.concatenate(blocks, axis=0).astype(BF)
            mode.spread[member] = dot(mat, to_columns).astype(BF)
            mode.collect[member] = dot_nt(from_tiles, mat).astype(BF)

        def unpack_pair(n, carry):
            for i in range(2):
                unpack(2 * n + i)
            return carry

        arrived(mode.words_in.at[: mode.members - 1], words_recv)
        lax.fori_loop(0, mode.members // 2, unpack_pair, 0)

        tiles = TILE_DEV * mode.members
        about = mode.words_in[0, slots]
        for member in range(1, mode.members):
            about = about + mode.words_in[member, slots]
        all_dest = about[2:3, :]
        if tiles > 128:
            all_dest = jnp.concatenate([all_dest, about[3:4, :]], axis=1)
        block_of = lax.broadcasted_iota(jnp.int32, (BLOCK, tiles), 0)
        one_hot = jnp.where(block_of == all_dest, 1.0, 0.0).astype(BF)
        mode.select_cols[...] = jnp.concatenate([one_hot, one_hot], axis=1)
        eye_left = lax.broadcasted_iota(jnp.int32, (tiles, tiles), 0)
        eye_right = lax.broadcasted_iota(jnp.int32, (tiles, tiles), 1)
        eye = jnp.where(eye_left == eye_right, 1.0, 0.0).astype(BF)
        mode.select_rows[...] = lax.dot_general(
            eye, one_hot, (((1,), (1,)), ((), ())), preferred_element_type=F32
        ).astype(BF)

        behind(
            mode.members,
            mode.own_member,
            2,
            lambda: None,
            lambda member: arrived(mode.rows.at[0, member], rows_recv.at[member]),
            lambda members: add_tiles(mode, 0, members),
        )

    per_mode(take_rows)

    def owner_copy(mode, phase, column, to_core):
        return remote(
            mode.owner_out.at[phase, 2 * column + to_core],
            owner_in.at[phase, mode.first + mode.own_column],
            owner_send.at[phase],
            owner_recv.at[phase],
            mode.basket_shard(column),
            to_core,
        )

    def send_sums(mode, phase):
        def column_sums(columns):
            for k in range(0, len(columns), 2):
                pair = jnp.concatenate([mode.tile_sums[c] for c in columns[k : k + 2]], axis=1)
                total = dot(mode.select_cols[...], pair).astype(BF)
                for i, column in enumerate(columns[k : k + 2]):
                    mode.owner_out[phase, pl.ds(2 * column, 2)] = total[
                        :, i * HALF : (i + 1) * HALF
                    ].reshape(2, OWN, HALF)

        def send(column):
            for to_core in range(2):
                owner_copy(mode, phase, column, to_core).start()

        def send_own():
            owner_copy(mode, phase, mode.own_column, 1 - mode.core).start()

        ahead(mode.columns, mode.own_column, 4, column_sums, send, send_own)
        owner_in[phase, mode.first + mode.own_column] = mode.owner_out[
            phase, 2 * mode.own_column + mode.core
        ]

    def sum_at_owners(phase):
        per_mode(lambda mode: send_sums(mode, phase))
        arrived(owner_in.at[phase, : PARTS - 1], owner_recv.at[phase])
        halves = []
        for mode in modes:
            total = owner_in[phase, mode.first].astype(F32)
            for column in range(1, mode.columns):
                total = total + owner_in[phase, mode.first + column].astype(F32)
            halves.append(total)
        return jnp.concatenate(halves, axis=1)

    def block_copy(mode, phase, column):
        return remote(
            mode.block_out.at[phase],
            mode.block_in.at[phase, mode.own_column, rows16(m * OWN, OWN)],
            block_send.at[phase],
            block_recv.at[phase, mode.own_column],
            mode.basket_shard(column),
            mode.core,
        )

    def send_blocks(phase, values):
        for mode in modes:
            mode.block_out[phase] = values[:, mode.core * HALF : (mode.core + 1) * HALF]
        for mode in modes:

            @pl.when(m != mode.core)
            def _(mode=mode):
                block_copy(mode, phase, mode.own_column).start()

            around(
                mode.columns,
                mode.own_column,
                lambda column, mode=mode: block_copy(mode, phase, column).start(),
            )

            @pl.when(m == mode.core)
            def _(mode=mode):
                place = slice(mode.core * OWN, (mode.core + 1) * OWN)
                mode.block_in[phase, mode.own_column, place, :] = mode.block_out[phase]

    def pick_all(mode, phase):
        def pick(columns):
            for k in range(0, len(columns), 2):
                pair = jnp.concatenate(
                    [mode.block_in[phase, c] for c in columns[k : k + 2]], axis=1
                )
                chosen = dot(mode.select_rows[...], pair).astype(BF)
                for i, column in enumerate(columns[k : k + 2]):
                    mode.picked[:, rows16(column * TILE_DEV, TILE_DEV), :] = chosen[
                        :, i * HALF : (i + 1) * HALF
                    ].reshape(mode.members, TILE_DEV, HALF)

        behind(
            mode.columns,
            mode.own_column,
            4,
            lambda: arrived(
                mode.block_in.at[phase, mode.own_column, :OWN],
                block_recv.at[phase, mode.own_column],
            ),
            lambda column: arrived(mode.block_in.at[phase, column], block_recv.at[phase, column]),
            pick,
        )

    basket_gain = gain_b_ref[...]
    item_gain = gain_i_ref[...]

    basket_sum = sum_at_owners(0)
    sum_keep[...] = basket_sum
    for n in range(3):
        own_weight(n).wait()
        sibling_weight(n).wait_recv()
    normed = basket_sum * rms_scale(basket_sum) * basket_gain
    normed_bf = normed.astype(BF)
    total = normed
    for h in range(2):
        gate_pre = dot(normed_bf, wide[0, h])
        up_pre = dot(normed_bf, wide[1, h])
        gate_keep[h] = gate_pre
        up_keep[h] = up_pre
        hidden = (gate_pre * jax.nn.sigmoid(gate_pre) * up_pre).astype(BF)
        total = total + dot(hidden, tall[0, h])
    send_blocks(0, total.astype(BF))

    def item_copy(mode, member, to_core):
        return remote(
            mode.item_out.at[0, 2 * member + to_core],
            item_in.at[mode.first_item + mode.own_member],
            item_send,
            item_recv,
            mode.item_shard(member),
            to_core,
        )

    def send_items(mode):
        pick_all(mode, 0)

        def partials(members):
            totals = [dot(mode.spread[member], mode.picked[member]) for member in members]
            for member, total in zip(members, totals):
                mode.item_out[0, pl.ds(2 * member, 2)] = total.astype(BF).reshape(2, BLOCK, HALF)

        def send(member):
            for to_core in range(2):
                item_copy(mode, member, to_core).start()

        def send_own():
            item_copy(mode, mode.own_member, 1 - mode.core).start()

        ahead(mode.members, mode.own_member, 2, partials, send, send_own)
        item_in[mode.first_item + mode.own_member] = mode.item_out[
            0, 2 * mode.own_member + mode.core
        ]

    per_mode(send_items)

    for n in range(3, 6):
        own_weight(n).wait()
        sibling_weight(n).wait_recv()
    arrived(cot_whole.at[other], cot_recv)
    load_cot.wait()
    arrived(item_in.at[: PARTS - 1], item_recv)
    halves = []
    for mode in modes:
        summed = item_in[mode.first_item].astype(F32)
        for member in range(1, mode.members):
            summed = summed + item_in[mode.first_item + member].astype(F32)
        halves.append(summed)
    message = jnp.concatenate(halves, axis=1)
    cot_full = jnp.concatenate([cot_whole[0], cot_whole[1]], axis=1)
    scale_item = rms_scale(message)
    query = (message * scale_item * item_gain).astype(BF)
    grad_query = jnp.zeros((BLOCK, D), F32)
    for h in range(2):
        gate_pre = dot(query, wide[2, h])
        up_pre = dot(query, wide[3, h])
        grad_hidden = dot_nt(cot_full, tall[1, h])
        value, slope = silu_parts(gate_pre)
        grad_up = (grad_hidden * value).astype(BF)
        grad_gate = (grad_hidden * up_pre * slope).astype(BF)
        grad_query = grad_query + dot_nt(grad_gate, wide[2, h]) + dot_nt(grad_up, wide[3, h])
    inner = jnp.sum(item_gain * grad_query * message, axis=1, keepdims=True)
    cubed = scale_item * scale_item * scale_item
    grad_message = (scale_item * item_gain * grad_query - message * cubed * inner / D).astype(BF)

    def grad_copy(mode, member):
        return remote(
            mode.grad_out,
            mode.rows.at[1, mode.own_member, rows16(m * BLOCK, BLOCK)],
            grad_send,
            grad_recv.at[mode.own_member],
            mode.item_shard(member),
            mode.core,
        )

    for mode in modes:
        mode.grad_out[...] = grad_message[:, mode.core * HALF : (mode.core + 1) * HALF]
    for mode in modes:

        @pl.when(m != mode.core)
        def _(mode=mode):
            grad_copy(mode, mode.own_member).start()

        around(
            mode.members,
            mode.own_member,
            lambda member, mode=mode: grad_copy(mode, member).start(),
        )

        @pl.when(m == mode.core)
        def _(mode=mode):
            place = slice(mode.core * BLOCK, (mode.core + 1) * BLOCK)
            mode.rows[1, mode.own_member, place, :] = mode.grad_out[...]

    def take_grads(mode):
        behind(
            mode.members,
            mode.own_member,
            2,
            lambda: arrived(
                mode.rows.at[1, mode.own_member, :BLOCK], grad_recv.at[mode.own_member]
            ),
            lambda member: arrived(mode.rows.at[1, member], grad_recv.at[member]),
            lambda members: add_tiles(mode, 1, members),
        )

    per_mode(take_grads)
    grad_out = sum_at_owners(1)
    grad_out_bf = grad_out.astype(BF)
    grad_normed = grad_out
    for h in range(2):
        grad_hidden = dot_nt(grad_out_bf, tall[0, h])
        value, slope = silu_parts(gate_keep[h])
        grad_up = (grad_hidden * value).astype(BF)
        grad_gate = (grad_hidden * up_keep[h] * slope).astype(BF)
        grad_normed = grad_normed + (dot_nt(grad_gate, wide[0, h]) + dot_nt(grad_up, wide[1, h]))
    sums = sum_keep[...]
    scale_basket = rms_scale(sums)
    inner_basket = jnp.sum(basket_gain * grad_normed * sums, axis=1, keepdims=True)
    cubed_basket = scale_basket * scale_basket * scale_basket
    grad_sum = scale_basket * basket_gain * grad_normed - sums * cubed_basket * inner_basket / D
    send_blocks(1, grad_sum.astype(BF))

    def back_copy(mode, member):
        return remote(
            mode.item_out.at[1, pl.ds(2 * member, 2)],
            mode.back_in.at[mode.own_member],
            back_send,
            back_recv,
            mode.item_shard(member),
            mode.core,
        )

    def finish(mode):
        pick_all(mode, 1)

        def partials(members):
            totals = [dot(mode.spread[member], mode.picked[member]) for member in members]
            for member, total in zip(members, totals):
                mode.item_out[1, pl.ds(2 * member, 2)] = total.astype(BF).reshape(2, BLOCK, HALF)

        ahead(
            mode.members,
            mode.own_member,
            2,
            partials,
            lambda member: back_copy(mode, member).start(),
            lambda: None,
        )
        mode.back_in[mode.own_member] = mode.item_out[1, pl.ds(2 * mode.own_member, 2)]
        sent(mode.words_out.at[: mode.members - 1], words_send)
        sent(mode.rows.at[0, : mode.members - 1], rows_send)
        sent(mode.item_out.at[0, : 2 * mode.members - 1], item_send)
        for phase in range(2):
            sent(mode.owner_out.at[phase, : 2 * mode.columns - 1], owner_send.at[phase])
            sent(owner_in.at[phase, : PARTS - 1], block_send.at[phase])
        sent(item_in.at[: PARTS - 1], grad_send)
        arrived(mode.back_in.at[: mode.members - 1], back_recv)
        for block in range(2):
            back = mode.back_in[0, block].astype(F32)
            for member in range(1, mode.members):
                back = back + mode.back_in[member, block].astype(F32)
            back_ref[block * BLOCK : (block + 1) * BLOCK, :] = back
        sent(mode.back_in.at[: mode.members - 1], back_send)

    per_mode(finish)

    for n in range(6):
        sibling_weight(n).wait_send()
    cot_copy().wait_send()


def local(
    item_rows,
    first_moment,
    second_moment,
    item_cot,
    tile_bits,
    tile_item,
    tile_dest,
    basket_gain,
    item_gain,
    gate_basket,
    up_basket,
    down_basket,
    gate_item,
    up_item,
    down_item,
):
    vmem = pl.BlockSpec(memory_space=pltpu.VMEM)
    smem = pl.BlockSpec(memory_space=pltpu.SMEM)
    anywhere = pl.BlockSpec(memory_space=pltpu.HBM)
    back_items = pl.pallas_call(
        kernel,
        out_shape=jax.ShapeDtypeStruct((2 * BLOCK, HALF), F32),
        in_specs=[anywhere] * 3 + [smem, smem, vmem, vmem] + [anywhere] * 6,
        out_specs=vmem,
        scratch_shapes=[
            common_scratch(),
            mode_scratch(RING, PLANE),
            mode_scratch(PLANE, RING),
        ],
        compiler_params=pltpu.CompilerParams(
            collective_id=0, has_side_effects=True, vmem_limit_bytes=60 * 1024 * 1024
        ),
        name="layer",
    )(
        item_rows,
        item_cot,
        tile_bits,
        tile_item,
        tile_dest,
        basket_gain.reshape(1, D),
        item_gain.reshape(1, D),
        gate_basket,
        up_basket,
        down_basket,
        gate_item,
        up_item,
        down_item,
    )
    gradient = item_cot.astype(F32) + back_items
    new_first = BETA_FIRST * first_moment + (1.0 - BETA_FIRST) * gradient
    new_second = BETA_SECOND * second_moment + (1.0 - BETA_SECOND) * gradient * gradient
    new_rows = item_rows - LEARNING_RATE * new_first / (jnp.sqrt(new_second) + ADAM_EPSILON)
    return (new_rows, new_first, new_second)


def solution(mesh):
    split = P("shard", "mp")
    return jax.shard_map(
        local,
        mesh=mesh,
        in_specs=(
            split,
            split,
            split,
            split,
            P("shard", None, None),
            P("shard"),
            P("shard"),
            P(),
            P(),
            P(None, "mp"),
            P(None, "mp"),
            P("mp", None),
            P(None, "mp"),
            P(None, "mp"),
            P("mp", None),
        ),
        out_specs=(split, split, split),
        check_vma=False,
    )
```

```python
import jax
import jax.numpy as jnp
from jax import lax
from jax.experimental import pallas as pl
from jax.experimental.pallas import tpu as pltpu
from jax.sharding import PartitionSpec as P

D = 256
HALF = 128
BLOCK = 128
TILE_DEV = 16
RING = 8
PLANE = 16
PARTS = RING + PLANE
OWN = 64
HIDDEN = 1024

NORM_EPSILON = 1e-05
LEARNING_RATE = 0.01
BETA_FIRST = 0.9
BETA_SECOND = 0.99
ADAM_EPSILON = 1e-08

MESH = pl.DeviceIdType.MESH
BF = jnp.bfloat16
F32 = jnp.float32


def dot(a, b):
    return jnp.dot(a, b, preferred_element_type=F32)


def dot_nt(a, b):
    return lax.dot_general(a, b, (((1,), (1,)), ((), ())), preferred_element_type=F32)


def silu_parts(gate_values):
    sigmoid = jax.nn.sigmoid(gate_values)
    return (gate_values * sigmoid, sigmoid * (1.0 + gate_values * (1.0 - sigmoid)))


def rms_scale(values):
    return lax.rsqrt(jnp.mean(values * values, axis=-1, keepdims=True) + NORM_EPSILON)


def rows16(start, size):
    return pl.ds(pl.multiple_of(start, 16), size)


def mode_scratch(members, columns):
    wide = TILE_DEV * columns
    tiles = TILE_DEV * members
    slots = wide // 128 + 1
    return {
        "words_out": pltpu.VMEM((members, slots, 8, 128), jnp.int32),
        "words_in": pltpu.VMEM((members, slots, 8, 128), jnp.int32),
        "rows": pltpu.VMEM((2, members, 2 * BLOCK, HALF), BF),
        "spread": pltpu.VMEM((members, 2 * BLOCK, wide), BF),
        "collect": pltpu.VMEM((members, wide, 2 * BLOCK), BF),
        "select_cols": pltpu.VMEM((BLOCK, 2 * tiles), BF),
        "select_rows": pltpu.VMEM((tiles, BLOCK), BF),
        "tile_sums": pltpu.VMEM((columns, 2 * tiles, HALF), BF),
        "owner_out": pltpu.VMEM((2, 2 * columns, OWN, HALF), BF),
        "block_out": pltpu.VMEM((2, OWN, HALF), BF),
        "block_in": pltpu.VMEM((2, columns, BLOCK, HALF), BF),
        "picked": pltpu.VMEM((members, wide, HALF), BF),
        "item_out": pltpu.VMEM((2, 2 * members, BLOCK, HALF), BF),
        "back_in": pltpu.VMEM((members, 2, BLOCK, HALF), BF),
        "grad_out": pltpu.VMEM((BLOCK, HALF), BF),
    }


def common_scratch():
    dma = pltpu.SemaphoreType.DMA
    return {
        "wide": pltpu.VMEM((4, 2, D, HIDDEN), BF),
        "tall": pltpu.VMEM((2, 2, HIDDEN, D), BF),
        "cot_whole": pltpu.VMEM((2, BLOCK, HALF), BF),
        "gate_keep": pltpu.VMEM((2, OWN, HIDDEN), F32),
        "up_keep": pltpu.VMEM((2, OWN, HIDDEN), F32),
        "sum_keep": pltpu.VMEM((OWN, D), F32),
        "item_rows": pltpu.VMEM((2 * BLOCK, HALF), F32),
        "tile_bits": pltpu.VMEM((TILE_DEV, 8, 128), jnp.int32),
        "load_sem": dma((3,)),
        "weight_own": dma((6,)),
        "weight_send": dma((6,)),
        "weight_recv": dma((6,)),
        "cot_send": dma,
        "cot_recv": dma,
        "owner_in": pltpu.VMEM((2, PARTS, OWN, HALF), BF),
        "item_in": pltpu.VMEM((2, PARTS, BLOCK // 2, HALF), BF),
        "words_send": dma,
        "words_recv": dma,
        "rows_send": dma,
        "rows_recv": dma((PLANE,)),
        "owner_send": dma((2,)),
        "owner_recv": dma((2,)),
        "block_send": dma((2,)),
        "block_recv": dma((2, PLANE)),
        "item_send": dma,
        "item_recv": dma((2,)),
        "grad_send": dma((2,)),
        "grad_recv": dma((PLANE,)),
        "back_send": dma,
        "back_recv": dma,
    }


class Mode:
    def __init__(self, core, refs, z, q):
        self.core = core
        self.members, self.columns = (RING, PLANE) if core == 0 else (PLANE, RING)
        self.own_member, self.own_column = (z, q) if core == 0 else (q, z)
        self.first = 0 if core == 0 else PLANE
        self.first_item = 0 if core == 0 else RING
        self.z, self.q = z, q
        self.__dict__.update(refs)

    def item_shard(self, member):
        return member * PLANE + self.q if self.core == 0 else self.z * PLANE + member

    def basket_shard(self, column):
        return self.z * PLANE + column if self.core == 0 else column * PLANE + self.q


def kernel(
    rows_hbm,
    cot_hbm,
    bits_hbm,
    item_ref,
    dest_ref,
    gain_b_ref,
    gain_i_ref,
    gate_b_ref,
    up_b_ref,
    down_b_ref,
    gate_i_ref,
    up_i_ref,
    down_i_ref,
    back_ref,
    common,
    ring_refs,
    plane_refs,
):
    shard = lax.axis_index("shard")
    m = lax.axis_index("mp")
    other = 1 - m
    z = lax.div(shard, PLANE)
    q = lax.rem(shard, PLANE)
    me = 2 * q + m
    modes = (Mode(0, ring_refs, z, q), Mode(1, plane_refs, z, q))
    wide, tall, cot_whole = common["wide"], common["tall"], common["cot_whole"]
    gate_keep, up_keep, sum_keep = common["gate_keep"], common["up_keep"], common["sum_keep"]
    rows_ref, bits_ref, load_sem = common["item_rows"], common["tile_bits"], common["load_sem"]
    weight_own, weight_send = common["weight_own"], common["weight_send"]
    weight_recv = common["weight_recv"]
    cot_send, cot_recv = common["cot_send"], common["cot_recv"]
    owner_in, item_in = common["owner_in"], common["item_in"]
    words_send, words_recv = common["words_send"], common["words_recv"]
    rows_send, rows_recv = common["rows_send"], common["rows_recv"]
    owner_send, owner_recv = common["owner_send"], common["owner_recv"]
    block_send, block_recv = common["block_send"], common["block_recv"]
    item_send, item_recv = common["item_send"], common["item_recv"]
    grad_send, grad_recv = common["grad_send"], common["grad_recv"]
    back_send, back_recv = common["back_send"], common["back_recv"]

    def remote(src, dst, send, recv, to_shard, to_core):
        return pltpu.make_async_remote_copy(
            src_ref=src,
            dst_ref=dst,
            send_sem=send,
            recv_sem=recv,
            device_id=(to_shard, to_core),
            device_id_type=MESH,
        )

    def arrived(ref, recv):
        remote(ref, ref, cot_send, recv, shard, other).wait_recv()

    def sent(ref, send):
        remote(ref, ref, send, cot_recv, shard, other).wait_send()

    def around(count, own, body):
        def step(n, carry):
            body(lax.rem(own + n, count))
            return carry

        lax.fori_loop(1, count, step, 0)

    def ahead(count, own, size, work, send, send_own):
        def group(n, last):
            places = [lax.rem(own + n * size + i + 1, count) for i in range(size)]
            work(places)
            for place in places[: size - 1] if last else places:
                send(place)
            if last:
                send_own()

        def step(n, carry):
            group(n, False)
            return carry

        lax.fori_loop(0, count // size - 1, step, 0)
        group(count // size - 1, True)

    def behind(count, own, size, wait_own, wait, work):
        def group(n, first):
            places = [lax.rem(own + count - n * size - i, count) for i in range(size)]
            if first:
                wait_own()
            for place in places[1:] if first else places:
                wait(place)
            work(places)

        def step(n, carry):
            group(n, False)
            return carry

        group(0, True)
        lax.fori_loop(1, count // size, step, 0)

    def per_mode(body):
        for mode in modes:

            @pl.when(m == mode.core)
            def _(mode=mode):
                body(mode)

    weights = (
        (gate_b_ref, wide.at[0]),
        (up_b_ref, wide.at[1]),
        (down_b_ref, tall.at[0]),
        (gate_i_ref, wide.at[2]),
        (up_i_ref, wide.at[3]),
        (down_i_ref, tall.at[1]),
    )

    def own_weight(n):
        src, dst = weights[n]
        return pltpu.make_async_copy(src, dst.at[m], weight_own.at[n])

    def sibling_weight(n):
        src, dst = weights[n]
        return remote(src, dst.at[m], weight_send.at[n], weight_recv.at[n], shard, other)

    load_rows = pltpu.make_async_copy(rows_hbm, rows_ref, load_sem.at[0])
    load_bits = pltpu.make_async_copy(bits_hbm, bits_ref, load_sem.at[1])
    load_cot = pltpu.make_async_copy(
        cot_hbm.at[rows16(m * BLOCK, BLOCK)], cot_whole.at[m], load_sem.at[2]
    )
    load_rows.start()
    load_bits.start()

    barrier = pltpu.get_barrier_semaphore()

    def greet(to_shard, to_core):
        pl.semaphore_signal(
            barrier, inc=1, device_id=(to_shard, to_core), device_id_type=MESH
        )

    def greet_ring(z_to):
        for core in range(2):
            greet(z_to * PLANE + q, core)

    around(RING, z, greet_ring)
    around(2 * PLANE, me, lambda k: greet(z * PLANE + lax.div(k, 2), lax.rem(k, 2)))
    load_cot.start()
    for n in range(6):
        own_weight(n).start()

    sub = lax.broadcasted_iota(jnp.int32, (8, 128), 0)
    lane = lax.broadcasted_iota(jnp.int32, (8, 128), 1)

    def prepare(mode):
        mode.rows[0, mode.own_member] = rows_ref[...].astype(BF)
        columns = mode.columns
        per_slot = 128 // columns
        slots = TILE_DEV // per_slot
        if mode.core == 0:
            tiles = [bits_ref[t] for t in range(TILE_DEV)]
        else:
            left = lax.broadcasted_iota(jnp.int32, (128, 128), 0)
            right = lax.broadcasted_iota(jnp.int32, (128, 128), 1)
            order = jnp.where(
                (left % PLANE == right // columns) & (left // PLANE == right % columns), 1.0, 0.0
            ).astype(BF)
            words = bits_ref[...].reshape(128, 128)
            low = dot((words & 255).astype(F32).astype(BF), order)
            high = dot(jnp.right_shift(words, 8).astype(F32).astype(BF), order)
            words = (low + 256.0 * high).astype(jnp.int32).reshape(TILE_DEV, 8, 128)
            tiles = [words[t] for t in range(TILE_DEV)]
        group = lane // columns
        about = jnp.zeros((8, 128), jnp.int32)
        start = mode.own_member * TILE_DEV
        dest_sub = 2 + lax.div(start, 128)
        dest_lane = lax.rem(start, 128)
        for t in range(TILE_DEV):
            slot, place = t // per_slot, t % per_slot
            about = jnp.where((sub == slot) & (group == place), item_ref[t], about)
            about = jnp.where((sub == dest_sub) & (lane == dest_lane + t), dest_ref[t], about)
        for member in range(mode.members):
            for slot in range(slots):
                values = jnp.zeros((8, 128), jnp.int32)
                for place in range(per_slot):
                    turned = tiles[slot * per_slot + place]
                    shift = (columns * (place - member)) % 128
                    if shift:
                        turned = pltpu.roll(turned, shift, 1)
                    values = jnp.where(group == place, turned, values)
                mode.words_out[member, slot] = values
            mode.words_out[member, slots] = about
        mode.words_in[mode.own_member] = mode.words_out[mode.own_member]

    load_rows.wait()
    load_bits.wait()
    per_mode(prepare)

    pl.semaphore_wait(barrier, 2 * PLANE - 1 + 2 * (RING - 1))

    def words_copy(mode, member):
        return remote(
            mode.words_out.at[member],
            mode.words_in.at[mode.own_member],
            words_send,
            words_recv,
            mode.item_shard(member),
            mode.core,
        )

    def rows_copy(mode, member):
        return remote(
            mode.rows.at[0, mode.own_member],
            mode.rows.at[0, mode.own_member],
            rows_send,
            rows_recv.at[mode.own_member],
            mode.item_shard(member),
            mode.core,
        )

    def start_rows(mode):
        around(mode.members, mode.own_member, lambda member: words_copy(mode, member).start())
        around(mode.members, mode.own_member, lambda member: rows_copy(mode, member).start())

    per_mode(start_rows)

    def cot_copy():
        return remote(
            cot_hbm.at[rows16(other * BLOCK, BLOCK)],
            cot_whole.at[m],
            cot_send,
            cot_recv,
            shard,
            other,
        )

    for n in range(3):
        sibling_weight(n).start()
    cot_copy().start()
    for n in range(3, 6):
        sibling_weight(n).start()

    def add_tiles(mode, phase, members):
        all_sums = [dot(mode.collect[member], mode.rows[phase, member]) for member in members]
        shape = (mode.columns, TILE_DEV, HALF)
        tiles = TILE_DEV * mode.members
        for member, sums in zip(members, all_sums):
            high = sums.astype(BF)
            low = (sums - high.astype(F32)).astype(BF)
            mode.tile_sums[:, rows16(member * TILE_DEV, TILE_DEV), :] = high.reshape(shape)
            mode.tile_sums[:, rows16(tiles + member * TILE_DEV, TILE_DEV), :] = low.reshape(shape)

    def take_rows(mode):
        size = TILE_DEV * mode.columns
        slots = size // 128
        left = lax.broadcasted_iota(jnp.int32, (size, size), 0)
        right = lax.broadcasted_iota(jnp.int32, (size, size), 1)

        def turn(tile_major, column_major):
            same = (tile_major // mode.columns == column_major % TILE_DEV) & (
                tile_major % mode.columns == column_major // TILE_DEV
            )
            return jnp.where(same, 1.0, 0.0).astype(BF)

        to_columns = turn(left, right)
        from_tiles = turn(right, left)
        shifts = lax.broadcasted_iota(jnp.int32, (8, 16, 128), 1)

        def unpack(member):
            about = mode.words_in[member, slots]
            halves = []
            for slot in range(slots):
                packed = jnp.broadcast_to(mode.words_in[member, slot][:, None, :], (8, 16, 128))
                bits = (jnp.right_shift(packed, shifts) & 1).reshape(128, 128).astype(F32)
                halves.append((bits, jnp.broadcast_to(about[slot : slot + 1, :], (128, 128))))
            blocks = []
            for block in range(2):
                parts = [jnp.where(item == block, bits, 0.0) for bits, item in halves]
                blocks.append(parts[0] if slots == 1 else jnp.concatenate(parts, axis=1))
            mat = jnp.concatenate(blocks, axis=0).astype(BF)
            mode.spread[member] = dot(mat, to_columns).astype(BF)
            mode.collect[member] = dot_nt(from_tiles, mat).astype(BF)

        def unpack_some(n, carry):
            for i in range(4):
                unpack(4 * n + i)
            return carry

        arrived(mode.words_in.at[: mode.members - 1], words_recv)
        lax.fori_loop(0, mode.members // 4, unpack_some, 0)

        tiles = TILE_DEV * mode.members
        about = mode.words_in[0, slots]
        for member in range(1, mode.members):
            about = about + mode.words_in[member, slots]
        all_dest = about[2:3, :]
        if tiles > 128:
            all_dest = jnp.concatenate([all_dest, about[3:4, :]], axis=1)
        block_of = lax.broadcasted_iota(jnp.int32, (BLOCK, tiles), 0)
        one_hot = jnp.where(block_of == all_dest, 1.0, 0.0).astype(BF)
        mode.select_cols[...] = jnp.concatenate([one_hot, one_hot], axis=1)
        eye_left = lax.broadcasted_iota(jnp.int32, (tiles, tiles), 0)
        eye_right = lax.broadcasted_iota(jnp.int32, (tiles, tiles), 1)
        eye = jnp.where(eye_left == eye_right, 1.0, 0.0).astype(BF)
        mode.select_rows[...] = lax.dot_general(
            eye, one_hot, (((1,), (1,)), ((), ())), preferred_element_type=F32
        ).astype(BF)

        behind(
            mode.members,
            mode.own_member,
            2,
            lambda: None,
            lambda member: arrived(mode.rows.at[0, member], rows_recv.at[member]),
            lambda members: add_tiles(mode, 0, members),
        )

    per_mode(take_rows)

    def owner_copy(mode, phase, column, to_core):
        return remote(
            mode.owner_out.at[phase, 2 * column + to_core],
            owner_in.at[phase, mode.first + mode.own_column],
            owner_send.at[phase],
            owner_recv.at[phase],
            mode.basket_shard(column),
            to_core,
        )

    def send_sums(mode, phase):
        def column_sums(columns):
            for k in range(0, len(columns), 2):
                pair = jnp.concatenate([mode.tile_sums[c] for c in columns[k : k + 2]], axis=1)
                total = dot(mode.select_cols[...], pair).astype(BF)
                for i, column in enumerate(columns[k : k + 2]):
                    mode.owner_out[phase, pl.ds(2 * column, 2)] = total[
                        :, i * HALF : (i + 1) * HALF
                    ].reshape(2, OWN, HALF)

        def send(column):
            for to_core in range(2):
                owner_copy(mode, phase, column, to_core).start()

        def send_own():
            owner_copy(mode, phase, mode.own_column, 1 - mode.core).start()

        ahead(mode.columns, mode.own_column, 4, column_sums, send, send_own)
        owner_in[phase, mode.first + mode.own_column] = mode.owner_out[
            phase, 2 * mode.own_column + mode.core
        ]

    def sum_at_owners(phase):
        per_mode(lambda mode: send_sums(mode, phase))
        arrived(owner_in.at[phase, : PARTS - 1], owner_recv.at[phase])
        halves = []
        for mode in modes:
            total = owner_in[phase, mode.first].astype(F32)
            for column in range(1, mode.columns):
                total = total + owner_in[phase, mode.first + column].astype(F32)
            halves.append(total)
        return jnp.concatenate(halves, axis=1)

    def block_copy(mode, phase, column):
        return remote(
            mode.block_out.at[phase],
            mode.block_in.at[phase, mode.own_column, rows16(m * OWN, OWN)],
            block_send.at[phase],
            block_recv.at[phase, mode.own_column],
            mode.basket_shard(column),
            mode.core,
        )

    def send_blocks(phase, values):
        for mode in modes:
            mode.block_out[phase] = values[:, mode.core * HALF : (mode.core + 1) * HALF]
        for mode in modes:

            @pl.when(m != mode.core)
            def _(mode=mode):
                block_copy(mode, phase, mode.own_column).start()

            around(
                mode.columns,
                mode.own_column,
                lambda column, mode=mode: block_copy(mode, phase, column).start(),
            )

            @pl.when(m == mode.core)
            def _(mode=mode):
                place = slice(mode.core * OWN, (mode.core + 1) * OWN)
                mode.block_in[phase, mode.own_column, place, :] = mode.block_out[phase]

    def pick_all(mode, phase):
        def pick(columns):
            for k in range(0, len(columns), 2):
                pair = jnp.concatenate(
                    [mode.block_in[phase, c] for c in columns[k : k + 2]], axis=1
                )
                chosen = dot(mode.select_rows[...], pair).astype(BF)
                for i, column in enumerate(columns[k : k + 2]):
                    mode.picked[:, rows16(column * TILE_DEV, TILE_DEV), :] = chosen[
                        :, i * HALF : (i + 1) * HALF
                    ].reshape(mode.members, TILE_DEV, HALF)

        behind(
            mode.columns,
            mode.own_column,
            4,
            lambda: arrived(
                mode.block_in.at[phase, mode.own_column, :OWN],
                block_recv.at[phase, mode.own_column],
            ),
            lambda column: arrived(mode.block_in.at[phase, column], block_recv.at[phase, column]),
            pick,
        )

    basket_gain = gain_b_ref[...]
    item_gain = gain_i_ref[...]

    basket_sum = sum_at_owners(0)
    sum_keep[...] = basket_sum
    for n in range(3):
        own_weight(n).wait()
        sibling_weight(n).wait_recv()
    normed = basket_sum * rms_scale(basket_sum) * basket_gain
    normed_bf = normed.astype(BF)
    total = normed
    for h in range(2):
        gate_pre = dot(normed_bf, wide[0, h])
        up_pre = dot(normed_bf, wide[1, h])
        gate_keep[h] = gate_pre
        up_keep[h] = up_pre
        hidden = (gate_pre * jax.nn.sigmoid(gate_pre) * up_pre).astype(BF)
        total = total + dot(hidden, tall[0, h])
    send_blocks(0, total.astype(BF))

    def item_copy(mode, member, to_core, part):
        return remote(
            mode.item_out.at[0, 2 * member + to_core, pl.ds(part * BLOCK // 2, BLOCK // 2)],
            item_in.at[part, mode.first_item + mode.own_member],
            item_send,
            item_recv.at[part],
            mode.item_shard(member),
            to_core,
        )

    def send_items(mode):
        pick_all(mode, 0)

        def partials(members):
            totals = [dot(mode.spread[member], mode.picked[member]) for member in members]
            for member, total in zip(members, totals):
                mode.item_out[0, pl.ds(2 * member, 2)] = total.astype(BF).reshape(2, BLOCK, HALF)

        def send(member):
            for to_core in range(2):
                item_copy(mode, member, to_core, 0).start()

        def send_own():
            item_copy(mode, mode.own_member, 1 - mode.core, 0).start()

        def send_rest(member):
            for to_core in range(2):
                item_copy(mode, member, to_core, 1).start()

        ahead(mode.members, mode.own_member, 2, partials, send, send_own)
        around(mode.members, mode.own_member, send_rest)
        item_copy(mode, mode.own_member, 1 - mode.core, 1).start()
        own_out = mode.item_out[0, 2 * mode.own_member + mode.core]
        for part in range(2):
            rows = slice(part * BLOCK // 2, (part + 1) * BLOCK // 2)
            item_in[part, mode.first_item + mode.own_member] = own_out[rows, :]

    per_mode(send_items)

    for n in range(3, 6):
        own_weight(n).wait()
        sibling_weight(n).wait_recv()
    arrived(cot_whole.at[other], cot_recv)
    load_cot.wait()
    cot_full = jnp.concatenate([cot_whole[0], cot_whole[1]], axis=1)

    def item_layer(part):
        arrived(item_in.at[part, : PARTS - 1], item_recv.at[part])
        halves = []
        for mode in modes:
            summed = item_in[part, mode.first_item].astype(F32)
            for member in range(1, mode.members):
                summed = summed + item_in[part, mode.first_item + member].astype(F32)
            halves.append(summed)
        message = jnp.concatenate(halves, axis=1)
        cot = cot_full[part * BLOCK // 2 : (part + 1) * BLOCK // 2, :]
        scale_item = rms_scale(message)
        query = (message * scale_item * item_gain).astype(BF)
        grad_query = jnp.zeros((BLOCK // 2, D), F32)
        for h in range(2):
            gate_pre = dot(query, wide[2, h])
            up_pre = dot(query, wide[3, h])
            grad_hidden = dot_nt(cot, tall[1, h])
            value, slope = silu_parts(gate_pre)
            grad_up = (grad_hidden * value).astype(BF)
            grad_gate = (grad_hidden * up_pre * slope).astype(BF)
            grad_query = grad_query + dot_nt(grad_gate, wide[2, h]) + dot_nt(grad_up, wide[3, h])
        inner = jnp.sum(item_gain * grad_query * message, axis=1, keepdims=True)
        cubed = scale_item * scale_item * scale_item
        return (scale_item * item_gain * grad_query - message * cubed * inner / D).astype(BF)

    def grad_copy(mode, member, part):
        return remote(
            mode.grad_out.at[pl.ds(part * BLOCK // 2, BLOCK // 2)],
            mode.rows.at[1, mode.own_member, rows16(m * BLOCK + part * BLOCK // 2, BLOCK // 2)],
            grad_send.at[part],
            grad_recv.at[mode.own_member],
            mode.item_shard(member),
            mode.core,
        )

    for part in range(2):
        grad_message = item_layer(part)
        for mode in modes:
            rows = slice(part * BLOCK // 2, (part + 1) * BLOCK // 2)
            mode.grad_out[rows, :] = grad_message[:, mode.core * HALF : (mode.core + 1) * HALF]
        for mode in modes:

            @pl.when(m != mode.core)
            def _(mode=mode, part=part):
                grad_copy(mode, mode.own_member, part).start()

            around(
                mode.members,
                mode.own_member,
                lambda member, mode=mode, part=part: grad_copy(mode, member, part).start(),
            )
    for mode in modes:

        @pl.when(m == mode.core)
        def _(mode=mode):
            place = slice(mode.core * BLOCK, (mode.core + 1) * BLOCK)
            mode.rows[1, mode.own_member, place, :] = mode.grad_out[...]

    def take_grads(mode):
        behind(
            mode.members,
            mode.own_member,
            2,
            lambda: arrived(
                mode.rows.at[1, mode.own_member, :BLOCK], grad_recv.at[mode.own_member]
            ),
            lambda member: arrived(mode.rows.at[1, member], grad_recv.at[member]),
            lambda members: add_tiles(mode, 1, members),
        )

    per_mode(take_grads)
    grad_out = sum_at_owners(1)
    grad_out_bf = grad_out.astype(BF)
    grad_normed = grad_out
    for h in range(2):
        grad_hidden = dot_nt(grad_out_bf, tall[0, h])
        value, slope = silu_parts(gate_keep[h])
        grad_up = (grad_hidden * value).astype(BF)
        grad_gate = (grad_hidden * up_keep[h] * slope).astype(BF)
        grad_normed = grad_normed + (dot_nt(grad_gate, wide[0, h]) + dot_nt(grad_up, wide[1, h]))
    sums = sum_keep[...]
    scale_basket = rms_scale(sums)
    inner_basket = jnp.sum(basket_gain * grad_normed * sums, axis=1, keepdims=True)
    cubed_basket = scale_basket * scale_basket * scale_basket
    grad_sum = scale_basket * basket_gain * grad_normed - sums * cubed_basket * inner_basket / D
    send_blocks(1, grad_sum.astype(BF))

    def back_copy(mode, member):
        return remote(
            mode.item_out.at[1, pl.ds(2 * member, 2)],
            mode.back_in.at[mode.own_member],
            back_send,
            back_recv,
            mode.item_shard(member),
            mode.core,
        )

    def finish(mode):
        pick_all(mode, 1)

        def partials(members):
            totals = [dot(mode.spread[member], mode.picked[member]) for member in members]
            for member, total in zip(members, totals):
                mode.item_out[1, pl.ds(2 * member, 2)] = total.astype(BF).reshape(2, BLOCK, HALF)

        ahead(
            mode.members,
            mode.own_member,
            2,
            partials,
            lambda member: back_copy(mode, member).start(),
            lambda: None,
        )
        mode.back_in[mode.own_member] = mode.item_out[1, pl.ds(2 * mode.own_member, 2)]
        sent(mode.words_out.at[: mode.members - 1], words_send)
        sent(mode.rows.at[0, : mode.members - 1], rows_send)
        sent(mode.item_out.at[0, : 2 * mode.members - 1], item_send)
        for phase in range(2):
            sent(mode.owner_out.at[phase, : 2 * mode.columns - 1], owner_send.at[phase])
            sent(owner_in.at[phase, : PARTS - 1], block_send.at[phase])
        for part in range(2):
            sent(item_in.at[part, : PARTS - 1], grad_send.at[part])
        arrived(mode.back_in.at[: mode.members - 1], back_recv)
        for block in range(2):
            back = mode.back_in[0, block].astype(F32)
            for member in range(1, mode.members):
                back = back + mode.back_in[member, block].astype(F32)
            back_ref[block * BLOCK : (block + 1) * BLOCK, :] = back
        sent(mode.back_in.at[: mode.members - 1], back_send)

    per_mode(finish)

    for n in range(6):
        sibling_weight(n).wait_send()
    cot_copy().wait_send()


def local(
    item_rows,
    first_moment,
    second_moment,
    item_cot,
    tile_bits,
    tile_item,
    tile_dest,
    basket_gain,
    item_gain,
    gate_basket,
    up_basket,
    down_basket,
    gate_item,
    up_item,
    down_item,
):
    vmem = pl.BlockSpec(memory_space=pltpu.VMEM)
    smem = pl.BlockSpec(memory_space=pltpu.SMEM)
    anywhere = pl.BlockSpec(memory_space=pltpu.HBM)
    back_items = pl.pallas_call(
        kernel,
        out_shape=pltpu.VMEM((2 * BLOCK, HALF), F32),
        in_specs=[anywhere] * 3 + [smem, smem, vmem, vmem] + [anywhere] * 6,
        out_specs=vmem,
        scratch_shapes=[
            common_scratch(),
            mode_scratch(RING, PLANE),
            mode_scratch(PLANE, RING),
        ],
        compiler_params=pltpu.CompilerParams(
            collective_id=0, has_side_effects=True, vmem_limit_bytes=60 * 1024 * 1024
        ),
        name="layer",
    )(
        item_rows,
        item_cot,
        tile_bits,
        tile_item,
        tile_dest,
        basket_gain.reshape(1, D),
        item_gain.reshape(1, D),
        gate_basket,
        up_basket,
        down_basket,
        gate_item,
        up_item,
        down_item,
    )
    gradient = item_cot.astype(F32) + back_items
    new_first = BETA_FIRST * first_moment + (1.0 - BETA_FIRST) * gradient
    new_second = BETA_SECOND * second_moment + (1.0 - BETA_SECOND) * gradient * gradient
    new_rows = item_rows - LEARNING_RATE * new_first / (jnp.sqrt(new_second) + ADAM_EPSILON)
    return (new_rows, new_first, new_second)


def solution(mesh):
    split = P("shard", "mp")
    return jax.shard_map(
        local,
        mesh=mesh,
        in_specs=(
            split,
            split,
            split,
            split,
            P("shard", None, None),
            P("shard"),
            P("shard"),
            P(),
            P(),
            P(None, "mp"),
            P(None, "mp"),
            P("mp", None),
            P(None, "mp"),
            P(None, "mp"),
            P("mp", None),
        ),
        out_specs=(split, split, split),
        check_vma=False,
    )
```

```python
import jax
import jax.numpy as jnp
from jax import lax
from jax.experimental import pallas as pl
from jax.experimental.pallas import tpu as pltpu
from jax.sharding import PartitionSpec as P

D = 256
HALF = 128
BLOCK = 128
TILE_DEV = 16
RING = 8
PLANE = 16
PARTS = RING + PLANE
OWN = 64
HIDDEN = 1024

NORM_EPSILON = 1e-05
LEARNING_RATE = 0.01
BETA_FIRST = 0.9
BETA_SECOND = 0.99
ADAM_EPSILON = 1e-08

MESH = pl.DeviceIdType.MESH
BF = jnp.bfloat16
F32 = jnp.float32


def dot(a, b):
    return jnp.dot(a, b, preferred_element_type=F32)


def dot_nt(a, b):
    return lax.dot_general(a, b, (((1,), (1,)), ((), ())), preferred_element_type=F32)


def silu_parts(gate_values):
    sigmoid = jax.nn.sigmoid(gate_values)
    return (gate_values * sigmoid, sigmoid * (1.0 + gate_values * (1.0 - sigmoid)))


def rms_scale(values):
    return lax.rsqrt(jnp.mean(values * values, axis=-1, keepdims=True) + NORM_EPSILON)


def rows16(start, size):
    return pl.ds(pl.multiple_of(start, 16), size)


def mode_scratch(members, columns):
    wide = TILE_DEV * columns
    tiles = TILE_DEV * members
    slots = wide // 128 + 1
    return {
        "words_out": pltpu.VMEM((members, slots, 8, 128), jnp.int32),
        "words_in": pltpu.VMEM((members, slots, 8, 128), jnp.int32),
        "rows": pltpu.VMEM((2, members, 2 * BLOCK, HALF), BF),
        "spread": pltpu.VMEM((members, 2 * BLOCK, wide), BF),
        "collect": pltpu.VMEM((members, wide, 2 * BLOCK), BF),
        "select_cols": pltpu.VMEM((BLOCK, 2 * tiles), BF),
        "select_rows": pltpu.VMEM((tiles, BLOCK), BF),
        "tile_sums": pltpu.VMEM((columns, 2 * tiles, HALF), BF),
        "owner_out": pltpu.VMEM((2, 2 * columns, OWN, HALF), BF),
        "block_out": pltpu.VMEM((2, OWN, HALF), BF),
        "block_in": pltpu.VMEM((2, columns, BLOCK, HALF), BF),
        "picked": pltpu.VMEM((members, wide, HALF), BF),
        "item_out": pltpu.VMEM((2, 2 * members, BLOCK, HALF), BF),
        "back_in": pltpu.VMEM((members, 2, BLOCK, HALF), BF),
        "grad_out": pltpu.VMEM((BLOCK, HALF), BF),
    }


def common_scratch():
    dma = pltpu.SemaphoreType.DMA
    return {
        "wide": pltpu.VMEM((4, 2, D, HIDDEN), BF),
        "tall": pltpu.VMEM((2, 2, HIDDEN, D), BF),
        "cot_whole": pltpu.VMEM((2, BLOCK, HALF), BF),
        "gate_keep": pltpu.VMEM((2, OWN, HIDDEN), F32),
        "up_keep": pltpu.VMEM((2, OWN, HIDDEN), F32),
        "sum_keep": pltpu.VMEM((OWN, D), F32),
        "item_rows": pltpu.VMEM((2 * BLOCK, HALF), F32),
        "tile_bits": pltpu.VMEM((TILE_DEV, 8, 128), jnp.int32),
        "tile_item": pltpu.SMEM((TILE_DEV,), jnp.int32),
        "tile_dest": pltpu.SMEM((TILE_DEV,), jnp.int32),
        "basket_gain": pltpu.VMEM((1, D), F32),
        "item_gain": pltpu.VMEM((1, D), F32),
        "load_sem": dma((7,)),
        "weight_own": dma((2,)),
        "weight_send": dma,
        "weight_recv": dma((2,)),
        "cot_send": dma,
        "cot_recv": dma,
        "owner_in": pltpu.VMEM((2, PARTS, OWN, HALF), BF),
        "item_in": pltpu.VMEM((2, PARTS, BLOCK // 2, HALF), BF),
        "words_send": dma,
        "words_recv": dma,
        "rows_send": dma,
        "rows_recv": dma((PLANE // 2,)),
        "owner_send": dma((2,)),
        "owner_recv": dma((2,)),
        "block_send": dma((2,)),
        "block_recv": dma((2, PLANE // 4)),
        "item_send": dma,
        "item_recv": dma((2,)),
        "grad_send": dma((2,)),
        "grad_recv": dma((PLANE // 2,)),
        "back_send": dma,
        "back_recv": dma,
    }


class Mode:
    def __init__(self, core, refs, z, q):
        self.core = core
        self.members, self.columns = (RING, PLANE) if core == 0 else (PLANE, RING)
        self.own_member, self.own_column = (z, q) if core == 0 else (q, z)
        self.first = 0 if core == 0 else PLANE
        self.first_item = 0 if core == 0 else RING
        self.z, self.q = z, q
        self.__dict__.update(refs)

    def item_shard(self, member):
        return member * PLANE + self.q if self.core == 0 else self.z * PLANE + member

    def basket_shard(self, column):
        return self.z * PLANE + column if self.core == 0 else column * PLANE + self.q


def kernel(
    rows_hbm,
    cot_hbm,
    bits_hbm,
    item_hbm,
    dest_hbm,
    gain_b_hbm,
    gain_i_hbm,
    gate_b_ref,
    up_b_ref,
    down_b_ref,
    gate_i_ref,
    up_i_ref,
    down_i_ref,
    back_ref,
    common,
    ring_refs,
    plane_refs,
):
    shard = lax.axis_index("shard")
    m = lax.axis_index("mp")
    other = 1 - m
    z = lax.div(shard, PLANE)
    q = lax.rem(shard, PLANE)
    me = 2 * q + m
    modes = (Mode(0, ring_refs, z, q), Mode(1, plane_refs, z, q))
    wide, tall, cot_whole = common["wide"], common["tall"], common["cot_whole"]
    gate_keep, up_keep, sum_keep = common["gate_keep"], common["up_keep"], common["sum_keep"]
    rows_ref, bits_ref, load_sem = common["item_rows"], common["tile_bits"], common["load_sem"]
    weight_own, weight_send = common["weight_own"], common["weight_send"]
    weight_recv = common["weight_recv"]
    cot_send, cot_recv = common["cot_send"], common["cot_recv"]
    owner_in, item_in = common["owner_in"], common["item_in"]
    words_send, words_recv = common["words_send"], common["words_recv"]
    rows_send, rows_recv = common["rows_send"], common["rows_recv"]
    owner_send, owner_recv = common["owner_send"], common["owner_recv"]
    block_send, block_recv = common["block_send"], common["block_recv"]
    item_send, item_recv = common["item_send"], common["item_recv"]
    grad_send, grad_recv = common["grad_send"], common["grad_recv"]
    back_send, back_recv = common["back_send"], common["back_recv"]

    def remote(src, dst, send, recv, to_shard, to_core):
        return pltpu.make_async_remote_copy(
            src_ref=src,
            dst_ref=dst,
            send_sem=send,
            recv_sem=recv,
            device_id=(to_shard, to_core),
            device_id_type=MESH,
        )

    def arrived(ref, recv):
        remote(ref, ref, cot_send, recv, shard, other).wait_recv()

    def sent(ref, send):
        remote(ref, ref, send, cot_recv, shard, other).wait_send()

    def around(count, own, body):
        def step(n, carry):
            body(lax.rem(own + n, count))
            return carry

        lax.fori_loop(1, count, step, 0)

    def ahead(count, own, size, work, send, send_own):
        def group(n, last):
            places = [lax.rem(own + n * size + i + 1, count) for i in range(size)]
            work(places)
            for place in places[: size - 1] if last else places:
                send(place)
            if last:
                send_own()

        def step(n, carry):
            group(n, False)
            return carry

        lax.fori_loop(0, count // size - 1, step, 0)
        group(count // size - 1, True)

    def turn_at(count, own, place, size):
        return lax.div(lax.rem(place - own + count, count), size)

    def behind(count, own, size, wait_first, wait, work):
        def group(n, first):
            places = [lax.rem(own + count - n * size - i, count) for i in range(size)]
            if first:
                wait_first()
            else:
                wait(n)
            work(places)

        def step(n, carry):
            group(n, False)
            return carry

        group(0, True)
        lax.fori_loop(1, count // size, step, 0)

    def per_mode(body):
        for mode in modes:

            @pl.when(m == mode.core)
            def _(mode=mode):
                body(mode)

    weights = (
        (gate_b_ref, wide.at[0]),
        (up_b_ref, wide.at[1]),
        (down_b_ref, tall.at[0]),
        (gate_i_ref, wide.at[2]),
        (up_i_ref, wide.at[3]),
        (down_i_ref, tall.at[1]),
    )

    def own_weight(n):
        src, dst = weights[n]
        return pltpu.make_async_copy(src, dst.at[m], weight_own.at[n // 3])

    def sibling_weight(n):
        src, dst = weights[n]
        return remote(src, dst.at[m], weight_send, weight_recv.at[n // 3], shard, other)

    item_ref, dest_ref = common["tile_item"], common["tile_dest"]
    gain_b_ref, gain_i_ref = common["basket_gain"], common["item_gain"]
    small_loads = [
        pltpu.make_async_copy(src, dst, load_sem.at[3 + n])
        for n, (src, dst) in enumerate(
            (
                (item_hbm, item_ref),
                (dest_hbm, dest_ref),
                (gain_b_hbm, gain_b_ref),
                (gain_i_hbm, gain_i_ref),
            )
        )
    ]
    load_rows = pltpu.make_async_copy(rows_hbm, rows_ref, load_sem.at[0])
    load_bits = pltpu.make_async_copy(bits_hbm, bits_ref, load_sem.at[1])
    load_cot = pltpu.make_async_copy(
        cot_hbm.at[rows16(m * BLOCK, BLOCK)], cot_whole.at[m], load_sem.at[2]
    )
    barrier = pltpu.get_barrier_semaphore()

    def greet(to_shard, to_core):
        pl.semaphore_signal(
            barrier, inc=1, device_id=(to_shard, to_core), device_id_type=MESH
        )

    def greet_ring(z_to):
        for core in range(2):
            greet(z_to * PLANE + q, core)

    load_rows.start()
    load_bits.start()
    for load in small_loads:
        load.start()
    around(RING, z, greet_ring)
    around(2 * PLANE, me, lambda k: greet(z * PLANE + lax.div(k, 2), lax.rem(k, 2)))
    load_cot.start()
    for n in range(6):
        own_weight(n).start()

    sub = lax.broadcasted_iota(jnp.int32, (8, 128), 0)
    lane = lax.broadcasted_iota(jnp.int32, (8, 128), 1)

    def prepare(mode):
        mode.rows[0, mode.own_member] = rows_ref[...].astype(BF)
        columns = mode.columns
        per_slot = 128 // columns
        slots = TILE_DEV // per_slot
        if mode.core == 0:
            tiles = [bits_ref[t] for t in range(TILE_DEV)]
        else:
            left = lax.broadcasted_iota(jnp.int32, (128, 128), 0)
            right = lax.broadcasted_iota(jnp.int32, (128, 128), 1)
            order = jnp.where(
                (left % PLANE == right // columns) & (left // PLANE == right % columns), 1.0, 0.0
            ).astype(BF)
            words = bits_ref[...].reshape(128, 128)
            low = dot((words & 255).astype(F32).astype(BF), order)
            high = dot(jnp.right_shift(words, 8).astype(F32).astype(BF), order)
            words = (low + 256.0 * high).astype(jnp.int32).reshape(TILE_DEV, 8, 128)
            tiles = [words[t] for t in range(TILE_DEV)]
        group = lane // columns
        about = jnp.zeros((8, 128), jnp.int32)
        start = mode.own_member * TILE_DEV
        dest_sub = 2 + lax.div(start, 128)
        dest_lane = lax.rem(start, 128)
        for t in range(TILE_DEV):
            slot, place = t // per_slot, t % per_slot
            about = jnp.where((sub == slot) & (group == place), item_ref[t], about)
            about = jnp.where((sub == dest_sub) & (lane == dest_lane + t), dest_ref[t], about)
        for member in range(mode.members):
            for slot in range(slots):
                values = jnp.zeros((8, 128), jnp.int32)
                for place in range(per_slot):
                    turned = tiles[slot * per_slot + place]
                    shift = (columns * (place - member)) % 128
                    if shift:
                        turned = pltpu.roll(turned, shift, 1)
                    values = jnp.where(group == place, turned, values)
                mode.words_out[member, slot] = values
            mode.words_out[member, slots] = about
        mode.words_in[mode.own_member] = mode.words_out[mode.own_member]

    load_rows.wait()
    load_bits.wait()
    for load in small_loads:
        load.wait()
    per_mode(prepare)

    pl.semaphore_wait(barrier, 2 * PLANE - 1 + 2 * (RING - 1))

    def words_copy(mode, member):
        return remote(
            mode.words_out.at[member],
            mode.words_in.at[mode.own_member],
            words_send,
            words_recv,
            mode.item_shard(member),
            mode.core,
        )

    def rows_copy(mode, member):
        return remote(
            mode.rows.at[0, mode.own_member],
            mode.rows.at[0, mode.own_member],
            rows_send,
            rows_recv.at[turn_at(mode.members, mode.own_member, member, 2)],
            mode.item_shard(member),
            mode.core,
        )

    def start_rows(mode):
        around(mode.members, mode.own_member, lambda member: words_copy(mode, member).start())
        around(mode.members, mode.own_member, lambda member: rows_copy(mode, member).start())

    per_mode(start_rows)

    def cot_copy():
        return remote(
            cot_hbm.at[rows16(other * BLOCK, BLOCK)],
            cot_whole.at[m],
            cot_send,
            cot_recv,
            shard,
            other,
        )

    for n in range(3):
        sibling_weight(n).start()
    cot_copy().start()
    for n in range(3, 6):
        sibling_weight(n).start()

    def add_tiles(mode, phase, members):
        all_sums = [dot(mode.collect[member], mode.rows[phase, member]) for member in members]
        shape = (mode.columns, TILE_DEV, HALF)
        tiles = TILE_DEV * mode.members
        for member, sums in zip(members, all_sums):
            high = sums.astype(BF)
            low = (sums - high.astype(F32)).astype(BF)
            mode.tile_sums[:, rows16(member * TILE_DEV, TILE_DEV), :] = high.reshape(shape)
            mode.tile_sums[:, rows16(tiles + member * TILE_DEV, TILE_DEV), :] = low.reshape(shape)

    def turned(mode, tile_major, column_major):
        same = (tile_major // mode.columns == column_major % TILE_DEV) & (
            tile_major % mode.columns == column_major // TILE_DEV
        )
        return jnp.where(same, 1.0, 0.0).astype(BF)

    def finish_selection(mode):
        size = TILE_DEV * mode.columns
        left = lax.broadcasted_iota(jnp.int32, (size, size), 0)
        right = lax.broadcasted_iota(jnp.int32, (size, size), 1)
        to_columns = turned(mode, left, right)

        def turn_some(n, carry):
            mats = [dot(mode.spread[4 * n + i], to_columns).astype(BF) for i in range(4)]
            for i in range(4):
                mode.spread[4 * n + i] = mats[i]
            return carry

        lax.fori_loop(0, mode.members // 4, turn_some, 0)
        tiles = TILE_DEV * mode.members
        eye_left = lax.broadcasted_iota(jnp.int32, (tiles, tiles), 0)
        eye_right = lax.broadcasted_iota(jnp.int32, (tiles, tiles), 1)
        eye = jnp.where(eye_left == eye_right, 1.0, 0.0).astype(BF)
        mode.select_rows[...] = dot_nt(eye, mode.select_cols[:, :tiles]).astype(BF)

    def take_rows(mode):
        size = TILE_DEV * mode.columns
        slots = size // 128
        left = lax.broadcasted_iota(jnp.int32, (size, size), 0)
        right = lax.broadcasted_iota(jnp.int32, (size, size), 1)

        from_tiles = turned(mode, right, left)
        shifts = lax.broadcasted_iota(jnp.int32, (8, 16, 128), 1)

        def unpack(member):
            about = mode.words_in[member, slots]
            halves = []
            for slot in range(slots):
                packed = jnp.broadcast_to(mode.words_in[member, slot][:, None, :], (8, 16, 128))
                bits = (jnp.right_shift(packed, shifts) & 1).reshape(128, 128).astype(F32)
                halves.append((bits, jnp.broadcast_to(about[slot : slot + 1, :], (128, 128))))
            blocks = []
            for block in range(2):
                parts = [jnp.where(item == block, bits, 0.0) for bits, item in halves]
                blocks.append(parts[0] if slots == 1 else jnp.concatenate(parts, axis=1))
            mat = jnp.concatenate(blocks, axis=0).astype(BF)
            mode.spread[member] = mat
            mode.collect[member] = dot_nt(from_tiles, mat).astype(BF)

        def unpack_some(n, carry):
            for i in range(4):
                unpack(4 * n + i)
            return carry

        arrived(mode.words_in.at[: mode.members - 1], words_recv)
        lax.fori_loop(0, mode.members // 4, unpack_some, 0)

        tiles = TILE_DEV * mode.members
        about = mode.words_in[0, slots]
        for member in range(1, mode.members):
            about = about + mode.words_in[member, slots]
        all_dest = about[2:3, :]
        if tiles > 128:
            all_dest = jnp.concatenate([all_dest, about[3:4, :]], axis=1)
        block_of = lax.broadcasted_iota(jnp.int32, (BLOCK, tiles), 0)
        one_hot = jnp.where(block_of == all_dest, 1.0, 0.0).astype(BF)
        mode.select_cols[...] = jnp.concatenate([one_hot, one_hot], axis=1)
        behind(
            mode.members,
            mode.own_member,
            2,
            lambda: arrived(mode.rows.at[0, 0], rows_recv.at[0]),
            lambda n: arrived(mode.rows.at[0, :2], rows_recv.at[n]),
            lambda members: add_tiles(mode, 0, members),
        )

    per_mode(take_rows)

    def owner_copy(mode, phase, column, to_core):
        return remote(
            mode.owner_out.at[phase, 2 * column + to_core],
            owner_in.at[phase, mode.first + mode.own_column],
            owner_send.at[phase],
            owner_recv.at[phase],
            mode.basket_shard(column),
            to_core,
        )

    def send_sums(mode, phase):
        def column_sums(columns):
            for k in range(0, len(columns), 2):
                pair = jnp.concatenate([mode.tile_sums[c] for c in columns[k : k + 2]], axis=1)
                total = dot(mode.select_cols[...], pair).astype(BF)
                for i, column in enumerate(columns[k : k + 2]):
                    mode.owner_out[phase, pl.ds(2 * column, 2)] = total[
                        :, i * HALF : (i + 1) * HALF
                    ].reshape(2, OWN, HALF)

        def send(column):
            for to_core in range(2):
                owner_copy(mode, phase, column, to_core).start()

        def send_own():
            owner_copy(mode, phase, mode.own_column, 1 - mode.core).start()

        ahead(mode.columns, mode.own_column, 4, column_sums, send, send_own)
        owner_in[phase, mode.first + mode.own_column] = mode.owner_out[
            phase, 2 * mode.own_column + mode.core
        ]
        if phase == 0:
            finish_selection(mode)

    def sum_at_owners(phase):
        per_mode(lambda mode: send_sums(mode, phase))
        arrived(owner_in.at[phase, : PARTS - 1], owner_recv.at[phase])
        halves = []
        for mode in modes:
            total = owner_in[phase, mode.first].astype(F32)
            for column in range(1, mode.columns):
                total = total + owner_in[phase, mode.first + column].astype(F32)
            halves.append(total)
        return jnp.concatenate(halves, axis=1)

    def block_copy(mode, phase, column):
        return remote(
            mode.block_out.at[phase],
            mode.block_in.at[phase, mode.own_column, rows16(m * OWN, OWN)],
            block_send.at[phase],
            block_recv.at[phase, turn_at(mode.columns, mode.own_column, column, 4)],
            mode.basket_shard(column),
            mode.core,
        )

    def send_blocks(phase, values):
        for mode in modes:
            mode.block_out[phase] = values[:, mode.core * HALF : (mode.core + 1) * HALF]
        for mode in modes:

            @pl.when(m != mode.core)
            def _(mode=mode):
                block_copy(mode, phase, mode.own_column).start()

            around(
                mode.columns,
                mode.own_column,
                lambda column, mode=mode: block_copy(mode, phase, column).start(),
            )

            @pl.when(m == mode.core)
            def _(mode=mode):
                place = slice(mode.core * OWN, (mode.core + 1) * OWN)
                mode.block_in[phase, mode.own_column, place, :] = mode.block_out[phase]

    def pick_all(mode, phase):
        def pick(columns):
            for k in range(0, len(columns), 2):
                pair = jnp.concatenate(
                    [mode.block_in[phase, c] for c in columns[k : k + 2]], axis=1
                )
                chosen = dot(mode.select_rows[...], pair).astype(BF)
                for i, column in enumerate(columns[k : k + 2]):
                    mode.picked[:, rows16(column * TILE_DEV, TILE_DEV), :] = chosen[
                        :, i * HALF : (i + 1) * HALF
                    ].reshape(mode.members, TILE_DEV, HALF)

        behind(
            mode.columns,
            mode.own_column,
            4,
            lambda: arrived(owner_in.at[phase, :7], block_recv.at[phase, 0]),
            lambda n: arrived(mode.block_in.at[phase, :4], block_recv.at[phase, n]),
            pick,
        )

    basket_gain = gain_b_ref[...]
    item_gain = gain_i_ref[...]

    basket_sum = sum_at_owners(0)
    sum_keep[...] = basket_sum
    three = wide.at[:3, 0]
    pltpu.make_async_copy(three, three, weight_own.at[0]).wait()
    arrived(three, weight_recv.at[0])
    normed = basket_sum * rms_scale(basket_sum) * basket_gain
    normed_bf = normed.astype(BF)
    total = normed
    for h in range(2):
        gate_pre = dot(normed_bf, wide[0, h])
        up_pre = dot(normed_bf, wide[1, h])
        gate_keep[h] = gate_pre
        up_keep[h] = up_pre
        hidden = (gate_pre * jax.nn.sigmoid(gate_pre) * up_pre).astype(BF)
        total = total + dot(hidden, tall[0, h])
    send_blocks(0, total.astype(BF))

    def item_copy(mode, member, to_core, part):
        return remote(
            mode.item_out.at[0, 2 * member + to_core, pl.ds(part * BLOCK // 2, BLOCK // 2)],
            item_in.at[part, mode.first_item + mode.own_member],
            item_send,
            item_recv.at[part],
            mode.item_shard(member),
            to_core,
        )

    def send_items(mode):
        pick_all(mode, 0)

        def partials(members):
            totals = [dot(mode.spread[member], mode.picked[member]) for member in members]
            for member, total in zip(members, totals):
                mode.item_out[0, pl.ds(2 * member, 2)] = total.astype(BF).reshape(2, BLOCK, HALF)

        def send(member):
            for to_core in range(2):
                item_copy(mode, member, to_core, 0).start()

        def send_own():
            item_copy(mode, mode.own_member, 1 - mode.core, 0).start()

        def send_rest(member):
            for to_core in range(2):
                item_copy(mode, member, to_core, 1).start()

        ahead(mode.members, mode.own_member, 2, partials, send, send_own)
        around(mode.members, mode.own_member, send_rest)
        item_copy(mode, mode.own_member, 1 - mode.core, 1).start()
        own_out = mode.item_out[0, 2 * mode.own_member + mode.core]
        for part in range(2):
            rows = slice(part * BLOCK // 2, (part + 1) * BLOCK // 2)
            item_in[part, mode.first_item + mode.own_member] = own_out[rows, :]

    per_mode(send_items)

    pltpu.make_async_copy(three, three, weight_own.at[1]).wait()
    arrived(three, weight_recv.at[1])
    arrived(cot_whole.at[other], cot_recv)
    load_cot.wait()
    cot_full = jnp.concatenate([cot_whole[0], cot_whole[1]], axis=1)

    def item_layer(part):
        arrived(item_in.at[part, : PARTS - 1], item_recv.at[part])
        halves = []
        for mode in modes:
            summed = item_in[part, mode.first_item].astype(F32)
            for member in range(1, mode.members):
                summed = summed + item_in[part, mode.first_item + member].astype(F32)
            halves.append(summed)
        message = jnp.concatenate(halves, axis=1)
        cot = cot_full[part * BLOCK // 2 : (part + 1) * BLOCK // 2, :]
        scale_item = rms_scale(message)
        query = (message * scale_item * item_gain).astype(BF)
        grad_query = jnp.zeros((BLOCK // 2, D), F32)
        for h in range(2):
            gate_pre = dot(query, wide[2, h])
            up_pre = dot(query, wide[3, h])
            grad_hidden = dot_nt(cot, tall[1, h])
            value, slope = silu_parts(gate_pre)
            grad_up = (grad_hidden * value).astype(BF)
            grad_gate = (grad_hidden * up_pre * slope).astype(BF)
            grad_query = grad_query + dot_nt(grad_gate, wide[2, h]) + dot_nt(grad_up, wide[3, h])
        inner = jnp.sum(item_gain * grad_query * message, axis=1, keepdims=True)
        cubed = scale_item * scale_item * scale_item
        return (scale_item * item_gain * grad_query - message * cubed * inner / D).astype(BF)

    def grad_copy(mode, member, part):
        return remote(
            mode.grad_out.at[pl.ds(part * BLOCK // 2, BLOCK // 2)],
            mode.rows.at[1, mode.own_member, rows16(m * BLOCK + part * BLOCK // 2, BLOCK // 2)],
            grad_send.at[part],
            grad_recv.at[turn_at(mode.members, mode.own_member, member, 2)],
            mode.item_shard(member),
            mode.core,
        )

    for part in range(2):
        grad_message = item_layer(part)
        for mode in modes:
            rows = slice(part * BLOCK // 2, (part + 1) * BLOCK // 2)
            mode.grad_out[rows, :] = grad_message[:, mode.core * HALF : (mode.core + 1) * HALF]
        for mode in modes:

            @pl.when(m != mode.core)
            def _(mode=mode, part=part):
                grad_copy(mode, mode.own_member, part).start()

            around(
                mode.members,
                mode.own_member,
                lambda member, mode=mode, part=part: grad_copy(mode, member, part).start(),
            )
    for mode in modes:

        @pl.when(m == mode.core)
        def _(mode=mode):
            place = slice(mode.core * BLOCK, (mode.core + 1) * BLOCK)
            mode.rows[1, mode.own_member, place, :] = mode.grad_out[...]

    def take_grads(mode):
        behind(
            mode.members,
            mode.own_member,
            2,
            lambda: arrived(mode.item_out.at[0, :3], grad_recv.at[0]),
            lambda n: arrived(mode.rows.at[1, :2], grad_recv.at[n]),
            lambda members: add_tiles(mode, 1, members),
        )

    per_mode(take_grads)
    grad_out = sum_at_owners(1)
    grad_out_bf = grad_out.astype(BF)
    grad_normed = grad_out
    for h in range(2):
        grad_hidden = dot_nt(grad_out_bf, tall[0, h])
        value, slope = silu_parts(gate_keep[h])
        grad_up = (grad_hidden * value).astype(BF)
        grad_gate = (grad_hidden * up_keep[h] * slope).astype(BF)
        grad_normed = grad_normed + (dot_nt(grad_gate, wide[0, h]) + dot_nt(grad_up, wide[1, h]))
    sums = sum_keep[...]
    scale_basket = rms_scale(sums)
    inner_basket = jnp.sum(basket_gain * grad_normed * sums, axis=1, keepdims=True)
    cubed_basket = scale_basket * scale_basket * scale_basket
    grad_sum = scale_basket * basket_gain * grad_normed - sums * cubed_basket * inner_basket / D
    send_blocks(1, grad_sum.astype(BF))

    def back_copy(mode, member):
        return remote(
            mode.item_out.at[1, pl.ds(2 * member, 2)],
            mode.back_in.at[mode.own_member],
            back_send,
            back_recv,
            mode.item_shard(member),
            mode.core,
        )

    def finish(mode):
        pick_all(mode, 1)

        def partials(members):
            totals = [dot(mode.spread[member], mode.picked[member]) for member in members]
            for member, total in zip(members, totals):
                mode.item_out[1, pl.ds(2 * member, 2)] = total.astype(BF).reshape(2, BLOCK, HALF)

        ahead(
            mode.members,
            mode.own_member,
            2,
            partials,
            lambda member: back_copy(mode, member).start(),
            lambda: None,
        )
        mode.back_in[mode.own_member] = mode.item_out[1, pl.ds(2 * mode.own_member, 2)]
        sent(mode.words_out.at[: mode.members - 1], words_send)
        sent(mode.rows.at[0, : mode.members - 1], rows_send)
        sent(mode.item_out.at[0, : 2 * mode.members - 1], item_send)
        for phase in range(2):
            sent(mode.owner_out.at[phase, : 2 * mode.columns - 1], owner_send.at[phase])
            sent(owner_in.at[phase, : PARTS - 1], block_send.at[phase])
        for part in range(2):
            sent(item_in.at[part, : PARTS - 1], grad_send.at[part])
        arrived(mode.back_in.at[: mode.members - 1], back_recv)
        for block in range(2):
            back = mode.back_in[0, block].astype(F32)
            for member in range(1, mode.members):
                back = back + mode.back_in[member, block].astype(F32)
            back_ref[block * BLOCK : (block + 1) * BLOCK, :] = back
        sent(mode.back_in.at[: mode.members - 1], back_send)

    per_mode(finish)

    sent(wide.at[:3], weight_send)
    cot_copy().wait_send()


def local(
    item_rows,
    first_moment,
    second_moment,
    item_cot,
    tile_bits,
    tile_item,
    tile_dest,
    basket_gain,
    item_gain,
    gate_basket,
    up_basket,
    down_basket,
    gate_item,
    up_item,
    down_item,
):
    vmem = pl.BlockSpec(memory_space=pltpu.VMEM)
    anywhere = pl.BlockSpec(memory_space=pltpu.HBM)
    back_items = pl.pallas_call(
        kernel,
        out_shape=pltpu.VMEM((2 * BLOCK, HALF), F32),
        in_specs=[anywhere] * 13,
        out_specs=vmem,
        scratch_shapes=[
            common_scratch(),
            mode_scratch(RING, PLANE),
            mode_scratch(PLANE, RING),
        ],
        compiler_params=pltpu.CompilerParams(
            collective_id=0, has_side_effects=True, vmem_limit_bytes=60 * 1024 * 1024
        ),
        name="layer",
    )(
        item_rows,
        item_cot,
        tile_bits,
        tile_item,
        tile_dest,
        basket_gain.reshape(1, D),
        item_gain.reshape(1, D),
        gate_basket,
        up_basket,
        down_basket,
        gate_item,
        up_item,
        down_item,
    )
    gradient = item_cot.astype(F32) + back_items
    new_first = BETA_FIRST * first_moment + (1.0 - BETA_FIRST) * gradient
    new_second = BETA_SECOND * second_moment + (1.0 - BETA_SECOND) * gradient * gradient
    new_rows = item_rows - LEARNING_RATE * new_first / (jnp.sqrt(new_second) + ADAM_EPSILON)
    return (new_rows, new_first, new_second)


def solution(mesh):
    split = P("shard", "mp")
    return jax.shard_map(
        local,
        mesh=mesh,
        in_specs=(
            split,
            split,
            split,
            split,
            P("shard", None, None),
            P("shard"),
            P("shard"),
            P(),
            P(),
            P(None, "mp"),
            P(None, "mp"),
            P("mp", None),
            P(None, "mp"),
            P(None, "mp"),
            P("mp", None),
        ),
        out_specs=(split, split, split),
        check_vma=False,
    )
```

```python
import jax
import jax.numpy as jnp
from jax import lax
from jax.experimental import pallas as pl
from jax.experimental.pallas import tpu as pltpu
from jax.sharding import PartitionSpec as P

D = 256
HALF = 128
BLOCK = 128
TILE_DEV = 16
RING = 8
PLANE = 16
PARTS = RING + PLANE
OWN = 64
PART = OWN // 2
HIDDEN = 1024

NORM_EPSILON = 1e-05
LEARNING_RATE = 0.01
BETA_FIRST = 0.9
BETA_SECOND = 0.99
ADAM_EPSILON = 1e-08

MESH = pl.DeviceIdType.MESH
BF = jnp.bfloat16
F32 = jnp.float32


def dot(a, b):
    return jnp.dot(a, b, preferred_element_type=F32)


def dot_nt(a, b):
    return lax.dot_general(a, b, (((1,), (1,)), ((), ())), preferred_element_type=F32)


def silu_parts(gate_values):
    sigmoid = jax.nn.sigmoid(gate_values)
    return (gate_values * sigmoid, sigmoid * (1.0 + gate_values * (1.0 - sigmoid)))


def rms_scale(values):
    return lax.rsqrt(jnp.mean(values * values, axis=-1, keepdims=True) + NORM_EPSILON)


def rows16(start, size):
    return pl.ds(pl.multiple_of(start, 16), size)


def mode_scratch(members, columns):
    wide = TILE_DEV * columns
    tiles = TILE_DEV * members
    slots = wide // 128 + 1
    return {
        "words_out": pltpu.VMEM((members, slots, 8, 128), jnp.int32),
        "words_in": pltpu.VMEM((members, slots, 8, 128), jnp.int32),
        "rows": pltpu.VMEM((2, members, 2 * BLOCK, HALF), BF),
        "spread": pltpu.VMEM((members, 2 * BLOCK, wide), BF),
        "collect": pltpu.VMEM((members, wide, 2 * BLOCK), BF),
        "select_cols": pltpu.VMEM((BLOCK, 2 * tiles), BF),
        "select_rows": pltpu.VMEM((tiles, BLOCK), BF),
        "tile_sums": pltpu.VMEM((columns, 2 * tiles, HALF), BF),
        "owner_out": pltpu.VMEM((2, 2 * columns, OWN, HALF), BF),
        "block_out": pltpu.VMEM((2, OWN, HALF), BF),
        "block_in": pltpu.VMEM((2, columns, BLOCK, HALF), BF),
        "picked": pltpu.VMEM((members, wide, HALF), BF),
        "item_out": pltpu.VMEM((2, 2 * members, BLOCK, HALF), BF),
        "back_in": pltpu.VMEM((members, 2, BLOCK, HALF), BF),
        "grad_out": pltpu.VMEM((BLOCK, HALF), BF),
    }


def common_scratch():
    dma = pltpu.SemaphoreType.DMA
    return {
        "wide": pltpu.VMEM((4, 2, D, HIDDEN), BF),
        "tall": pltpu.VMEM((2, 2, HIDDEN, D), BF),
        "cot_whole": pltpu.VMEM((2, BLOCK, HALF), BF),
        "gate_keep": pltpu.VMEM((2, 2, PART, HIDDEN), F32),
        "up_keep": pltpu.VMEM((2, 2, PART, HIDDEN), F32),
        "sum_keep": pltpu.VMEM((2, PART, D), F32),
        "item_rows": pltpu.VMEM((2 * BLOCK, HALF), F32),
        "tile_bits": pltpu.VMEM((TILE_DEV, 8, 128), jnp.int32),
        "tile_item": pltpu.SMEM((TILE_DEV,), jnp.int32),
        "tile_dest": pltpu.SMEM((TILE_DEV,), jnp.int32),
        "basket_gain": pltpu.VMEM((1, D), F32),
        "item_gain": pltpu.VMEM((1, D), F32),
        "load_sem": dma((7,)),
        "weight_own": dma((2,)),
        "weight_send": dma,
        "weight_recv": dma((2,)),
        "cot_send": dma,
        "cot_recv": dma,
        "owner_in": pltpu.VMEM((2, 2, PARTS, PART, HALF), BF),
        "item_in": pltpu.VMEM((2, PARTS, BLOCK // 2, HALF), BF),
        "words_send": dma,
        "words_recv": dma,
        "rows_send": dma,
        "rows_recv": dma((PLANE // 2,)),
        "owner_send": dma((2,)),
        "owner_recv": dma((2, 2)),
        "block_send": dma((2, 2)),
        "block_recv": dma((2, PLANE // 4)),
        "item_send": dma,
        "item_recv": dma((2,)),
        "grad_send": dma((2,)),
        "grad_recv": dma((PLANE // 2,)),
        "back_send": dma,
        "back_recv": dma,
    }


class Mode:
    def __init__(self, core, refs, z, q):
        self.core = core
        self.members, self.columns = (RING, PLANE) if core == 0 else (PLANE, RING)
        self.own_member, self.own_column = (z, q) if core == 0 else (q, z)
        self.first = 0 if core == 0 else PLANE
        self.first_item = 0 if core == 0 else RING
        self.z, self.q = z, q
        self.__dict__.update(refs)

    def item_shard(self, member):
        return member * PLANE + self.q if self.core == 0 else self.z * PLANE + member

    def basket_shard(self, column):
        return self.z * PLANE + column if self.core == 0 else column * PLANE + self.q


def kernel(
    rows_hbm,
    cot_hbm,
    bits_hbm,
    item_hbm,
    dest_hbm,
    gain_b_hbm,
    gain_i_hbm,
    gate_b_ref,
    up_b_ref,
    down_b_ref,
    gate_i_ref,
    up_i_ref,
    down_i_ref,
    back_ref,
    common,
    ring_refs,
    plane_refs,
):
    shard = lax.axis_index("shard")
    m = lax.axis_index("mp")
    other = 1 - m
    z = lax.div(shard, PLANE)
    q = lax.rem(shard, PLANE)
    me = 2 * q + m
    modes = (Mode(0, ring_refs, z, q), Mode(1, plane_refs, z, q))
    wide, tall, cot_whole = common["wide"], common["tall"], common["cot_whole"]
    gate_keep, up_keep, sum_keep = common["gate_keep"], common["up_keep"], common["sum_keep"]
    rows_ref, bits_ref, load_sem = common["item_rows"], common["tile_bits"], common["load_sem"]
    weight_own, weight_send = common["weight_own"], common["weight_send"]
    weight_recv = common["weight_recv"]
    cot_send, cot_recv = common["cot_send"], common["cot_recv"]
    owner_in, item_in = common["owner_in"], common["item_in"]
    words_send, words_recv = common["words_send"], common["words_recv"]
    rows_send, rows_recv = common["rows_send"], common["rows_recv"]
    owner_send, owner_recv = common["owner_send"], common["owner_recv"]
    block_send, block_recv = common["block_send"], common["block_recv"]
    item_send, item_recv = common["item_send"], common["item_recv"]
    grad_send, grad_recv = common["grad_send"], common["grad_recv"]
    back_send, back_recv = common["back_send"], common["back_recv"]

    def remote(src, dst, send, recv, to_shard, to_core):
        return pltpu.make_async_remote_copy(
            src_ref=src,
            dst_ref=dst,
            send_sem=send,
            recv_sem=recv,
            device_id=(to_shard, to_core),
            device_id_type=MESH,
        )

    def arrived(ref, recv):
        remote(ref, ref, cot_send, recv, shard, other).wait_recv()

    def sent(ref, send):
        remote(ref, ref, send, cot_recv, shard, other).wait_send()

    def around(count, own, body):
        def step(n, carry):
            body(lax.rem(own + n, count))
            return carry

        lax.fori_loop(1, count, step, 0)

    def ahead(count, own, size, work, send, send_own):
        def group(n, last):
            places = [lax.rem(own + n * size + i + 1, count) for i in range(size)]
            work(places)
            for place in places[: size - 1] if last else places:
                send(place)
            if last:
                send_own()

        def step(n, carry):
            group(n, False)
            return carry

        lax.fori_loop(0, count // size - 1, step, 0)
        group(count // size - 1, True)

    def turn_at(count, own, place, size):
        return lax.div(lax.rem(place - own + count, count), size)

    def behind(count, own, size, wait_first, wait, work):
        def group(n, first):
            places = [lax.rem(own + count - n * size - i, count) for i in range(size)]
            if first:
                wait_first()
            else:
                wait(n)
            work(places)

        def step(n, carry):
            group(n, False)
            return carry

        group(0, True)
        lax.fori_loop(1, count // size, step, 0)

    def per_mode(body):
        for mode in modes:

            @pl.when(m == mode.core)
            def _(mode=mode):
                body(mode)

    weights = (
        (gate_b_ref, wide.at[0]),
        (up_b_ref, wide.at[1]),
        (down_b_ref, tall.at[0]),
        (gate_i_ref, wide.at[2]),
        (up_i_ref, wide.at[3]),
        (down_i_ref, tall.at[1]),
    )

    def own_weight(n):
        src, dst = weights[n]
        return pltpu.make_async_copy(src, dst.at[m], weight_own.at[n // 3])

    def sibling_weight(n):
        src, dst = weights[n]
        return remote(src, dst.at[m], weight_send, weight_recv.at[n // 3], shard, other)

    item_ref, dest_ref = common["tile_item"], common["tile_dest"]
    gain_b_ref, gain_i_ref = common["basket_gain"], common["item_gain"]
    small_loads = [
        pltpu.make_async_copy(src, dst, load_sem.at[3 + n])
        for n, (src, dst) in enumerate(
            (
                (item_hbm, item_ref),
                (dest_hbm, dest_ref),
                (gain_b_hbm, gain_b_ref),
                (gain_i_hbm, gain_i_ref),
            )
        )
    ]
    load_rows = pltpu.make_async_copy(rows_hbm, rows_ref, load_sem.at[0])
    load_bits = pltpu.make_async_copy(bits_hbm, bits_ref, load_sem.at[1])
    load_cot = pltpu.make_async_copy(
        cot_hbm.at[rows16(m * BLOCK, BLOCK)], cot_whole.at[m], load_sem.at[2]
    )
    barrier = pltpu.get_barrier_semaphore()

    def greet(to_shard, to_core):
        pl.semaphore_signal(
            barrier, inc=1, device_id=(to_shard, to_core), device_id_type=MESH
        )

    def greet_ring(z_to):
        for core in range(2):
            greet(z_to * PLANE + q, core)

    load_rows.start()
    load_bits.start()
    for load in small_loads:
        load.start()
    around(RING, z, greet_ring)
    around(2 * PLANE, me, lambda k: greet(z * PLANE + lax.div(k, 2), lax.rem(k, 2)))
    load_cot.start()
    for n in range(6):
        own_weight(n).start()

    sub = lax.broadcasted_iota(jnp.int32, (8, 128), 0)
    lane = lax.broadcasted_iota(jnp.int32, (8, 128), 1)

    def prepare(mode):
        mode.rows[0, mode.own_member] = rows_ref[...].astype(BF)
        columns = mode.columns
        per_slot = 128 // columns
        slots = TILE_DEV // per_slot
        if mode.core == 0:
            tiles = [bits_ref[t] for t in range(TILE_DEV)]
        else:
            left = lax.broadcasted_iota(jnp.int32, (128, 128), 0)
            right = lax.broadcasted_iota(jnp.int32, (128, 128), 1)
            order = jnp.where(
                (left % PLANE == right // columns) & (left // PLANE == right % columns), 1.0, 0.0
            ).astype(BF)
            words = bits_ref[...].reshape(128, 128)
            low = dot((words & 255).astype(F32).astype(BF), order)
            high = dot(jnp.right_shift(words, 8).astype(F32).astype(BF), order)
            words = (low + 256.0 * high).astype(jnp.int32).reshape(TILE_DEV, 8, 128)
            tiles = [words[t] for t in range(TILE_DEV)]
        group = lane // columns
        about = jnp.zeros((8, 128), jnp.int32)
        start = mode.own_member * TILE_DEV
        dest_sub = 2 + lax.div(start, 128)
        dest_lane = lax.rem(start, 128)
        for t in range(TILE_DEV):
            slot, place = t // per_slot, t % per_slot
            about = jnp.where((sub == slot) & (group == place), item_ref[t], about)
            about = jnp.where((sub == dest_sub) & (lane == dest_lane + t), dest_ref[t], about)
        for member in range(mode.members):
            for slot in range(slots):
                values = jnp.zeros((8, 128), jnp.int32)
                for place in range(per_slot):
                    turned = tiles[slot * per_slot + place]
                    shift = (columns * (place - member)) % 128
                    if shift:
                        turned = pltpu.roll(turned, shift, 1)
                    values = jnp.where(group == place, turned, values)
                mode.words_out[member, slot] = values
            mode.words_out[member, slots] = about
        mode.words_in[mode.own_member] = mode.words_out[mode.own_member]

    load_rows.wait()
    load_bits.wait()
    for load in small_loads:
        load.wait()
    per_mode(prepare)

    pl.semaphore_wait(barrier, 2 * PLANE - 1 + 2 * (RING - 1))

    def words_copy(mode, member):
        return remote(
            mode.words_out.at[member],
            mode.words_in.at[mode.own_member],
            words_send,
            words_recv,
            mode.item_shard(member),
            mode.core,
        )

    def rows_copy(mode, member):
        return remote(
            mode.rows.at[0, mode.own_member],
            mode.rows.at[0, mode.own_member],
            rows_send,
            rows_recv.at[turn_at(mode.members, mode.own_member, member, 2)],
            mode.item_shard(member),
            mode.core,
        )

    def start_rows(mode):
        around(mode.members, mode.own_member, lambda member: words_copy(mode, member).start())
        around(mode.members, mode.own_member, lambda member: rows_copy(mode, member).start())

    per_mode(start_rows)

    def cot_copy():
        return remote(
            cot_hbm.at[rows16(other * BLOCK, BLOCK)],
            cot_whole.at[m],
            cot_send,
            cot_recv,
            shard,
            other,
        )

    for n in range(3):
        sibling_weight(n).start()
    cot_copy().start()
    for n in range(3, 6):
        sibling_weight(n).start()

    def add_tiles(mode, phase, members):
        all_sums = [dot(mode.collect[member], mode.rows[phase, member]) for member in members]
        shape = (mode.columns, TILE_DEV, HALF)
        tiles = TILE_DEV * mode.members
        for member, sums in zip(members, all_sums):
            high = sums.astype(BF)
            low = (sums - high.astype(F32)).astype(BF)
            mode.tile_sums[:, rows16(member * TILE_DEV, TILE_DEV), :] = high.reshape(shape)
            mode.tile_sums[:, rows16(tiles + member * TILE_DEV, TILE_DEV), :] = low.reshape(shape)

    def turned(mode, tile_major, column_major):
        same = (tile_major // mode.columns == column_major % TILE_DEV) & (
            tile_major % mode.columns == column_major // TILE_DEV
        )
        return jnp.where(same, 1.0, 0.0).astype(BF)

    def finish_selection(mode):
        size = TILE_DEV * mode.columns
        left = lax.broadcasted_iota(jnp.int32, (size, size), 0)
        right = lax.broadcasted_iota(jnp.int32, (size, size), 1)
        to_columns = turned(mode, left, right)

        def turn_some(n, carry):
            mats = [dot(mode.spread[4 * n + i], to_columns).astype(BF) for i in range(4)]
            for i in range(4):
                mode.spread[4 * n + i] = mats[i]
            return carry

        lax.fori_loop(0, mode.members // 4, turn_some, 0)
        tiles = TILE_DEV * mode.members
        eye_left = lax.broadcasted_iota(jnp.int32, (tiles, tiles), 0)
        eye_right = lax.broadcasted_iota(jnp.int32, (tiles, tiles), 1)
        eye = jnp.where(eye_left == eye_right, 1.0, 0.0).astype(BF)
        mode.select_rows[...] = dot_nt(eye, mode.select_cols[:, :tiles]).astype(BF)

    def take_rows(mode):
        size = TILE_DEV * mode.columns
        slots = size // 128
        left = lax.broadcasted_iota(jnp.int32, (size, size), 0)
        right = lax.broadcasted_iota(jnp.int32, (size, size), 1)

        from_tiles = turned(mode, right, left)
        shifts = lax.broadcasted_iota(jnp.int32, (8, 16, 128), 1)

        def unpack(member):
            about = mode.words_in[member, slots]
            halves = []
            for slot in range(slots):
                packed = jnp.broadcast_to(mode.words_in[member, slot][:, None, :], (8, 16, 128))
                bits = (jnp.right_shift(packed, shifts) & 1).reshape(128, 128).astype(F32)
                halves.append((bits, jnp.broadcast_to(about[slot : slot + 1, :], (128, 128))))
            blocks = []
            for block in range(2):
                parts = [jnp.where(item == block, bits, 0.0) for bits, item in halves]
                blocks.append(parts[0] if slots == 1 else jnp.concatenate(parts, axis=1))
            mat = jnp.concatenate(blocks, axis=0).astype(BF)
            mode.spread[member] = mat
            mode.collect[member] = dot_nt(from_tiles, mat).astype(BF)

        def unpack_some(n, carry):
            for i in range(4):
                unpack(4 * n + i)
            return carry

        arrived(mode.words_in.at[: mode.members - 1], words_recv)
        lax.fori_loop(0, mode.members // 4, unpack_some, 0)

        tiles = TILE_DEV * mode.members
        about = mode.words_in[0, slots]
        for member in range(1, mode.members):
            about = about + mode.words_in[member, slots]
        all_dest = about[2:3, :]
        if tiles > 128:
            all_dest = jnp.concatenate([all_dest, about[3:4, :]], axis=1)
        block_of = lax.broadcasted_iota(jnp.int32, (BLOCK, tiles), 0)
        one_hot = jnp.where(block_of == all_dest, 1.0, 0.0).astype(BF)
        mode.select_cols[...] = jnp.concatenate([one_hot, one_hot], axis=1)
        behind(
            mode.members,
            mode.own_member,
            2,
            lambda: arrived(mode.rows.at[0, 0], rows_recv.at[0]),
            lambda n: arrived(mode.rows.at[0, :2], rows_recv.at[n]),
            lambda members: add_tiles(mode, 0, members),
        )

    per_mode(take_rows)

    def owner_copy(mode, phase, column, to_core, part):
        return remote(
            mode.owner_out.at[phase, 2 * column + to_core, pl.ds(part * PART, PART)],
            owner_in.at[phase, part, mode.first + mode.own_column],
            owner_send.at[phase],
            owner_recv.at[phase, part],
            mode.basket_shard(column),
            to_core,
        )

    def send_sums(mode, phase):
        def column_sums(columns):
            for k in range(0, len(columns), 2):
                pair = jnp.concatenate([mode.tile_sums[c] for c in columns[k : k + 2]], axis=1)
                total = dot(mode.select_cols[...], pair).astype(BF)
                for i, column in enumerate(columns[k : k + 2]):
                    mode.owner_out[phase, pl.ds(2 * column, 2)] = total[
                        :, i * HALF : (i + 1) * HALF
                    ].reshape(2, OWN, HALF)

        def send(column):
            for to_core in range(2):
                owner_copy(mode, phase, column, to_core, 0).start()

        def send_own():
            owner_copy(mode, phase, mode.own_column, 1 - mode.core, 0).start()

        def send_rest(column):
            for to_core in range(2):
                owner_copy(mode, phase, column, to_core, 1).start()

        ahead(mode.columns, mode.own_column, 4, column_sums, send, send_own)
        around(mode.columns, mode.own_column, send_rest)
        owner_copy(mode, phase, mode.own_column, 1 - mode.core, 1).start()
        own_out = mode.owner_out[phase, 2 * mode.own_column + mode.core]
        for part in range(2):
            rows = slice(part * PART, (part + 1) * PART)
            owner_in[phase, part, mode.first + mode.own_column] = own_out[rows, :]
        if phase == 0:
            finish_selection(mode)

    def sum_at_owners(phase, part):
        arrived(owner_in.at[phase, part, : PARTS - 1], owner_recv.at[phase, part])
        halves = []
        for mode in modes:
            total = owner_in[phase, part, mode.first].astype(F32)
            for column in range(1, mode.columns):
                total = total + owner_in[phase, part, mode.first + column].astype(F32)
            halves.append(total)
        return jnp.concatenate(halves, axis=1)

    def block_copy(mode, phase, column, part):
        return remote(
            mode.block_out.at[phase, pl.ds(part * PART, PART)],
            mode.block_in.at[phase, mode.own_column, rows16(m * OWN + part * PART, PART)],
            block_send.at[phase, part],
            block_recv.at[phase, turn_at(mode.columns, mode.own_column, column, 4)],
            mode.basket_shard(column),
            mode.core,
        )

    def send_blocks(phase, part, values):
        for mode in modes:
            rows = slice(part * PART, (part + 1) * PART)
            mode.block_out[phase, rows, :] = values[:, mode.core * HALF : (mode.core + 1) * HALF]
        for mode in modes:

            @pl.when(m != mode.core)
            def _(mode=mode):
                block_copy(mode, phase, mode.own_column, part).start()

            around(
                mode.columns,
                mode.own_column,
                lambda column, mode=mode: block_copy(mode, phase, column, part).start(),
            )

            @pl.when(m == mode.core)
            def _(mode=mode):
                start = mode.core * OWN + part * PART
                mode.block_in[phase, mode.own_column, start : start + PART, :] = mode.block_out[
                    phase, part * PART : (part + 1) * PART
                ]

    def pick_all(mode, phase):
        def pick(columns):
            for k in range(0, len(columns), 2):
                pair = jnp.concatenate(
                    [mode.block_in[phase, c] for c in columns[k : k + 2]], axis=1
                )
                chosen = dot(mode.select_rows[...], pair).astype(BF)
                for i, column in enumerate(columns[k : k + 2]):
                    mode.picked[:, rows16(column * TILE_DEV, TILE_DEV), :] = chosen[
                        :, i * HALF : (i + 1) * HALF
                    ].reshape(mode.members, TILE_DEV, HALF)

        behind(
            mode.columns,
            mode.own_column,
            4,
            lambda: arrived(owner_in.at[phase, 0, :14], block_recv.at[phase, 0]),
            lambda n: arrived(mode.block_in.at[phase, :4], block_recv.at[phase, n]),
            pick,
        )

    basket_gain = gain_b_ref[...]
    item_gain = gain_i_ref[...]

    three = wide.at[:3, 0]
    per_mode(lambda mode: send_sums(mode, 0))

    def basket_layer(part):
        basket_sum = sum_at_owners(0, part)
        sum_keep[part] = basket_sum
        if part == 0:
            pltpu.make_async_copy(three, three, weight_own.at[0]).wait()
            arrived(three, weight_recv.at[0])
        normed = basket_sum * rms_scale(basket_sum) * basket_gain
        normed_bf = normed.astype(BF)
        total = normed
        for h in range(2):
            gate_pre = dot(normed_bf, wide[0, h])
            up_pre = dot(normed_bf, wide[1, h])
            gate_keep[part, h] = gate_pre
            up_keep[part, h] = up_pre
            hidden = (gate_pre * jax.nn.sigmoid(gate_pre) * up_pre).astype(BF)
            total = total + dot(hidden, tall[0, h])
        send_blocks(0, part, total.astype(BF))

    for part in range(2):
        basket_layer(part)

    def item_copy(mode, member, to_core, part):
        return remote(
            mode.item_out.at[0, 2 * member + to_core, pl.ds(part * BLOCK // 2, BLOCK // 2)],
            item_in.at[part, mode.first_item + mode.own_member],
            item_send,
            item_recv.at[part],
            mode.item_shard(member),
            to_core,
        )

    def send_items(mode):
        pick_all(mode, 0)

        def partials(members):
            totals = [dot(mode.spread[member], mode.picked[member]) for member in members]
            for member, total in zip(members, totals):
                mode.item_out[0, pl.ds(2 * member, 2)] = total.astype(BF).reshape(2, BLOCK, HALF)

        def send(member):
            for to_core in range(2):
                item_copy(mode, member, to_core, 0).start()

        def send_own():
            item_copy(mode, mode.own_member, 1 - mode.core, 0).start()

        def send_rest(member):
            for to_core in range(2):
                item_copy(mode, member, to_core, 1).start()

        ahead(mode.members, mode.own_member, 2, partials, send, send_own)
        around(mode.members, mode.own_member, send_rest)
        item_copy(mode, mode.own_member, 1 - mode.core, 1).start()
        own_out = mode.item_out[0, 2 * mode.own_member + mode.core]
        for part in range(2):
            rows = slice(part * BLOCK // 2, (part + 1) * BLOCK // 2)
            item_in[part, mode.first_item + mode.own_member] = own_out[rows, :]

    per_mode(send_items)

    pltpu.make_async_copy(three, three, weight_own.at[1]).wait()
    arrived(three, weight_recv.at[1])
    arrived(cot_whole.at[other], cot_recv)
    load_cot.wait()
    cot_full = jnp.concatenate([cot_whole[0], cot_whole[1]], axis=1)

    def item_layer(part):
        arrived(item_in.at[part, : PARTS - 1], item_recv.at[part])
        halves = []
        for mode in modes:
            summed = item_in[part, mode.first_item].astype(F32)
            for member in range(1, mode.members):
                summed = summed + item_in[part, mode.first_item + member].astype(F32)
            halves.append(summed)
        message = jnp.concatenate(halves, axis=1)
        cot = cot_full[part * BLOCK // 2 : (part + 1) * BLOCK // 2, :]
        scale_item = rms_scale(message)
        query = (message * scale_item * item_gain).astype(BF)
        grad_query = jnp.zeros((BLOCK // 2, D), F32)
        for h in range(2):
            gate_pre = dot(query, wide[2, h])
            up_pre = dot(query, wide[3, h])
            grad_hidden = dot_nt(cot, tall[1, h])
            value, slope = silu_parts(gate_pre)
            grad_up = (grad_hidden * value).astype(BF)
            grad_gate = (grad_hidden * up_pre * slope).astype(BF)
            grad_query = grad_query + dot_nt(grad_gate, wide[2, h]) + dot_nt(grad_up, wide[3, h])
        inner = jnp.sum(item_gain * grad_query * message, axis=1, keepdims=True)
        cubed = scale_item * scale_item * scale_item
        return (scale_item * item_gain * grad_query - message * cubed * inner / D).astype(BF)

    def grad_copy(mode, member, part):
        return remote(
            mode.grad_out.at[pl.ds(part * BLOCK // 2, BLOCK // 2)],
            mode.rows.at[1, mode.own_member, rows16(m * BLOCK + part * BLOCK // 2, BLOCK // 2)],
            grad_send.at[part],
            grad_recv.at[turn_at(mode.members, mode.own_member, member, 2)],
            mode.item_shard(member),
            mode.core,
        )

    for part in range(2):
        grad_message = item_layer(part)
        for mode in modes:
            rows = slice(part * BLOCK // 2, (part + 1) * BLOCK // 2)
            mode.grad_out[rows, :] = grad_message[:, mode.core * HALF : (mode.core + 1) * HALF]
        for mode in modes:

            @pl.when(m != mode.core)
            def _(mode=mode, part=part):
                grad_copy(mode, mode.own_member, part).start()

            around(
                mode.members,
                mode.own_member,
                lambda member, mode=mode, part=part: grad_copy(mode, member, part).start(),
            )
    for mode in modes:

        @pl.when(m == mode.core)
        def _(mode=mode):
            place = slice(mode.core * BLOCK, (mode.core + 1) * BLOCK)
            mode.rows[1, mode.own_member, place, :] = mode.grad_out[...]

    def take_grads(mode):
        behind(
            mode.members,
            mode.own_member,
            2,
            lambda: arrived(mode.item_out.at[0, :3], grad_recv.at[0]),
            lambda n: arrived(mode.rows.at[1, :2], grad_recv.at[n]),
            lambda members: add_tiles(mode, 1, members),
        )

    per_mode(take_grads)
    per_mode(lambda mode: send_sums(mode, 1))

    def basket_backward(part):
        grad_out = sum_at_owners(1, part)
        grad_out_bf = grad_out.astype(BF)
        grad_normed = grad_out
        for h in range(2):
            grad_hidden = dot_nt(grad_out_bf, tall[0, h])
            value, slope = silu_parts(gate_keep[part, h])
            grad_up = (grad_hidden * value).astype(BF)
            grad_gate = (grad_hidden * up_keep[part, h] * slope).astype(BF)
            grad_normed = grad_normed + (
                dot_nt(grad_gate, wide[0, h]) + dot_nt(grad_up, wide[1, h])
            )
        sums = sum_keep[part]
        scale_basket = rms_scale(sums)
        inner_basket = jnp.sum(basket_gain * grad_normed * sums, axis=1, keepdims=True)
        cubed_basket = scale_basket * scale_basket * scale_basket
        grad_sum = scale_basket * basket_gain * grad_normed - sums * cubed_basket * inner_basket / D
        send_blocks(1, part, grad_sum.astype(BF))

    for part in range(2):
        basket_backward(part)

    def back_copy(mode, member):
        return remote(
            mode.item_out.at[1, pl.ds(2 * member, 2)],
            mode.back_in.at[mode.own_member],
            back_send,
            back_recv,
            mode.item_shard(member),
            mode.core,
        )

    def finish(mode):
        pick_all(mode, 1)

        def partials(members):
            totals = [dot(mode.spread[member], mode.picked[member]) for member in members]
            for member, total in zip(members, totals):
                mode.item_out[1, pl.ds(2 * member, 2)] = total.astype(BF).reshape(2, BLOCK, HALF)

        ahead(
            mode.members,
            mode.own_member,
            2,
            partials,
            lambda member: back_copy(mode, member).start(),
            lambda: None,
        )
        mode.back_in[mode.own_member] = mode.item_out[1, pl.ds(2 * mode.own_member, 2)]
        sent(mode.words_out.at[: mode.members - 1], words_send)
        sent(mode.rows.at[0, : mode.members - 1], rows_send)
        sent(mode.item_out.at[0, : 2 * mode.members - 1], item_send)
        for phase in range(2):
            sent(mode.owner_out.at[phase, : 2 * mode.columns - 1], owner_send.at[phase])
            for part in range(2):
                sent(owner_in.at[phase, part, : PARTS - 1], block_send.at[phase, part])
        for part in range(2):
            sent(item_in.at[part, : PARTS - 1], grad_send.at[part])
        arrived(mode.back_in.at[: mode.members - 1], back_recv)
        for block in range(2):
            back = mode.back_in[0, block].astype(F32)
            for member in range(1, mode.members):
                back = back + mode.back_in[member, block].astype(F32)
            back_ref[block * BLOCK : (block + 1) * BLOCK, :] = back
        sent(mode.back_in.at[: mode.members - 1], back_send)

    per_mode(finish)

    sent(wide.at[:3], weight_send)
    cot_copy().wait_send()


def local(
    item_rows,
    first_moment,
    second_moment,
    item_cot,
    tile_bits,
    tile_item,
    tile_dest,
    basket_gain,
    item_gain,
    gate_basket,
    up_basket,
    down_basket,
    gate_item,
    up_item,
    down_item,
):
    vmem = pl.BlockSpec(memory_space=pltpu.VMEM)
    anywhere = pl.BlockSpec(memory_space=pltpu.HBM)
    back_items = pl.pallas_call(
        kernel,
        out_shape=pltpu.VMEM((2 * BLOCK, HALF), F32),
        in_specs=[anywhere] * 13,
        out_specs=vmem,
        scratch_shapes=[
            common_scratch(),
            mode_scratch(RING, PLANE),
            mode_scratch(PLANE, RING),
        ],
        compiler_params=pltpu.CompilerParams(
            collective_id=0, has_side_effects=True, vmem_limit_bytes=60 * 1024 * 1024
        ),
        name="layer",
    )(
        item_rows,
        item_cot,
        tile_bits,
        tile_item,
        tile_dest,
        basket_gain.reshape(1, D),
        item_gain.reshape(1, D),
        gate_basket,
        up_basket,
        down_basket,
        gate_item,
        up_item,
        down_item,
    )
    gradient = item_cot.astype(F32) + back_items
    new_first = BETA_FIRST * first_moment + (1.0 - BETA_FIRST) * gradient
    new_second = BETA_SECOND * second_moment + (1.0 - BETA_SECOND) * gradient * gradient
    new_rows = item_rows - LEARNING_RATE * new_first / (jnp.sqrt(new_second) + ADAM_EPSILON)
    return (new_rows, new_first, new_second)


def solution(mesh):
    split = P("shard", "mp")
    return jax.shard_map(
        local,
        mesh=mesh,
        in_specs=(
            split,
            split,
            split,
            split,
            P("shard", None, None),
            P("shard"),
            P("shard"),
            P(),
            P(),
            P(None, "mp"),
            P(None, "mp"),
            P("mp", None),
            P(None, "mp"),
            P(None, "mp"),
            P("mp", None),
        ),
        out_specs=(split, split, split),
        check_vma=False,
    )
```

```python
import jax
import jax.numpy as jnp
from jax import lax
from jax.experimental import pallas as pl
from jax.experimental.pallas import tpu as pltpu
from jax.sharding import PartitionSpec as P

D = 256
HALF = 128
BLOCK = 128
TILE_DEV = 16
RING = 8
PLANE = 16
PARTS = RING + PLANE
OWN = 64
PART = OWN // 2
HIDDEN = 1024

NORM_EPSILON = 1e-05
LEARNING_RATE = 0.01
BETA_FIRST = 0.9
BETA_SECOND = 0.99
ADAM_EPSILON = 1e-08

MESH = pl.DeviceIdType.MESH
BF = jnp.bfloat16
F32 = jnp.float32


def dot(a, b):
    return jnp.dot(a, b, preferred_element_type=F32)


def dot_nt(a, b):
    return lax.dot_general(a, b, (((1,), (1,)), ((), ())), preferred_element_type=F32)


def silu_parts(gate_values):
    sigmoid = jax.nn.sigmoid(gate_values)
    return (gate_values * sigmoid, sigmoid * (1.0 + gate_values * (1.0 - sigmoid)))


def rms_scale(values):
    return lax.rsqrt(jnp.mean(values * values, axis=-1, keepdims=True) + NORM_EPSILON)


def rows16(start, size):
    return pl.ds(pl.multiple_of(start, 16), size)


def mode_scratch(members, columns):
    wide = TILE_DEV * columns
    tiles = TILE_DEV * members
    slots = wide // 128 + 1
    return {
        "words_out": pltpu.VMEM((members, slots, 8, 128), jnp.int32),
        "words_in": pltpu.VMEM((members, slots, 8, 128), jnp.int32),
        "rows": pltpu.VMEM((2, members, 2 * BLOCK, HALF), BF),
        "spread": pltpu.VMEM((members, 2 * BLOCK, wide), BF),
        "collect": pltpu.VMEM((members, wide, 2 * BLOCK), BF),
        "select_cols": pltpu.VMEM((BLOCK, 2 * tiles), BF),
        "select_rows": pltpu.VMEM((tiles, BLOCK), BF),
        "tile_sums": pltpu.VMEM((columns, 2 * tiles, HALF), BF),
        "owner_out": pltpu.VMEM((2, 2 * columns, OWN, HALF), BF),
        "block_out": pltpu.VMEM((2, OWN, HALF), BF),
        "block_in": pltpu.VMEM((2, columns, BLOCK, HALF), BF),
        "picked": pltpu.VMEM((members, wide, HALF), BF),
        "item_out": pltpu.VMEM((2, 2 * members, BLOCK, HALF), BF),
        "back_in": pltpu.VMEM((members, 2, BLOCK, HALF), BF),
        "grad_out": pltpu.VMEM((BLOCK, HALF), BF),
    }


def common_scratch():
    dma = pltpu.SemaphoreType.DMA
    return {
        "wide": pltpu.VMEM((4, 2, D, HIDDEN), BF),
        "tall": pltpu.VMEM((2, 2, HIDDEN, D), BF),
        "cot_whole": pltpu.VMEM((2, BLOCK, HALF), BF),
        "gate_keep": pltpu.VMEM((2, 2, PART, HIDDEN), F32),
        "up_keep": pltpu.VMEM((2, 2, PART, HIDDEN), F32),
        "sum_keep": pltpu.VMEM((2, PART, D), F32),
        "item_rows": pltpu.VMEM((2 * BLOCK, HALF), F32),
        "tile_bits": pltpu.VMEM((TILE_DEV, 8, 128), jnp.int32),
        "tile_item": pltpu.SMEM((TILE_DEV,), jnp.int32),
        "tile_dest": pltpu.SMEM((TILE_DEV,), jnp.int32),
        "basket_gain": pltpu.VMEM((1, D), F32),
        "item_gain": pltpu.VMEM((1, D), F32),
        "load_sem": dma((7,)),
        "weight_own": dma((2,)),
        "weight_send": dma,
        "weight_recv": dma((2,)),
        "cot_send": dma,
        "cot_recv": dma,
        "owner_in": pltpu.VMEM((2, 2, PARTS, PART, HALF), BF),
        "item_in": pltpu.VMEM((2, PARTS, BLOCK // 2, HALF), BF),
        "words_send": dma,
        "words_recv": dma,
        "rows_send": dma,
        "rows_recv": dma((PLANE // 2,)),
        "owner_send": dma((2,)),
        "owner_recv": dma((2, 2)),
        "block_send": dma((2, 2)),
        "block_recv": dma((2, PLANE // 4)),
        "item_send": dma,
        "item_recv": dma((2,)),
        "grad_send": dma((2,)),
        "grad_recv": dma((PLANE // 2,)),
        "back_send": dma,
        "back_recv": dma,
    }


class Mode:
    def __init__(self, core, refs, z, q):
        self.core = core
        self.members, self.columns = (RING, PLANE) if core == 0 else (PLANE, RING)
        self.own_member, self.own_column = (z, q) if core == 0 else (q, z)
        self.first = 0 if core == 0 else PLANE
        self.first_item = 0 if core == 0 else RING
        self.z, self.q = z, q
        self.__dict__.update(refs)

    def item_shard(self, member):
        return member * PLANE + self.q if self.core == 0 else self.z * PLANE + member

    def basket_shard(self, column):
        return self.z * PLANE + column if self.core == 0 else column * PLANE + self.q


def kernel(
    rows_hbm,
    cot_hbm,
    bits_hbm,
    item_hbm,
    dest_hbm,
    gain_b_hbm,
    gain_i_hbm,
    gate_b_ref,
    up_b_ref,
    down_b_ref,
    gate_i_ref,
    up_i_ref,
    down_i_ref,
    back_ref,
    common,
    ring_refs,
    plane_refs,
):
    shard = lax.axis_index("shard")
    m = lax.axis_index("mp")
    other = 1 - m
    z = lax.div(shard, PLANE)
    q = lax.rem(shard, PLANE)
    me = 2 * q + m
    modes = (Mode(0, ring_refs, z, q), Mode(1, plane_refs, z, q))
    wide, tall, cot_whole = common["wide"], common["tall"], common["cot_whole"]
    gate_keep, up_keep, sum_keep = common["gate_keep"], common["up_keep"], common["sum_keep"]
    rows_ref, bits_ref, load_sem = common["item_rows"], common["tile_bits"], common["load_sem"]
    weight_own, weight_send = common["weight_own"], common["weight_send"]
    weight_recv = common["weight_recv"]
    cot_send, cot_recv = common["cot_send"], common["cot_recv"]
    owner_in, item_in = common["owner_in"], common["item_in"]
    words_send, words_recv = common["words_send"], common["words_recv"]
    rows_send, rows_recv = common["rows_send"], common["rows_recv"]
    owner_send, owner_recv = common["owner_send"], common["owner_recv"]
    block_send, block_recv = common["block_send"], common["block_recv"]
    item_send, item_recv = common["item_send"], common["item_recv"]
    grad_send, grad_recv = common["grad_send"], common["grad_recv"]
    back_send, back_recv = common["back_send"], common["back_recv"]

    def remote(src, dst, send, recv, to_shard, to_core):
        return pltpu.make_async_remote_copy(
            src_ref=src,
            dst_ref=dst,
            send_sem=send,
            recv_sem=recv,
            device_id=(to_shard, to_core),
            device_id_type=MESH,
        )

    def arrived(ref, recv):
        remote(ref, ref, cot_send, recv, shard, other).wait_recv()

    def sent(ref, send):
        remote(ref, ref, send, cot_recv, shard, other).wait_send()

    def around(count, own, body):
        def step(n, carry):
            body(lax.rem(own + n, count))
            return carry

        lax.fori_loop(1, count, step, 0)

    def ahead(count, own, size, work, send, send_own):
        def group(n, last):
            places = [lax.rem(own + n * size + i + 1, count) for i in range(size)]
            work(places)
            for place in places[: size - 1] if last else places:
                send(place)
            if last:
                send_own()

        def step(n, carry):
            group(n, False)
            return carry

        lax.fori_loop(0, count // size - 1, step, 0)
        group(count // size - 1, True)

    def turn_at(count, own, place, size):
        return lax.div(lax.rem(place - own + count, count), size)

    def behind(count, own, size, wait_first, wait, work):
        def group(n, first):
            places = [lax.rem(own + count - n * size - i, count) for i in range(size)]
            if first:
                wait_first()
            else:
                wait(n)
            work(places)

        def step(n, carry):
            group(n, False)
            return carry

        group(0, True)
        lax.fori_loop(1, count // size, step, 0)

    def per_mode(body):
        for mode in modes:

            @pl.when(m == mode.core)
            def _(mode=mode):
                body(mode)

    weights = (
        (gate_b_ref, wide.at[0]),
        (up_b_ref, wide.at[1]),
        (down_b_ref, tall.at[0]),
        (gate_i_ref, wide.at[2]),
        (up_i_ref, wide.at[3]),
        (down_i_ref, tall.at[1]),
    )

    def own_weight(n):
        src, dst = weights[n]
        return pltpu.make_async_copy(src, dst.at[m], weight_own.at[n // 3])

    def sibling_weight(n):
        src, dst = weights[n]
        return remote(src, dst.at[m], weight_send, weight_recv.at[n // 3], shard, other)

    item_ref, dest_ref = common["tile_item"], common["tile_dest"]
    gain_b_ref, gain_i_ref = common["basket_gain"], common["item_gain"]
    small_loads = [
        pltpu.make_async_copy(src, dst, load_sem.at[3 + n])
        for n, (src, dst) in enumerate(
            (
                (item_hbm, item_ref),
                (dest_hbm, dest_ref),
                (gain_b_hbm, gain_b_ref),
                (gain_i_hbm, gain_i_ref),
            )
        )
    ]
    load_rows = pltpu.make_async_copy(rows_hbm, rows_ref, load_sem.at[0])
    load_bits = pltpu.make_async_copy(bits_hbm, bits_ref, load_sem.at[1])
    load_cot = pltpu.make_async_copy(
        cot_hbm.at[rows16(m * BLOCK, BLOCK)], cot_whole.at[m], load_sem.at[2]
    )
    barrier = pltpu.get_barrier_semaphore()

    def greet(to_shard, to_core):
        pl.semaphore_signal(
            barrier, inc=1, device_id=(to_shard, to_core), device_id_type=MESH
        )

    def greet_ring(z_to):
        for core in range(2):
            greet(z_to * PLANE + q, core)

    load_rows.start()
    load_bits.start()
    for load in small_loads:
        load.start()
    around(RING, z, greet_ring)
    around(2 * PLANE, me, lambda k: greet(z * PLANE + lax.div(k, 2), lax.rem(k, 2)))
    load_cot.start()
    for n in range(6):
        own_weight(n).start()

    sub = lax.broadcasted_iota(jnp.int32, (8, 128), 0)
    lane = lax.broadcasted_iota(jnp.int32, (8, 128), 1)

    def prepare(mode):
        mode.rows[0, mode.own_member] = rows_ref[...].astype(BF)
        columns = mode.columns
        per_slot = 128 // columns
        slots = TILE_DEV // per_slot
        if mode.core == 0:
            tiles = [bits_ref[t] for t in range(TILE_DEV)]
        else:
            left = lax.broadcasted_iota(jnp.int32, (128, 128), 0)
            right = lax.broadcasted_iota(jnp.int32, (128, 128), 1)
            order = jnp.where(
                (left % PLANE == right // columns) & (left // PLANE == right % columns), 1.0, 0.0
            ).astype(BF)
            words = bits_ref[...].reshape(128, 128)
            low = dot((words & 255).astype(F32).astype(BF), order)
            high = dot(jnp.right_shift(words, 8).astype(F32).astype(BF), order)
            words = (low + 256.0 * high).astype(jnp.int32).reshape(TILE_DEV, 8, 128)
            tiles = [words[t] for t in range(TILE_DEV)]
        group = lane // columns
        about = jnp.zeros((8, 128), jnp.int32)
        start = mode.own_member * TILE_DEV
        dest_sub = 2 + lax.div(start, 128)
        dest_lane = lax.rem(start, 128)
        for t in range(TILE_DEV):
            slot, place = t // per_slot, t % per_slot
            about = jnp.where((sub == slot) & (group == place), item_ref[t], about)
            about = jnp.where((sub == dest_sub) & (lane == dest_lane + t), dest_ref[t], about)
        for member in range(mode.members):
            for slot in range(slots):
                values = jnp.zeros((8, 128), jnp.int32)
                for place in range(per_slot):
                    turned = tiles[slot * per_slot + place]
                    shift = (columns * (place - member)) % 128
                    if shift:
                        turned = pltpu.roll(turned, shift, 1)
                    values = jnp.where(group == place, turned, values)
                mode.words_out[member, slot] = values
            mode.words_out[member, slots] = about
        mode.words_in[mode.own_member] = mode.words_out[mode.own_member]

    load_rows.wait()
    load_bits.wait()
    for load in small_loads:
        load.wait()
    per_mode(prepare)

    pl.semaphore_wait(barrier, 2 * PLANE - 1 + 2 * (RING - 1))

    def words_copy(mode, member):
        return remote(
            mode.words_out.at[member],
            mode.words_in.at[mode.own_member],
            words_send,
            words_recv,
            mode.item_shard(member),
            mode.core,
        )

    def rows_copy(mode, member):
        return remote(
            mode.rows.at[0, mode.own_member],
            mode.rows.at[0, mode.own_member],
            rows_send,
            rows_recv.at[turn_at(mode.members, mode.own_member, member, 2)],
            mode.item_shard(member),
            mode.core,
        )

    def start_rows(mode):
        around(mode.members, mode.own_member, lambda member: words_copy(mode, member).start())
        around(mode.members, mode.own_member, lambda member: rows_copy(mode, member).start())

    per_mode(start_rows)

    def cot_copy():
        return remote(
            cot_hbm.at[rows16(other * BLOCK, BLOCK)],
            cot_whole.at[m],
            cot_send,
            cot_recv,
            shard,
            other,
        )

    for n in range(3):
        sibling_weight(n).start()
    cot_copy().start()
    for n in range(3, 6):
        sibling_weight(n).start()

    def add_tiles(mode, phase, members):
        all_sums = [dot(mode.collect[member], mode.rows[phase, member]) for member in members]
        shape = (mode.columns, TILE_DEV, HALF)
        tiles = TILE_DEV * mode.members
        for member, sums in zip(members, all_sums):
            high = sums.astype(BF)
            low = (sums - high.astype(F32)).astype(BF)
            mode.tile_sums[:, rows16(member * TILE_DEV, TILE_DEV), :] = high.reshape(shape)
            mode.tile_sums[:, rows16(tiles + member * TILE_DEV, TILE_DEV), :] = low.reshape(shape)

    def turned(mode, tile_major, column_major):
        same = (tile_major // mode.columns == column_major % TILE_DEV) & (
            tile_major % mode.columns == column_major // TILE_DEV
        )
        return jnp.where(same, 1.0, 0.0).astype(BF)

    def finish_selection(mode):
        size = TILE_DEV * mode.columns
        left = lax.broadcasted_iota(jnp.int32, (size, size), 0)
        right = lax.broadcasted_iota(jnp.int32, (size, size), 1)
        to_columns = turned(mode, left, right)

        def turn_some(n, carry):
            mats = [dot(mode.spread[4 * n + i], to_columns).astype(BF) for i in range(4)]
            for i in range(4):
                mode.spread[4 * n + i] = mats[i]
            return carry

        lax.fori_loop(0, mode.members // 4, turn_some, 0)
        tiles = TILE_DEV * mode.members
        eye_left = lax.broadcasted_iota(jnp.int32, (tiles, tiles), 0)
        eye_right = lax.broadcasted_iota(jnp.int32, (tiles, tiles), 1)
        eye = jnp.where(eye_left == eye_right, 1.0, 0.0).astype(BF)
        mode.select_rows[...] = dot_nt(eye, mode.select_cols[:, :tiles]).astype(BF)

    def take_rows(mode):
        size = TILE_DEV * mode.columns
        slots = size // 128
        left = lax.broadcasted_iota(jnp.int32, (size, size), 0)
        right = lax.broadcasted_iota(jnp.int32, (size, size), 1)

        from_tiles = turned(mode, right, left)
        shifts = lax.broadcasted_iota(jnp.int32, (8, 16, 128), 1)

        def unpack(member):
            about = mode.words_in[member, slots]
            halves = []
            for slot in range(slots):
                packed = jnp.broadcast_to(mode.words_in[member, slot][:, None, :], (8, 16, 128))
                bits = (jnp.right_shift(packed, shifts) & 1).reshape(128, 128).astype(F32)
                halves.append((bits, jnp.broadcast_to(about[slot : slot + 1, :], (128, 128))))
            blocks = []
            for block in range(2):
                parts = [jnp.where(item == block, bits, 0.0) for bits, item in halves]
                blocks.append(parts[0] if slots == 1 else jnp.concatenate(parts, axis=1))
            mat = jnp.concatenate(blocks, axis=0).astype(BF)
            mode.spread[member] = mat
            mode.collect[member] = dot_nt(from_tiles, mat).astype(BF)

        def unpack_some(n, carry):
            for i in range(4):
                unpack(4 * n + i)
            return carry

        arrived(mode.words_in.at[: mode.members - 1], words_recv)
        lax.fori_loop(0, mode.members // 4, unpack_some, 0)

        tiles = TILE_DEV * mode.members
        about = mode.words_in[0, slots]
        for member in range(1, mode.members):
            about = about + mode.words_in[member, slots]
        all_dest = about[2:3, :]
        if tiles > 128:
            all_dest = jnp.concatenate([all_dest, about[3:4, :]], axis=1)
        block_of = lax.broadcasted_iota(jnp.int32, (BLOCK, tiles), 0)
        one_hot = jnp.where(block_of == all_dest, 1.0, 0.0).astype(BF)
        mode.select_cols[...] = jnp.concatenate([one_hot, one_hot], axis=1)
        behind(
            mode.members,
            mode.own_member,
            2,
            lambda: arrived(mode.rows.at[0, 0], rows_recv.at[0]),
            lambda n: arrived(mode.rows.at[0, :2], rows_recv.at[n]),
            lambda members: add_tiles(mode, 0, members),
        )

    per_mode(take_rows)

    def owner_copy(mode, phase, column, to_core, part):
        return remote(
            mode.owner_out.at[phase, 2 * column + to_core, pl.ds(part * PART, PART)],
            owner_in.at[phase, part, mode.first + mode.own_column],
            owner_send.at[phase],
            owner_recv.at[phase, part],
            mode.basket_shard(column),
            to_core,
        )

    def send_sums(mode, phase):
        def column_sums(columns):
            for k in range(0, len(columns), 2):
                pair = jnp.concatenate([mode.tile_sums[c] for c in columns[k : k + 2]], axis=1)
                total = dot(mode.select_cols[...], pair).astype(BF)
                for i, column in enumerate(columns[k : k + 2]):
                    mode.owner_out[phase, pl.ds(2 * column, 2)] = total[
                        :, i * HALF : (i + 1) * HALF
                    ].reshape(2, OWN, HALF)

        def send(column):
            for to_core in range(2):
                owner_copy(mode, phase, column, to_core, 0).start()

        def send_own():
            owner_copy(mode, phase, mode.own_column, 1 - mode.core, 0).start()

        def send_rest(column):
            for to_core in range(2):
                owner_copy(mode, phase, column, to_core, 1).start()

        ahead(mode.columns, mode.own_column, 4, column_sums, send, send_own)
        around(mode.columns, mode.own_column, send_rest)
        owner_copy(mode, phase, mode.own_column, 1 - mode.core, 1).start()
        own_out = mode.owner_out[phase, 2 * mode.own_column + mode.core]
        for part in range(2):
            rows = slice(part * PART, (part + 1) * PART)
            owner_in[phase, part, mode.first + mode.own_column] = own_out[rows, :]
        if phase == 0:
            finish_selection(mode)

    def sum_at_owners(phase, part):
        arrived(owner_in.at[phase, part, : PARTS - 1], owner_recv.at[phase, part])
        halves = []
        for mode in modes:
            total = owner_in[phase, part, mode.first].astype(F32)
            for column in range(1, mode.columns):
                total = total + owner_in[phase, part, mode.first + column].astype(F32)
            halves.append(total)
        return jnp.concatenate(halves, axis=1)

    def block_copy(mode, phase, column, part):
        return remote(
            mode.block_out.at[phase, pl.ds(part * PART, PART)],
            mode.block_in.at[phase, mode.own_column, rows16(m * OWN + part * PART, PART)],
            block_send.at[phase, part],
            block_recv.at[phase, turn_at(mode.columns, mode.own_column, column, 4)],
            mode.basket_shard(column),
            mode.core,
        )

    def send_blocks(phase, part, values):
        for mode in modes:
            rows = slice(part * PART, (part + 1) * PART)
            mode.block_out[phase, rows, :] = values[:, mode.core * HALF : (mode.core + 1) * HALF]
        for mode in modes:

            @pl.when(m != mode.core)
            def _(mode=mode):
                block_copy(mode, phase, mode.own_column, part).start()

            around(
                mode.columns,
                mode.own_column,
                lambda column, mode=mode: block_copy(mode, phase, column, part).start(),
            )

            @pl.when(m == mode.core)
            def _(mode=mode):
                start = mode.core * OWN + part * PART
                mode.block_in[phase, mode.own_column, start : start + PART, :] = mode.block_out[
                    phase, part * PART : (part + 1) * PART
                ]

    def pick_all(mode, phase):
        def pick(columns):
            for k in range(0, len(columns), 2):
                pair = jnp.concatenate(
                    [mode.block_in[phase, c] for c in columns[k : k + 2]], axis=1
                )
                chosen = dot(mode.select_rows[...], pair).astype(BF)
                for i, column in enumerate(columns[k : k + 2]):
                    mode.picked[:, rows16(column * TILE_DEV, TILE_DEV), :] = chosen[
                        :, i * HALF : (i + 1) * HALF
                    ].reshape(mode.members, TILE_DEV, HALF)

        behind(
            mode.columns,
            mode.own_column,
            4,
            lambda: arrived(owner_in.at[phase, 0, :14], block_recv.at[phase, 0]),
            lambda n: arrived(mode.block_in.at[phase, :4], block_recv.at[phase, n]),
            pick,
        )

    basket_gain = gain_b_ref[...]
    item_gain = gain_i_ref[...]

    three = wide.at[:3, 0]
    per_mode(lambda mode: send_sums(mode, 0))

    def basket_layer(part):
        basket_sum = sum_at_owners(0, part)
        sum_keep[part] = basket_sum
        if part == 0:
            pltpu.make_async_copy(three, three, weight_own.at[0]).wait()
            arrived(three, weight_recv.at[0])
        normed = basket_sum * rms_scale(basket_sum) * basket_gain
        normed_bf = normed.astype(BF)
        total = normed
        for h in range(2):
            gate_pre = dot(normed_bf, wide[0, h])
            up_pre = dot(normed_bf, wide[1, h])
            gate_keep[part, h] = gate_pre
            up_keep[part, h] = up_pre
            hidden = (gate_pre * jax.nn.sigmoid(gate_pre) * up_pre).astype(BF)
            total = total + dot(hidden, tall[0, h])
        send_blocks(0, part, total.astype(BF))

    for part in range(2):
        basket_layer(part)

    def item_copy(mode, member, to_core, part):
        return remote(
            mode.item_out.at[0, 2 * member + to_core, pl.ds(part * BLOCK // 2, BLOCK // 2)],
            item_in.at[part, mode.first_item + mode.own_member],
            item_send,
            item_recv.at[part],
            mode.item_shard(member),
            to_core,
        )

    def send_items(mode):
        pick_all(mode, 0)

        def partials(members):
            totals = [dot(mode.spread[member], mode.picked[member]) for member in members]
            for member, total in zip(members, totals):
                mode.item_out[0, pl.ds(2 * member, 2)] = total.astype(BF).reshape(2, BLOCK, HALF)

        def send(member):
            for to_core in range(2):
                item_copy(mode, member, to_core, 0).start()

        def send_own():
            item_copy(mode, mode.own_member, 1 - mode.core, 0).start()

        def send_rest(member):
            for to_core in range(2):
                item_copy(mode, member, to_core, 1).start()

        ahead(mode.members, mode.own_member, 4, partials, send, send_own)
        around(mode.members, mode.own_member, send_rest)
        item_copy(mode, mode.own_member, 1 - mode.core, 1).start()
        own_out = mode.item_out[0, 2 * mode.own_member + mode.core]
        for part in range(2):
            rows = slice(part * BLOCK // 2, (part + 1) * BLOCK // 2)
            item_in[part, mode.first_item + mode.own_member] = own_out[rows, :]

    per_mode(send_items)

    pltpu.make_async_copy(three, three, weight_own.at[1]).wait()
    arrived(three, weight_recv.at[1])
    arrived(cot_whole.at[other], cot_recv)
    load_cot.wait()
    cot_full = jnp.concatenate([cot_whole[0], cot_whole[1]], axis=1)

    def item_layer(part):
        arrived(item_in.at[part, : PARTS - 1], item_recv.at[part])
        halves = []
        for mode in modes:
            summed = item_in[part, mode.first_item].astype(F32)
            for member in range(1, mode.members):
                summed = summed + item_in[part, mode.first_item + member].astype(F32)
            halves.append(summed)
        message = jnp.concatenate(halves, axis=1)
        cot = cot_full[part * BLOCK // 2 : (part + 1) * BLOCK // 2, :]
        scale_item = rms_scale(message)
        query = (message * scale_item * item_gain).astype(BF)
        grad_query = jnp.zeros((BLOCK // 2, D), F32)
        for h in range(2):
            gate_pre = dot(query, wide[2, h])
            up_pre = dot(query, wide[3, h])
            grad_hidden = dot_nt(cot, tall[1, h])
            value, slope = silu_parts(gate_pre)
            grad_up = (grad_hidden * value).astype(BF)
            grad_gate = (grad_hidden * up_pre * slope).astype(BF)
            grad_query = grad_query + dot_nt(grad_gate, wide[2, h]) + dot_nt(grad_up, wide[3, h])
        inner = jnp.sum(item_gain * grad_query * message, axis=1, keepdims=True)
        cubed = scale_item * scale_item * scale_item
        return (scale_item * item_gain * grad_query - message * cubed * inner / D).astype(BF)

    def grad_copy(mode, member, part):
        return remote(
            mode.grad_out.at[pl.ds(part * BLOCK // 2, BLOCK // 2)],
            mode.rows.at[1, mode.own_member, rows16(m * BLOCK + part * BLOCK // 2, BLOCK // 2)],
            grad_send.at[part],
            grad_recv.at[turn_at(mode.members, mode.own_member, member, 2)],
            mode.item_shard(member),
            mode.core,
        )

    for part in range(2):
        grad_message = item_layer(part)
        for mode in modes:
            rows = slice(part * BLOCK // 2, (part + 1) * BLOCK // 2)
            mode.grad_out[rows, :] = grad_message[:, mode.core * HALF : (mode.core + 1) * HALF]
        for mode in modes:

            @pl.when(m != mode.core)
            def _(mode=mode, part=part):
                grad_copy(mode, mode.own_member, part).start()

            around(
                mode.members,
                mode.own_member,
                lambda member, mode=mode, part=part: grad_copy(mode, member, part).start(),
            )
    for mode in modes:

        @pl.when(m == mode.core)
        def _(mode=mode):
            place = slice(mode.core * BLOCK, (mode.core + 1) * BLOCK)
            mode.rows[1, mode.own_member, place, :] = mode.grad_out[...]

    def take_grads(mode):
        behind(
            mode.members,
            mode.own_member,
            2,
            lambda: arrived(mode.item_out.at[0, :3], grad_recv.at[0]),
            lambda n: arrived(mode.rows.at[1, :2], grad_recv.at[n]),
            lambda members: add_tiles(mode, 1, members),
        )

    per_mode(take_grads)
    per_mode(lambda mode: send_sums(mode, 1))

    def basket_backward(part):
        grad_out = sum_at_owners(1, part)
        grad_out_bf = grad_out.astype(BF)
        grad_normed = grad_out
        for h in range(2):
            grad_hidden = dot_nt(grad_out_bf, tall[0, h])
            value, slope = silu_parts(gate_keep[part, h])
            grad_up = (grad_hidden * value).astype(BF)
            grad_gate = (grad_hidden * up_keep[part, h] * slope).astype(BF)
            grad_normed = grad_normed + (
                dot_nt(grad_gate, wide[0, h]) + dot_nt(grad_up, wide[1, h])
            )
        sums = sum_keep[part]
        scale_basket = rms_scale(sums)
        inner_basket = jnp.sum(basket_gain * grad_normed * sums, axis=1, keepdims=True)
        cubed_basket = scale_basket * scale_basket * scale_basket
        grad_sum = scale_basket * basket_gain * grad_normed - sums * cubed_basket * inner_basket / D
        send_blocks(1, part, grad_sum.astype(BF))

    for part in range(2):
        basket_backward(part)

    def back_copy(mode, member):
        return remote(
            mode.item_out.at[1, pl.ds(2 * member, 2)],
            mode.back_in.at[mode.own_member],
            back_send,
            back_recv,
            mode.item_shard(member),
            mode.core,
        )

    def finish(mode):
        pick_all(mode, 1)

        def partials(members):
            totals = [dot(mode.spread[member], mode.picked[member]) for member in members]
            for member, total in zip(members, totals):
                mode.item_out[1, pl.ds(2 * member, 2)] = total.astype(BF).reshape(2, BLOCK, HALF)

        ahead(
            mode.members,
            mode.own_member,
            4,
            partials,
            lambda member: back_copy(mode, member).start(),
            lambda: None,
        )
        mode.back_in[mode.own_member] = mode.item_out[1, pl.ds(2 * mode.own_member, 2)]
        sent(mode.words_out.at[: mode.members - 1], words_send)
        sent(mode.rows.at[0, : mode.members - 1], rows_send)
        sent(mode.item_out.at[0, : 2 * mode.members - 1], item_send)
        for phase in range(2):
            sent(mode.owner_out.at[phase, : 2 * mode.columns - 1], owner_send.at[phase])
            for part in range(2):
                sent(owner_in.at[phase, part, : PARTS - 1], block_send.at[phase, part])
        for part in range(2):
            sent(item_in.at[part, : PARTS - 1], grad_send.at[part])
        arrived(mode.back_in.at[: mode.members - 1], back_recv)
        for block in range(2):
            back = mode.back_in[0, block].astype(F32)
            for member in range(1, mode.members):
                back = back + mode.back_in[member, block].astype(F32)
            back_ref[block * BLOCK : (block + 1) * BLOCK, :] = back
        sent(mode.back_in.at[: mode.members - 1], back_send)

    per_mode(finish)

    sent(wide.at[:3], weight_send)
    cot_copy().wait_send()


def local(
    item_rows,
    first_moment,
    second_moment,
    item_cot,
    tile_bits,
    tile_item,
    tile_dest,
    basket_gain,
    item_gain,
    gate_basket,
    up_basket,
    down_basket,
    gate_item,
    up_item,
    down_item,
):
    vmem = pl.BlockSpec(memory_space=pltpu.VMEM)
    anywhere = pl.BlockSpec(memory_space=pltpu.HBM)
    back_items = pl.pallas_call(
        kernel,
        out_shape=pltpu.VMEM((2 * BLOCK, HALF), F32),
        in_specs=[anywhere] * 13,
        out_specs=vmem,
        scratch_shapes=[
            common_scratch(),
            mode_scratch(RING, PLANE),
            mode_scratch(PLANE, RING),
        ],
        compiler_params=pltpu.CompilerParams(
            collective_id=0, has_side_effects=True, vmem_limit_bytes=60 * 1024 * 1024
        ),
        name="layer",
    )(
        item_rows,
        item_cot,
        tile_bits,
        tile_item,
        tile_dest,
        basket_gain.reshape(1, D),
        item_gain.reshape(1, D),
        gate_basket,
        up_basket,
        down_basket,
        gate_item,
        up_item,
        down_item,
    )
    gradient = item_cot.astype(F32) + back_items
    new_first = BETA_FIRST * first_moment + (1.0 - BETA_FIRST) * gradient
    new_second = BETA_SECOND * second_moment + (1.0 - BETA_SECOND) * gradient * gradient
    new_rows = item_rows - LEARNING_RATE * new_first / (jnp.sqrt(new_second) + ADAM_EPSILON)
    return (new_rows, new_first, new_second)


def solution(mesh):
    split = P("shard", "mp")
    return jax.shard_map(
        local,
        mesh=mesh,
        in_specs=(
            split,
            split,
            split,
            split,
            P("shard", None, None),
            P("shard"),
            P("shard"),
            P(),
            P(),
            P(None, "mp"),
            P(None, "mp"),
            P("mp", None),
            P(None, "mp"),
            P(None, "mp"),
            P("mp", None),
        ),
        out_specs=(split, split, split),
        check_vma=False,
    )
```
